32 devices in a mesh: section: 2 (over core), expert: 8 (over z, y), shard: 2 (over x).
Axes of the slice: x: 2, y: 2, z: 4, core: 2. Of those that a mesh axis runs over, the one named last changes fastest.
Arguments:
- inputs: bfloat16 [2, 1024, 2048], P(None, 'expert'), may hold values from -6 to 6
- cotangent: bfloat16 [2, 1024, 2048], P(None, 'expert'), may hold values from -6 to 6
- segments: int32 [2, 8, 128], P(None, 'expert'), may hold values from 0 to 5, never falling along the last dimension, each value on 1 to 48 neighbouring positions
- routes: int32 [2, 2, 1024, 8], P('section', None, 'expert'), may hold values from 0 to 15, all different within a row; in each aligned block of 128 rows (0 to 127, 128 to 255, ..., all dimensions but the last counted through in order) at most 80 rows name the same one
- counts: int32 [2, 16], P('section'), may hold values from 1 to 5
- norm_attn: float32 [2, 2048], P('section'), may hold values from 0.5 to 1.5
- norm_ffn: float32 [2, 2048], P('section'), may hold values from 0.5 to 1.5
- q_gain: float32 [2, 128], P('section'), may hold values from 0.5 to 1.5
- k_gain: float32 [2, 128], P('section'), may hold values from 0.5 to 1.5
- w_query: bfloat16 [2, 2048, 4096], P('section', 'expert', 'shard'), may hold values from -0.125 to 0.125
- w_key: bfloat16 [2, 2048, 512], P('section', 'expert', 'shard'), may hold values from -0.125 to 0.125
- w_value: bfloat16 [2, 2048, 512], P('section', 'expert', 'shard'), may hold values from -0.125 to 0.125
- w_output: bfloat16 [2, 2048, 4096], P('section', 'expert', 'shard'), may hold values from -0.375 to 0.375
- w_router: bfloat16 [2, 2048, 16], P('section', 'expert'), may hold values from -0.0625 to 0.0625
- w_gate: bfloat16 [2, 16, 2048, 768], P('section', 'expert', None, 'shard'), may hold values from -0.125 to 0.125
- w_up: bfloat16 [2, 16, 2048, 768], P('section', 'expert', None, 'shard'), may hold values from -0.125 to 0.125
- w_down: bfloat16 [2, 16, 768, 2048], P('section', 'expert', 'shard'), may hold values from -0.875 to 0.875
Outputs:
- activations: bfloat16 [2, 2, 1024, 2048], P('section', None, 'expert')
- input_grads: bfloat16 [2, 2, 1024, 2048], P('section', None, 'expert')
- grad_norm_attn: float32 [2, 2048], P('section', 'expert')
- grad_norm_ffn: float32 [2, 2048], P('section', 'expert')
- grad_q_gain: float32 [2, 128], P('section', 'expert')
- grad_k_gain: float32 [2, 128], P('section', 'expert')
- grad_query: float32 [2, 2048, 4096], P('section', 'expert', 'shard')
- grad_key: float32 [2, 2048, 512], P('section', 'expert', 'shard')
- grad_value: float32 [2, 2048, 512], P('section', 'expert', 'shard')
- grad_output: float32 [2, 2048, 4096], P('section', 'expert', 'shard')
- grad_router: float32 [2, 2048, 16], P('section', 'expert')
- grad_gate: float32 [2, 16, 2048, 768], P('section', 'expert', None, 'shard')
- grad_up: float32 [2, 16, 2048, 768], P('section', 'expert', None, 'shard')
- grad_down: float32 [2, 16, 768, 2048], P('section', 'expert', 'shard')
The draws below stay inside these ranges and needn't reach their ends.
Inputs may be any that keep to these rules, and one draw needn't show every extreme that they name: `segments`: within a sequence the numbers never fall.
All inputs are finite; a program needn't handle non-finite values.
Results may differ from the reference program's by a relative error of at most 0.035.
Values may be sent and summed in bfloat16 or wider, within the bound.
No kernel may reach another device: no remote copies, remote signals or barrier semaphores. Data moves between devices by JAX's collectives and lax.ppermute only.
A program may use at most 384 MiB of HBM per device.

```python
import math
import jax
import jax.numpy as jnp
import numpy as np
from jax import lax

D = 2048
HEADS = 32
KV = 4
HD = 128
FF = 768
TOP = 8
MAXBLK = 5
MB = 2
TOK = 128
EXP = 16
BLK = 16
CAP = 80
SEQS = 8
TOKENS = 1024
N_SECTION = 2


def set_ends(drawn, key, smallest, high):
    longest = drawn.shape.index(max(drawn.shape))
    spots = []
    for shift in (0, 1):
        where = [jax.random.randint(jax.random.fold_in(key, axis), (), 0, length) for axis, length in enumerate(drawn.shape)]
        where[longest] = (where[longest] + shift) % drawn.shape[longest]
        spots.append(tuple(where))
    return drawn.at[spots[0]].set(smallest).at[spots[1]].set(high)


def levels(key, dims, split, smallest, high):
    gain = 1.0
    for axis_at, shards_of in split:
        draws = jax.random.uniform(jax.random.fold_in(jax.random.fold_in(key, 6), axis_at), (shards_of,), jnp.float32, smallest / len(split), high / len(split))
        gain = gain * jnp.repeat(jnp.exp(draws), dims[axis_at] // shards_of).reshape((-1,) + (1,) * (len(dims) - 1 - axis_at))
    return gain


def split_up(amount, total, limit, lean):
    loads = [(1 << 20) // math.isqrt(grade ** lean) + 1 for grade in range(2, amount + 1)]
    surplus, given = total - limit - (amount - 1), [1] * (amount - 1)
    while surplus > 0:
        movable = [i for i in range(amount - 1) if given[i] < limit]
        whole, budget = sum([loads[i] for i in movable]), surplus
        for i in movable:
            more = min(limit - given[i], max(1, budget * loads[i] // whole), surplus)
            given[i] = given[i] + more
            surplus = surplus - more
    return np.array([limit] + given)


def uneven(own_key, amount, total, reach, slope):
    if amount == 2:
        one = jax.random.randint(own_key, (), max(1, total - reach), min(reach, total - 1) + 1)
        return jnp.stack([one, total - one])
    lengths = jnp.asarray(split_up(amount, total, reach, slope), jnp.int32)
    twos = (amount - 1) // 2
    giver, taker = lengths[1:1 + 2 * twos:2], lengths[2:2 + 2 * twos:2]
    slack = jnp.minimum(giver - 1, reach - taker)
    passed = jax.random.randint(jax.random.fold_in(own_key, 1), (twos,), 0, 1 << 20) % (slack + 1)
    lengths = lengths.at[1:1 + 2 * twos:2].set(giver - passed).at[2:2 + 2 * twos:2].set(taker + passed)
    return lengths[jax.random.permutation(jax.random.fold_in(own_key, 2), amount)]


def assign_block(own_key, own, number, rows, amount, top, limit, skew):
    order = jax.random.permutation(own_key, amount)
    crowded, usual = portions_of(amount, rows * top, limit, skew, True), portions_of(amount, rows * top, limit, skew, False)
    places = jnp.arange(amount)

    def named(lengths, rotation):
        used = int((lengths > 0).sum())
        fixed = max(1, used // 4)
        shifted = fixed + (places - fixed + rotation * (used - fixed)) % max(1, amount - fixed)
        return jnp.zeros((amount,), jnp.int32).at[order[jnp.where(places < fixed, places, shifted)]].set(jnp.asarray(lengths, jnp.int32))

    lengths = jnp.where(number % 4 == 0, named(crowded, number // 4), named(usual, number - number // 4 - 1))
    mixed = jax.random.permutation(jax.random.fold_in(own, 3), amount)
    donor, taker = mixed[0:amount // 2 * 2:2], mixed[1:amount // 2 * 2:2]
    room = jnp.minimum(lengths[donor] - 1, limit - lengths[taker]) // 2
    room = jnp.where((donor == order[0]) | (taker == order[0]) | (lengths[taker] == 0), 0, jnp.maximum(room, 0))
    shifted = jax.random.randint(jax.random.fold_in(own, 4), (amount // 2,), 0, 1 << 20) % (room + 1)
    lengths = lengths.at[donor].add(-shifted).at[taker].add(shifted)
    labels = jnp.searchsorted(jnp.cumsum(lengths), jnp.arange(rows * top), side="right").astype(jnp.int32)
    table = labels.reshape(top, rows).T
    table = table[jax.random.permutation(jax.random.fold_in(own, 1), rows)]
    rotation = jax.random.randint(jax.random.fold_in(own, 2), (rows, 1), 0, top)
    return jnp.take_along_axis(table, (jnp.arange(top)[None, :] + rotation) % top, axis=1)


def portions_of(amount, total, limit, slope, full):
    portions = [(1 << 20) // math.isqrt(grade ** slope) + 1 for grade in range(1, amount + 1)]
    largest = limit if full else min(limit, max(-(-total // amount), total * portions[0] // sum(portions)))
    least = 1 if total - largest >= amount - 1 else 0
    holding, spare = [largest] + [least] * (amount - 1), total - largest - least * (amount - 1)
    while spare > 0:
        free = [i for i in range(1, amount) if holding[i] < largest] or [i for i in range(1, amount) if holding[i] < limit]
        mass, remaining = sum([portions[i] for i in free]), spare
        for i in free:
            extra = min(limit - holding[i], max(1, remaining * portions[i] // mass), spare)
            holding[i] = holding[i] + extra
            spare = spare - extra
    return np.array(holding)


def centred(rng, dims, deviation, most, split=(), kind=jnp.bfloat16):
    entries = jax.random.normal(rng, dims, jnp.float32) * deviation
    if len(split) > 0:
        entries = levels(rng, dims, split, -0.22, 0.18) * entries
    return jnp.clip(entries, min=-most, max=most).astype(kind)


def setup_inputs(seed: int = 0) -> dict:
    arg_keys = jax.random.split(jax.random.key(seed), 18)
    inputs = centred(arg_keys[0], (MB, TOKENS, D), 1.0, 6.0, ((1, 8),))
    cotangent = centred(arg_keys[1], (MB, TOKENS, D), 1.0, 6.0, ((1, 8),))
    segments = jax.vmap(lambda own: jnp.searchsorted(jnp.cumsum(uneven(own, 6, TOK, TOK * 3 // 8, 1)), jnp.arange(TOK), side="right"))(jax.random.split(arg_keys[2], MB * SEQS)).reshape((MB, SEQS, TOK)).astype(jnp.int32)
    routes_keys = jax.random.split(jax.random.fold_in(arg_keys[3], 1), N_SECTION * MB * TOKENS // TOK)
    routes_turns = jax.random.permutation(jax.random.fold_in(arg_keys[3], 3), N_SECTION * MB * TOKENS // TOK)
    routes = jax.vmap(lambda own, number: assign_block(jax.random.fold_in(arg_keys[3], 2), own, number, TOK, EXP, TOP, CAP, 2))(routes_keys, routes_turns).reshape((N_SECTION, MB, TOKENS, TOP))
    counts = set_ends(jax.random.randint(arg_keys[4], (N_SECTION, EXP), 1, MAXBLK + 1), jax.random.fold_in(arg_keys[4], 1), 1, MAXBLK).astype(jnp.int32)
    norm_attn = jnp.clip(1.0 + 0.1 * jax.random.normal(arg_keys[5], (N_SECTION, D), jnp.float32), 0.5, 1.5)
    norm_ffn = jnp.clip(1.0 + 0.1 * jax.random.normal(arg_keys[6], (N_SECTION, D), jnp.float32), 0.5, 1.5)
    q_gain = jnp.clip(1.0 + 0.1 * jax.random.normal(arg_keys[7], (N_SECTION, HD), jnp.float32), 0.5, 1.5)
    k_gain = jnp.clip(1.0 + 0.1 * jax.random.normal(arg_keys[8], (N_SECTION, HD), jnp.float32), 0.5, 1.5)
    w_query = centred(arg_keys[9], (N_SECTION, D, HEADS * HD), D ** -0.5, 0.125, ((0, 2), (1, 8), (2, 2)))
    w_key = centred(arg_keys[10], (N_SECTION, D, KV * HD), D ** -0.5, 0.125, ((0, 2), (1, 8), (2, 2)))
    w_value = centred(arg_keys[11], (N_SECTION, D, KV * HD), D ** -0.5, 0.125, ((0, 2), (1, 8), (2, 2)))
    w_output = centred(arg_keys[12], (N_SECTION, D, HEADS * HD), (HEADS * HD // 16) ** -0.5, 0.375, ((0, 2), (1, 8), (2, 2)))
    w_router = centred(arg_keys[13], (N_SECTION, D, EXP), 0.011, 0.0625, ((0, 2), (1, 8)))
    w_gate = centred(arg_keys[14], (N_SECTION, EXP, D, FF), D ** -0.5, 0.125, ((0, 2), (1, 8), (3, 2)))
    w_up = centred(arg_keys[15], (N_SECTION, EXP, D, FF), D ** -0.5, 0.125, ((0, 2), (1, 8), (3, 2)))
    w_down = centred(arg_keys[16], (N_SECTION, EXP, FF, D), (FF // 16) ** -0.5, 0.875, ((0, 2), (1, 8), (2, 2)))
    return dict(inputs=inputs, cotangent=cotangent, segments=segments, routes=routes, counts=counts, norm_attn=norm_attn, norm_ffn=norm_ffn, q_gain=q_gain, k_gain=k_gain, w_query=w_query, w_key=w_key, w_value=w_value, w_output=w_output, w_router=w_router, w_gate=w_gate, w_up=w_up, w_down=w_down)


@jax.custom_vjp
def low(v):
    return lax.optimization_barrier(v.astype(jnp.bfloat16)).astype(jnp.float32)

@jax.custom_vjp
def low_back(v):
    return v

def low_keep(v):
    return (low(v), None)

def low_pass(kept, grad):
    return (grad,)

def back_keep(v):
    return (v, None)

def back_low(kept, grad):
    return (low(grad),)
low.defvjp(low_keep, low_pass)
low_back.defvjp(back_keep, back_low)
eps = 1e-06
theta = 1000000.0
highest = lax.Precision.HIGHEST

def norm_rows(values, weight):
    inverse = lax.rsqrt(lax.optimization_barrier(jnp.mean(values * values, axis=-1, keepdims=True)) + eps)
    return values * inverse * weight

def rotary_tables(length, head_size):
    halfway = head_size // 2
    frequency = theta ** (-jnp.arange(halfway, dtype=jnp.float32) * 2.0 / head_size)
    angles = jnp.arange(length, dtype=jnp.float32)[:, None] * frequency[None, :]
    return (jnp.cos(angles), jnp.sin(angles))

def rotate(values, cosine, sine_table):
    halfway = values.shape[-1] // 2
    first_half = values[..., :halfway]
    second_half = values[..., halfway:]
    cos_rows = cosine[:, None, :]
    sin_rows = sine_table[:, None, :]
    return jnp.concatenate([first_half * cos_rows - second_half * sin_rows, second_half * cos_rows + first_half * sin_rows], axis=-1)

def router_gates(logits, chosen):
    largest = lax.optimization_barrier(jnp.max(logits, axis=-1, keepdims=True))
    raised = jnp.exp(logits - largest)
    shares = raised / lax.optimization_barrier(jnp.sum(raised, axis=-1, keepdims=True))
    picked = jnp.take_along_axis(shares, chosen, axis=1)
    return picked / lax.optimization_barrier(jnp.sum(picked, axis=-1, keepdims=True))

def attend(pieces):
    query_b, key_b, value_b, seg_ids = pieces
    length, kv_heads, head_size = key_b.shape
    group_size = query_b.shape[1] // kv_heads
    grouped = query_b.reshape(length, kv_heads, group_size, head_size)
    scores = jnp.einsum('tghd,sgd->ghts', grouped, key_b, precision=highest) * head_size ** (-0.5)
    scores = low_back(scores)
    positions = jnp.arange(length)
    allowed = (positions[:, None] >= positions[None, :]) & (seg_ids[:, None] == seg_ids[None, :])
    scores = jnp.where(allowed[None, None], scores, -1e+30)
    largest = lax.optimization_barrier(jnp.max(scores, axis=-1, keepdims=True))
    raised = jnp.exp(scores - largest)
    weights = low(raised / lax.optimization_barrier(jnp.sum(raised, axis=-1, keepdims=True)))
    return jnp.einsum('ghts,sgd->tghd', weights, value_b, precision=highest).reshape(length, -1)

def expert_apply(pieces):
    expert_rows, gate_w, up_w, down_w = pieces
    gate_vals = low_back(jnp.dot(expert_rows, gate_w, precision=highest))
    up_vals = low_back(jnp.dot(expert_rows, up_w, precision=highest))
    hidden_units = low(gate_vals * jax.nn.sigmoid(gate_vals) * up_vals)
    return low(low_back(jnp.dot(hidden_units, down_w, precision=highest)))

def layer_apply(inputs, params, chosen, counts_here, seg_rows):
    seq_count, length = seg_rows.shape
    total_rows, model_width = inputs.shape
    head_size = params['q_gain'].shape[0]
    normed_one = low(norm_rows(inputs, params['norm_attn']))
    query_proj = low_back(jnp.dot(normed_one, params['query'], precision=highest))
    key_proj = low_back(jnp.dot(normed_one, params['key'], precision=highest))
    value_rows = low(low_back(jnp.dot(normed_one, params['value'], precision=highest)))
    cosine, sine_table = rotary_tables(length, head_size)
    query_heads = norm_rows(query_proj.reshape(seq_count, length, -1, head_size), params['q_gain'])
    key_heads = norm_rows(key_proj.reshape(seq_count, length, -1, head_size), params['k_gain'])
    query_b = low(low_back(rotate(query_heads, cosine, sine_table)))
    key_b = low(low_back(rotate(key_heads, cosine, sine_table)))
    value_b = value_rows.reshape(seq_count, length, -1, head_size)
    attended = lax.map(jax.checkpoint(attend), (query_b, key_b, value_b, seg_rows))
    attended = low(low_back(attended.reshape(total_rows, -1)))
    branch = low_back(jnp.dot(attended, params['output'].T, precision=highest))
    hidden = inputs + branch
    normed_two = low(norm_rows(hidden, params['norm_ffn']))
    logits = low_back(jnp.dot(normed_two, params['router'], precision=highest))
    gate_weights = router_gates(logits, chosen)
    experts_all = counts_here.shape[0]
    top_count = chosen.shape[1]
    blocks = total_rows // length
    flat_routes = chosen.reshape(blocks, length * top_count)
    member = (flat_routes[:, :, None] == jnp.arange(experts_all, dtype=jnp.int32)[None, None, :]).astype(jnp.int32)
    rank_ids = lax.optimization_barrier(jnp.sum((jnp.cumsum(member, axis=1) - member) * member, axis=2))
    limits = counts_here[flat_routes] * BLK
    kept_mask = rank_ids < limits
    block_ids = jnp.arange(blocks, dtype=jnp.int32)[:, None]
    dump_slot = experts_all * blocks * CAP
    slot_ids = jnp.where(kept_mask, flat_routes * (blocks * CAP) + block_ids * CAP + rank_ids, dump_slot).reshape(-1).astype(jnp.int32)
    pair_ids = jnp.arange(total_rows * top_count, dtype=jnp.int32)
    owners = jnp.zeros((dump_slot + 1,), jnp.int32).at[slot_ids].set(pair_ids)[:-1]
    filled = jnp.zeros((dump_slot + 1,), inputs.dtype).at[slot_ids].set(1.0)[:-1]
    expert_rows = low_back(normed_two[owners // top_count] * filled[:, None])
    expert_rows = expert_rows.reshape(experts_all, blocks * CAP, model_width)
    outputs = lax.map(jax.checkpoint(expert_apply), (expert_rows, params['gate'], params['up'], params['down']))
    padded = jnp.concatenate([outputs.reshape(-1, model_width), jnp.zeros((1, model_width), inputs.dtype)], axis=0)
    pair_rows = padded[slot_ids].reshape(total_rows, top_count, model_width)
    gated_pairs = gate_weights * kept_mask.reshape(total_rows, top_count).astype(inputs.dtype)
    return hidden + lax.optimization_barrier(jnp.sum(gated_pairs[:, :, None] * pair_rows, axis=1))

def forward(params, inputs, shift_in, routes, counts, segments):
    first_params = jax.tree.map(lambda array_leaf: array_leaf[0], params)
    second_params = jax.tree.map(lambda array_leaf: array_leaf[1], params)
    middles = []
    finals = []
    for micro_index in range(inputs.shape[0]):
        first_out = layer_apply(inputs[micro_index], first_params, routes[0, micro_index], counts[0], segments[micro_index])
        middle = low(low_back(first_out)) + shift_in[micro_index]
        final_out = layer_apply(middle, second_params, routes[1, micro_index], counts[1], segments[micro_index])
        middles.append(middle)
        finals.append(low(low_back(final_out)))
    return (jnp.stack(finals), jnp.stack(middles))

def reference(inputs, cotangent, segments, routes, counts, norm_attn, norm_ffn, q_gain, k_gain, w_query, w_key, w_value, w_output, w_router, w_gate, w_up, w_down):
    params = {'norm_attn': norm_attn.astype(jnp.float32), 'norm_ffn': norm_ffn.astype(jnp.float32), 'q_gain': q_gain.astype(jnp.float32), 'k_gain': k_gain.astype(jnp.float32), 'query': w_query.astype(jnp.float32), 'key': w_key.astype(jnp.float32), 'value': w_value.astype(jnp.float32), 'output': w_output.astype(jnp.float32), 'router': w_router.astype(jnp.float32), 'gate': w_gate.astype(jnp.float32), 'up': w_up.astype(jnp.float32), 'down': w_down.astype(jnp.float32)}
    inputs_f = inputs.astype(jnp.float32)
    shift_zero = jnp.zeros_like(inputs_f)

    def whole_run(param_tree, first_in, shift_vals):
        return forward(param_tree, first_in, shift_vals, routes, counts, segments)
    (finals, middles), pullback = jax.vjp(whole_run, params, inputs_f, shift_zero)
    grads, input_grad, middle_grad = pullback((cotangent.astype(jnp.float32), jnp.zeros_like(middles)))
    activations = jnp.stack([middles, finals]).astype(jnp.bfloat16)
    input_grads = jnp.stack([input_grad, middle_grad]).astype(jnp.bfloat16)
    return (activations, input_grads, grads['norm_attn'], grads['norm_ffn'], grads['q_gain'], grads['k_gain'], grads['query'], grads['key'], grads['value'], grads['output'], grads['router'], grads['gate'], grads['up'], grads['down'])
```

```python
import jax
import jax.numpy as jnp
from jax import lax
from jax.sharding import PartitionSpec as P

C, E, H = "section", "expert", "shard"
f32 = jnp.float32
b16 = jnp.bfloat16

eps = 1e-06
theta = 1000000.0


def core_swap(x):
    return lax.ppermute(x, C, [(0, 1), (1, 0)])


def side_swap(x):
    return lax.ppermute(x, H, [(0, 1), (1, 0)])


def pair_swap(x):
    return lax.ppermute(x, E, [(e, e ^ 1) for e in range(lax.axis_size(E))])


def turn(x, by):
    length = lax.axis_size(E) // 2
    pairs = [(e, (e // 2 + by) % length * 2 + e % 2) for e in range(2 * length)]
    return lax.ppermute(x, E, pairs)


def turns():
    length = lax.axis_size(E) // 2
    return sorted(range(1, length), key=lambda d: (min(d, length - d), d))


def send(x, pairs):
    return lax.ppermute(x, (C, H), [(2 * a + b, 2 * c + d) for (a, b), (c, d) in pairs])


def after(x, marker):
    return lax.optimization_barrier((x, marker))[0]


def pick(x, index, axis=0):
    return lax.dynamic_index_in_dim(x, index, axis, keepdims=False)


def ordered(flag, own, other):
    return jnp.where(flag == 0, jnp.stack([own, other]), jnp.stack([other, own]))


def dot(left, right, at_left, at_right, batch=()):
    return lax.dot_general(
        left, right, (((at_left,), (at_right,)), (batch, batch)), preferred_element_type=f32
    )


def norm_rows(values, weight):
    inverse = lax.rsqrt(jnp.mean(values * values, axis=-1, keepdims=True) + eps)
    return values * inverse * weight


def rotary_tables(length, head_size):
    halfway = head_size // 2
    frequency = theta ** (-jnp.arange(halfway, dtype=f32) * 2.0 / head_size)
    angles = jnp.arange(length, dtype=f32)[:, None] * frequency[None, :]
    cosine, sine = jnp.cos(angles), jnp.sin(angles)
    return (
        jnp.concatenate([cosine, cosine], axis=1)[None, :, None, :],
        jnp.concatenate([-sine, sine], axis=1)[None, :, None, :],
    )


def rotate(values, tables):
    halfway = values.shape[-1] // 2
    turned = jnp.concatenate([values[..., halfway:], values[..., :halfway]], axis=-1)
    return values * tables[0] + turned * tables[1]


def swiglu(gate_vals, up_vals):
    return gate_vals * jax.nn.sigmoid(gate_vals) * up_vals


def gates_of(logits, chosen):
    largest = jnp.max(logits, axis=-1, keepdims=True)
    raised = jnp.exp(logits - largest)
    picked = raised / jnp.sum(raised, axis=-1, keepdims=True) * chosen
    return picked / jnp.sum(picked, axis=-1, keepdims=True)


def route_codes(chosen, counts, block_rows):
    tokens, experts = chosen.shape[0], counts.shape[0]
    ids = jnp.arange(experts, dtype=jnp.int32)
    member = jnp.any(chosen[:, :, None] == ids[None, None, :], axis=1)
    spots = jnp.arange(tokens)
    earlier = (spots[:, None] > spots[None, :]).astype(b16)
    rank = dot(earlier, member.astype(b16), 1, 0)
    kept = member & (rank < (counts * block_rows).astype(f32)[None, :])
    return member.astype(f32) + kept.astype(f32)


def gather_rows(x):
    turned = {0: x}
    for d in turns():
        turned[d] = turn(x, d)
    paired = {d: pair_swap(turned[d]) for d in [0] + turns()}
    length = lax.axis_size(E) // 2
    mine = jnp.stack([p for d in range(length) for p in (turned[d], paired[d])])
    return jnp.stack([mine, core_swap(mine)])


def scatter_rows(part):
    length = lax.axis_size(E) // 2
    summed = part[0].astype(f32) + core_swap(part[1]).astype(f32)
    pieces = summed.reshape((length, 2) + summed.shape[1:])
    lined = {}
    for d in turns()[::-1] + [0]:
        lined[d] = pieces[d, 0] + pair_swap(pieces[d, 1].astype(b16)).astype(f32)
    total = lined[0]
    for d in turns()[::-1]:
        total = total + turn(lined[d].astype(b16), -d).astype(f32)
    return total


def plane_gather(x, pair, half):
    cut = x.shape[1] // 2
    side, other = side_swap(x), pair_swap(x)
    across = jnp.concatenate([pair_swap(side[:, :cut]), side_swap(other[:, cut:])], axis=1)
    own_seq = ordered(half, x, side)
    other_seq = ordered(half, other, across)
    return ordered(pair, own_seq, other_seq).reshape(-1, x.shape[1])


def plane_scatter(part, pair, half):
    width = part.shape[1]
    cut = width // 2
    parts = part.reshape(2, 2, -1, width)
    one, two = parts[..., :cut], parts[..., cut:]
    one = pick(one, pair).astype(f32) + pair_swap(pick(one, 1 - pair)).astype(f32)
    two = pick(two, half, 1).astype(f32) + side_swap(pick(two, 1 - half, 1)).astype(f32)
    one = pick(one, half) + side_swap(pick(one, 1 - half).astype(b16)).astype(f32)
    two = pick(two, pair) + pair_swap(pick(two, 1 - pair).astype(b16)).astype(f32)
    return jnp.concatenate([one, two], axis=1)


def halves_for_cores(packed, core):
    halves = packed.reshape(packed.shape[0], 2, -1, packed.shape[2])
    own = pick(halves, core, 1)
    received = core_swap(pick(halves, 1 - core, 1))
    return jnp.where(core == 0, own, received), jnp.where(core == 0, received, own)


def gather_weight(half_rows, core, pair, line):
    length = lax.axis_size(E) // 2
    keep, got = pick(half_rows, pair), pair_swap(pick(half_rows, 1 - pair))
    both = ordered(pair, keep, got)
    rows, cols = both.shape[1:]
    whole = jnp.zeros((length, 2, 2, rows, cols), b16)
    for d in [0] + turns():
        piece = both if d == 0 else turn(both, d)
        spot = lax.rem(line + length - d, length)
        whole = lax.dynamic_update_slice(whole, piece[None, :, None], (spot, 0, core, 0, 0))
        whole = lax.dynamic_update_slice(
            whole, core_swap(piece)[None, :, None], (spot, 0, 1 - core, 0, 0)
        )
    return whole.reshape(-1, cols)


def scatter_weight(left, right, core, pair, line):
    n = lax.axis_size(E)
    length = n // 2
    tokens = left.shape[0]
    halves = left.reshape(tokens, n, 2, -1)
    lefts = [pick(halves, core, 2), core_swap(pick(halves, 1 - core, 2))]
    joined = jnp.concatenate([a.reshape(tokens, -1) for a in lefts], axis=0)
    rights = jnp.concatenate([right, core_swap(right)], axis=0)
    product = dot(joined, rights, 0, 0).astype(b16)
    pieces = product.reshape(length, 2, -1, right.shape[1])
    total = pick(pieces, line).astype(f32)
    for d in turns():
        total = total + turn(pick(pieces, lax.rem(line + d, length)), d).astype(f32)
    keep = pick(total, pair)
    got = pair_swap(pick(total, 1 - pair).astype(b16)).astype(f32)
    return ordered(pair, keep, got)


def to_owner(first, second, core):
    received = core_swap(jnp.where(core == 0, second, first))
    return ordered(core, jnp.where(core == 0, first, second), received)


def attention_forward(normed, weights_in, weights_out, gains, tables, allowed):
    head_size = gains[0].shape[0]
    length = tables[0].shape[1]
    projected = dot(normed, weights_in, 1, 0)
    cuts = weights_in.shape[1] - 2 * head_size
    query_proj = projected[:, :cuts].reshape(-1, length, cuts // head_size, head_size)
    key_proj = projected[:, cuts : cuts + head_size].reshape(-1, length, 1, head_size)
    value_b = projected[:, cuts + head_size :].astype(b16).reshape(-1, length, head_size)
    sequences, heads = query_proj.shape[0], query_proj.shape[2]
    query_b = rotate(norm_rows(query_proj, gains[0]), tables).astype(b16)
    query_b = query_b.reshape(sequences, -1, head_size)
    key_b = rotate(norm_rows(key_proj, gains[1]), tables).astype(b16).reshape(value_b.shape)
    scores = dot(query_b, key_b, 2, 2, (0,)) * head_size ** (-0.5)
    scores = scores.reshape(sequences, length, heads, length)
    scores = jnp.where(allowed[:, :, None, :], scores, -1e30)
    largest = jnp.max(scores, axis=-1, keepdims=True)
    raised = jnp.exp(scores - largest)
    shares = raised / jnp.sum(raised, axis=-1, keepdims=True)
    shares = shares.reshape(sequences, -1, length)
    attended = dot(shares.astype(b16), value_b, 2, 1, (0,)).astype(b16)
    attended = attended.reshape(sequences * length, -1)
    branch = dot(attended, weights_out, 1, 1).astype(b16)
    return branch, (normed, query_proj, key_proj, query_b, key_b, value_b, shares, attended)


def attention_backward(branch_b, saved, weights_in, weights_out, gains, tables):
    normed, query_proj, key_proj, query_b, key_b, value_b, shares, attended = saved
    head_size = gains[0].shape[0]
    score_scale = head_size ** (-0.5)
    attended_grad = dot(branch_b, weights_out, 1, 0).astype(b16).reshape(query_b.shape)
    value_grad = dot(shares.astype(b16), attended_grad, 1, 1, (0,)).astype(b16)
    share_grad = dot(attended_grad, value_b, 2, 2, (0,))
    delta_rows = jnp.sum(shares * share_grad, axis=-1, keepdims=True)
    score_b = (shares * (share_grad - delta_rows)).astype(b16)
    query_grad = (dot(score_b, key_b, 2, 1, (0,)) * score_scale).astype(b16).astype(f32)
    key_grad = (dot(score_b, query_b, 1, 1, (0,)) * score_scale).astype(b16).astype(f32)

    def prep(query_heads, key_heads, query_gain, key_gain):
        return (
            rotate(norm_rows(query_heads, query_gain), tables),
            rotate(norm_rows(key_heads, key_gain), tables),
        )

    prep_back = jax.vjp(prep, query_proj, key_proj, *gains)[1]
    query_proj_grad, key_proj_grad, q_gain_grad, k_gain_grad = prep_back(
        (query_grad.reshape(query_proj.shape), key_grad.reshape(key_proj.shape))
    )
    rows = normed.shape[0]
    projected_b = jnp.concatenate(
        [
            query_proj_grad.astype(b16).reshape(rows, -1),
            key_proj_grad.astype(b16).reshape(rows, -1),
            value_grad.reshape(rows, -1),
        ],
        axis=1,
    )
    normed_grad = dot(projected_b, weights_in, 1, 1).astype(b16)
    return normed_grad, projected_b, q_gain_grad, k_gain_grad


def local_gates(rows, codes, router, first_expert, local, units):
    experts = router.shape[1]
    gates = gates_of(dot(rows, router, 1, 0), (codes > 0.5).astype(f32))
    gates = jnp.where(codes > 1.5, gates, 0.0)
    ids = jnp.arange(experts, dtype=jnp.int32)[None, :]
    spread = []
    for j in range(local):
        own = jnp.sum(jnp.where(ids == first_expert + j, gates, 0.0), axis=1, keepdims=True)
        spread.append(jnp.broadcast_to(own, (rows.shape[0], units)))
    return jnp.concatenate(spread, axis=1)


def experts_forward(rows, codes, router, weights_gu, weights_down, first_expert, local):
    spread = local_gates(
        rows, codes, router, first_expert, local, weights_down.shape[0] // local
    )
    hidden = dot(rows, weights_gu, 1, 0)
    cut = hidden.shape[1] // 2
    units = swiglu(hidden[:, :cut], hidden[:, cut:])
    units_b = (units * spread).astype(b16)
    part = dot(units_b, weights_down, 1, 0).astype(b16)
    return part, (rows, spread, hidden, units_b)


def experts_backward(grads, saved, weights_gu, weights_down, first_expert, local, experts):
    rows, spread, hidden, units_b = saved
    cut = hidden.shape[1] // 2
    units, swiglu_back = jax.vjp(swiglu, hidden[:, :cut], hidden[:, cut:])
    raw = dot(grads, weights_down, 1, 1)
    gate_grad, up_grad = swiglu_back(raw * spread)
    hidden_b = jnp.concatenate([gate_grad.astype(b16), up_grad.astype(b16)], axis=1)
    part = dot(hidden_b, weights_gu, 1, 1).astype(b16)
    overlap = raw * units
    per = cut // local
    wide = -(-2 * experts // 128) * 128
    ids = jnp.arange(wide, dtype=jnp.int32)[None, :]
    extra = jnp.zeros((grads.shape[0], wide), f32)
    for j in range(local):
        value = jnp.sum(overlap[:, j * per : (j + 1) * per], axis=1, keepdims=True)
        high = value.astype(b16).astype(f32)
        extra = jnp.where(ids == first_expert + j, high, extra)
        extra = jnp.where(ids == experts + first_expert + j, value - high, extra)
    return jnp.concatenate([part, extra.astype(b16)], axis=1), hidden_b


def shards(
    inputs,
    cotangent,
    segments,
    routes,
    counts,
    norm_attn,
    norm_ffn,
    q_gain,
    k_gain,
    w_query,
    w_key,
    w_value,
    w_output,
    w_router,
    w_gate,
    w_up,
    w_down,
):
    core, at, half = lax.axis_index(C), lax.axis_index(E), lax.axis_index(H)
    pair, line = lax.rem(at, 2), at // 2
    n = lax.axis_size(E)
    _, tokens, width = inputs.shape
    rows = tokens // 2
    experts = counts.shape[1]
    local = w_gate.shape[1]
    units = w_gate.shape[3]
    first_expert = at * local
    head_size = q_gain.shape[1]

    def by_group(weight):
        return weight[0].reshape(weight.shape[1], 2, -1).transpose(1, 0, 2)

    packed_in = jnp.concatenate([by_group(w_query), by_group(w_key), by_group(w_value)], axis=2)
    in_halves = halves_for_cores(packed_in, core)
    out_halves = halves_for_cores(by_group(w_output), core)
    weights_in = [gather_weight(in_halves[0], core, pair, line)]
    weights_out = [gather_weight(out_halves[0], core, pair, line)]

    def both_layers(own):
        return ordered(core, own, core_swap(own))

    norm_attn, norm_ffn, q_gain, k_gain = (
        both_layers(a[0]) for a in (norm_attn, norm_ffn, q_gain, k_gain)
    )
    counts = both_layers(counts[0])
    chosen = ordered(core, pick(routes[0], core), core_swap(pick(routes[0], 1 - core)))
    router_rows = w_router[0].reshape(-1, 128)
    router_own = lax.all_gather(router_rows, E, axis=0, tiled=True).reshape(width, experts)
    routers = both_layers(router_own)
    block_rows = tokens * chosen.shape[2] // (4 * experts)
    codes = [route_codes(chosen[l], counts[l], block_rows) for l in range(2)]
    codes = jnp.concatenate(codes, axis=1)
    codes_own = lax.dynamic_slice_in_dim(codes, half * rows, rows, 0)
    wide = -(-2 * experts // 128) * 128
    codes_sent = jnp.pad(codes_own.astype(b16), ((0, 0), (0, wide - 2 * experts)))
    codes_all = gather_rows(codes_sent).reshape(-1, wide).astype(f32)
    codes_own = [codes_own[:, l * experts : (l + 1) * experts] for l in range(2)]
    codes_all = [codes_all[:, l * experts : (l + 1) * experts] for l in range(2)]

    seg_own = pick(segments, core)[0]
    seg_ids = ordered(pair, seg_own, pair_swap(seg_own))
    spots = jnp.arange(tokens)
    allowed = (spots[:, None] >= spots[None, :])[None] & (
        seg_ids[:, :, None] == seg_ids[:, None, :]
    )
    tables = rotary_tables(tokens, head_size)

    at_first = (core == 0) & (half == 0)
    at_last = (core == 1) & (half == 1)
    own_experts = (w_gate[0], w_up[0], w_down[0])

    def experts_of(layer, own):
        if layer == 0:
            by_side = [((0, 0), (0, 1)), ((0, 1), (1, 0))]
            by_core = [((0, 1), (1, 1))]
        else:
            by_side = [((1, 0), (0, 1)), ((1, 1), (1, 0))]
            by_core = [((1, 0), (0, 0))]
        keeps, takes = (at_first, at_last) if layer == 0 else (at_last, at_first)
        gate, up, down = [
            jnp.where(keeps, w, jnp.where(takes, send(w, by_core), send(w, by_side))) for w in own
        ]
        weights_gu = jnp.concatenate([w[j] for w in (gate, up) for j in range(local)], axis=1)
        return weights_gu, down.reshape(-1, width)

    weights_gu, weights_down = [None, None], [None, None]
    weights_gu[0], weights_down[0] = experts_of(0, own_experts)

    layer_in = lax.dynamic_slice_in_dim(pick(inputs, core), half * rows, rows, 0)
    whole_in = pick(inputs, core)
    whole_in = ordered(pair, whole_in, pair_swap(whole_in)).reshape(-1, width)
    normed = norm_rows(whole_in.astype(f32), norm_attn[0]).astype(b16)
    gains = [(q_gain[l], k_gain[l]) for l in range(2)]
    outs, kept_attn, kept_rows, kept_experts = [], [], [], []
    for l in range(2):
        if l == 1:
            mine = norm_rows(layer_in.astype(f32), norm_attn[1]).astype(b16)
            normed = plane_gather(mine, pair, half)
        branch, saved = attention_forward(
            normed, weights_in[l], weights_out[l], gains[l], tables, allowed
        )
        hidden = layer_in.astype(f32) + plane_scatter(branch, pair, half)
        normed_two = norm_rows(hidden, norm_ffn[l]).astype(b16)
        if l == 0:
            marker = normed_two
            weights_in.append(gather_weight(after(in_halves[1], marker), core, pair, line))
            weights_out.append(gather_weight(after(out_halves[1], marker), core, pair, line))
            weights_gu[1], weights_down[1] = experts_of(1, after(own_experts, marker))
        rows_all = gather_rows(normed_two).reshape(-1, width)
        part, saved_experts = experts_forward(
            rows_all,
            codes_all[l],
            routers[l],
            weights_gu[l],
            weights_down[l],
            first_expert,
            local,
        )
        moved = scatter_rows(part.reshape(2, n, rows, width))
        kept_attn.append(saved)
        kept_rows.append((layer_in, hidden, normed_two))
        kept_experts.append(saved_experts)
        layer_in = (hidden + moved).astype(b16)
        outs.append(layer_in)

    grad = lax.dynamic_slice_in_dim(pick(cotangent, core), half * rows, rows, 0)
    grads_in, small, grads_qkv, grads_out, grads_experts = [None] * 2, [None] * 2, [None] * 2, [None] * 2, [None] * 2
    for l in (1, 0):
        layer_in, hidden, normed_two = kept_rows[l]
        grad_f = grad.astype(f32)
        grads_all = gather_rows(grad).reshape(-1, width)
        part, hidden_b = experts_backward(
            grads_all,
            kept_experts[l],
            weights_gu[l],
            weights_down[l],
            first_expert,
            local,
            experts,
        )
        moved = scatter_rows(part.reshape(2, n, rows, -1))
        normed_grad, extra = moved[:, :width], moved[:, width:]
        overlap = extra[:, :experts] + extra[:, experts : 2 * experts]
        chosen_f = (codes_own[l] > 0.5).astype(f32)
        logits = dot(normed_two, routers[l], 1, 0)
        gates_back = jax.vjp(lambda v: gates_of(v, chosen_f), logits)[1]
        logit_b = gates_back(jnp.where(codes_own[l] > 1.5, overlap, 0.0))[0].astype(b16)
        normed_grad = normed_grad + dot(logit_b, routers[l], 1, 1)
        grad_router = dot(logit_b, normed_two, 0, 0)
        hidden_grad, grad_norm_ffn = jax.vjp(norm_rows, hidden, norm_ffn[l])[1](normed_grad)
        hidden_grad = hidden_grad + grad_f
        branch_b = plane_gather(hidden_grad.astype(b16), pair, half)
        normed_grad, projected_b, q_gain_grad, k_gain_grad = attention_backward(
            branch_b, kept_attn[l], weights_in[l], weights_out[l], gains[l], tables
        )
        input_grad, grad_norm_attn = jax.vjp(norm_rows, layer_in.astype(f32), norm_attn[l])[1](
            plane_scatter(normed_grad, pair, half)
        )
        grad = (input_grad + hidden_grad).astype(b16)
        grads_in[l] = grad
        gain_row = jnp.pad(
            jnp.concatenate([q_gain_grad, k_gain_grad]), (0, width - 2 * head_size)
        )
        small[l] = jnp.concatenate(
            [grad_router, grad_norm_attn[None], grad_norm_ffn[None], gain_row[None]], axis=0
        )
        grads_out[l] = scatter_weight(branch_b, kept_attn[l][7], core, pair, line)
        grads_qkv[l] = scatter_weight(kept_attn[l][0], projected_b, core, pair, line)
        rows_all, _, _, units_b = kept_experts[l]
        pieces = [
            dot(rows_all, hidden_b[:, k * units : (k + 1) * units], 0, 0).astype(b16)
            for k in range(2 * local)
        ] + [
            dot(units_b[:, k * units : (k + 1) * units], grads_all, 0, 0).astype(b16)
            for k in range(local)
        ]
        if l == 0:
            by_side = [((0, 1), (0, 0)), ((1, 0), (0, 1))]
            by_core = [((1, 1), (0, 1))]
        else:
            by_side = [((0, 1), (1, 0)), ((1, 0), (1, 1))]
            by_core = [((0, 0), (1, 0))]
        grads_experts[l] = [(p, send(p, by_side), send(p, by_core)) for p in pieces]

    def of_owner(k):
        own = jnp.where(core == 0, grads_experts[0][k][0], grads_experts[1][k][0])
        total = jnp.where(core == half, own.astype(f32), 0.0)
        for l in range(2):
            total = total + grads_experts[l][k][1].astype(f32) + grads_experts[l][k][2].astype(f32)
        return total

    expert_grads = [of_owner(k) for k in range(3 * local)]
    grad_gate, grad_up, grad_down = (
        jnp.stack(expert_grads[i * local : (i + 1) * local]) for i in range(3)
    )

    def columns(block):
        return block.transpose(0, 2, 1, 3).reshape(width // n, -1)

    qkv = to_owner(grads_qkv[0], grads_qkv[1], core)
    cut = qkv.shape[3] - 2 * head_size
    grad_query = columns(qkv[..., :cut])
    grad_key = columns(qkv[..., cut : cut + head_size])
    grad_value = columns(qkv[..., cut + head_size :])
    grad_output = columns(to_owner(grads_out[0], grads_out[1], core))

    small = lax.psum(jnp.stack(small), (C, E, H))
    small = pick(small, core)
    small_here = lax.dynamic_slice_in_dim(small, at * (width // n), width // n, 1)
    gain_rows = small[experts + 2, : 2 * head_size].reshape(2, n, head_size // n)
    gain_rows = pick(gain_rows, at, 1)

    def both_batches(first, second):
        received = core_swap(jnp.where(core == 0, second, first))
        mine = ordered(core, jnp.where(core == 0, first, second), received)
        return ordered(half, mine, side_swap(mine)).transpose(1, 0, 2, 3).reshape(2, tokens, width)

    activations = both_batches(outs[0], outs[1])
    input_grads = both_batches(grads_in[0], grads_in[1])
    return (
        activations[None],
        input_grads[None],
        small_here[experts][None],
        small_here[experts + 1][None],
        gain_rows[0][None],
        gain_rows[1][None],
        grad_query[None],
        grad_key[None],
        grad_value[None],
        grad_output[None],
        small_here[:experts].T[None],
        grad_gate[None],
        grad_up[None],
        grad_down[None],
    )


def solution(mesh):
    by_layer = P(C, None)
    in_specs = (
        P(None, E, None),
        P(None, E, None),
        P(None, E, None),
        P(C, None, E, None),
        by_layer,
        by_layer,
        by_layer,
        by_layer,
        by_layer,
        P(C, E, H),
        P(C, E, H),
        P(C, E, H),
        P(C, E, H),
        P(C, E, None),
        P(C, E, None, H),
        P(C, E, None, H),
        P(C, E, H, None),
    )
    out_specs = (
        P(C, None, E, None),
        P(C, None, E, None),
        P(C, E),
        P(C, E),
        P(C, E),
        P(C, E),
        P(C, E, H),
        P(C, E, H),
        P(C, E, H),
        P(C, E, H),
        P(C, E, None),
        P(C, E, None, H),
        P(C, E, None, H),
        P(C, E, H, None),
    )
    return jax.shard_map(shards, mesh=mesh, in_specs=in_specs, out_specs=out_specs, check_vma=False)
```

```python
import functools

import jax
import jax.numpy as jnp
from jax import lax
from jax.experimental import pallas as pl
from jax.experimental.pallas import tpu as pltpu
from jax.sharding import PartitionSpec as P

C, E, H = "section", "expert", "shard"
f32 = jnp.float32
b16 = jnp.bfloat16

eps = 1e-06
theta = 1000000.0


def core_swap(x):
    return lax.ppermute(x, C, [(0, 1), (1, 0)])


def side_swap(x):
    return lax.ppermute(x, H, [(0, 1), (1, 0)])


def near_swap(x):
    return lax.ppermute(x, E, [(e, e ^ 1) for e in range(lax.axis_size(E))])


def pair_swap(x):
    return lax.ppermute(x, E, [(e, e ^ 2) for e in range(lax.axis_size(E))])


def turn(x, by):
    length = lax.axis_size(E) // 4
    pairs = [(e, (e // 4 + by) % length * 4 + e % 4) for e in range(4 * length)]
    return lax.ppermute(x, E, pairs)


def turns():
    length = lax.axis_size(E) // 4
    return sorted(range(1, length), key=lambda d: (min(d, length - d), d))


def send(x, pairs):
    return lax.ppermute(x, (C, H), [(2 * a + b, 2 * c + d) for (a, b), (c, d) in pairs])


def tie(*refs):
    pass


def after(x, *markers):
    leaves, tree = jax.tree.flatten(x)
    here = pl.BlockSpec(memory_space=pl.ANY)
    tied = pl.pallas_call(
        tie,
        out_shape=[jax.ShapeDtypeStruct(a.shape, a.dtype) for a in leaves],
        in_specs=[here] * (len(leaves) + len(markers)),
        out_specs=[here] * len(leaves),
        input_output_aliases={i: i for i in range(len(leaves))},
        cost_estimate=pl.CostEstimate(flops=0, bytes_accessed=0, transcendentals=0),
    )(*leaves, *markers)
    return jax.tree.unflatten(tree, tied)


def pick(x, index, axis=0):
    return lax.dynamic_index_in_dim(x, index, axis, keepdims=False)


def either(flag, first, second):
    return jnp.where(flag == 0, first, second)


def ordered(flag, own, other):
    return jnp.where(flag == 0, jnp.stack([own, other]), jnp.stack([other, own]))


def dot(left, right, at_left, at_right, batch=()):
    return lax.dot_general(
        left, right, (((at_left,), (at_right,)), (batch, batch)), preferred_element_type=f32
    )


def norm_rows(values, weight):
    inverse = lax.rsqrt(jnp.mean(values * values, axis=-1, keepdims=True) + eps)
    return values * inverse * weight


def rotary_tables(length, head_size):
    halfway = head_size // 2
    frequency = theta ** (-jnp.arange(halfway, dtype=f32) * 2.0 / head_size)
    angles = jnp.arange(length, dtype=f32)[:, None] * frequency[None, :]
    cosine, sine = jnp.cos(angles), jnp.sin(angles)
    return (
        jnp.concatenate([cosine, cosine], axis=1),
        jnp.concatenate([-sine, sine], axis=1),
    )


def swiglu(gate_vals, up_vals):
    return gate_vals * jax.nn.sigmoid(gate_vals) * up_vals


def gates_of(logits, chosen):
    largest = jnp.max(logits, axis=-1, keepdims=True)
    raised = jnp.exp(logits - largest)
    picked = raised / jnp.sum(raised, axis=-1, keepdims=True) * chosen
    return picked / jnp.sum(picked, axis=-1, keepdims=True)


def route_codes(chosen, counts, block_rows):
    tokens, experts = chosen.shape[0], counts.shape[0]
    ids = jnp.arange(experts, dtype=jnp.int32)
    member = jnp.any(chosen[:, :, None] == ids[None, None, :], axis=1)
    spots = jnp.arange(tokens)
    earlier = (spots[:, None] > spots[None, :]).astype(b16)
    rank = dot(earlier, member.astype(b16), 1, 0)
    kept = member & (rank < (counts * block_rows).astype(f32)[None, :])
    return member.astype(f32) + kept.astype(f32)


def gather_rows(x):
    length = lax.axis_size(E) // 4
    held = {(0, 0): x}
    for d in turns():
        held[d, 0] = turn(x, d)
    for d in [0] + turns():
        held[d, 1] = pair_swap(held[d, 0])
    near = {k: near_swap(held[k]) for k in sorted(held, key=lambda k: sum(k))}
    spots = [(d, p) for d in range(length) for p in range(2)]
    mine = jnp.concatenate([v for k in spots for v in (held[k], near[k])], axis=0)
    return mine, core_swap(mine)


def scatter_rows(pieces):
    length = lax.axis_size(E) // 4
    pieces = pieces.reshape((length, 2, 2) + pieces.shape[1:])
    far = turns()[::-1] + [0]
    held = {}
    for p in (1, 0):
        for d in far:
            held[d, p] = pieces[d, p, 0].astype(f32)
            held[d, p] += near_swap(pieces[d, p, 1].astype(b16)).astype(f32)
    lined = {d: held[d, 0] + pair_swap(held[d, 1].astype(b16)).astype(f32) for d in far}
    total = lined[0]
    for d in far[:-1]:
        total = total + turn(lined[d].astype(b16), -d).astype(f32)
    return total


def sum_cores(own, other):
    summed = own.astype(f32) + core_swap(other).astype(f32)
    return summed.reshape(lax.axis_size(E), -1, own.shape[1])


def position(at):
    length = lax.axis_size(E) // 4
    spots = jnp.arange(4 * length)
    return lax.rem(at // 4 + length - spots // 4, length) * 4 + ((at % 4) ^ (spots % 4))


def plane_gather(x, pair, half):
    cut = x.shape[1] // 2
    side, other = side_swap(x), pair_swap(x)
    across = jnp.concatenate([pair_swap(side[:, :cut]), side_swap(other[:, cut:])], axis=1)
    own_seq = ordered(half, x, side)
    other_seq = ordered(half, other, across)
    return ordered(pair, own_seq, other_seq).reshape(-1, x.shape[1])


def plane_scatter(part, pair, half):
    width = part.shape[1]
    cut = width // 2
    parts = part.reshape(2, 2, -1, width)
    one, two = parts[..., :cut], parts[..., cut:]
    one = either(pair, one[0], one[1]).astype(f32) + pair_swap(
        either(pair, one[1], one[0])
    ).astype(f32)
    two = either(half, two[:, 0], two[:, 1]).astype(f32) + side_swap(
        either(half, two[:, 1], two[:, 0])
    ).astype(f32)
    one = either(half, one[0], one[1]) + side_swap(
        either(half, one[1], one[0]).astype(b16)
    ).astype(f32)
    two = either(pair, two[0], two[1]) + pair_swap(
        either(pair, two[1], two[0]).astype(b16)
    ).astype(f32)
    return jnp.concatenate([one, two], axis=1)


def halves_for_cores(packed, core):
    rows = packed.shape[1] // 2
    first, second = packed[:, :rows], packed[:, rows:]
    own, received = either(core, first, second), core_swap(either(core, second, first))
    return either(core, own, received), either(core, received, own)


def pair_rows(half_rows, pair):
    first, second = half_rows[0], half_rows[1]
    return ordered(pair, either(pair, first, second), pair_swap(either(pair, second, first)))


def relative_order(core, at):
    length = lax.axis_size(E) // 4
    spots = jnp.arange(16 * length // 2)
    c, d, y, p = spots // (4 * length), spots // 4 % length, spots // 2 % 2, spots % 2
    line = lax.rem(at // 4 + length - d, length)
    order = ((line * 2 + p) * 2 + (y ^ (at % 2))) * 2 + (c ^ core)
    line, p, y, c = spots // 8, spots // 4 % 2, spots // 2 % 2, spots % 2
    d = lax.rem(at // 4 + length - line, length)
    back = (((c ^ core) * length + d) * 2 + (y ^ (at % 2))) * 2 + p
    return order, back


def move_blocks(order, x, out, back=False):
    wide = x.shape[1] // order.shape[0]
    if wide % 128:
        out[...] = x[...]
        return
    for j in range(order.shape[0]):
        at = pl.multiple_of(order[j] * wide, wide)
        if back:
            out[:, pl.ds(at, wide)] = x[:, j * wide : (j + 1) * wide]
        else:
            out[:, j * wide : (j + 1) * wide] = x[:, pl.ds(at, wide)]


def shuffle_outside(x, order):
    blocks = order.shape[0]
    if x.shape[1] // blocks % 128 == 0:
        return x
    return jnp.take(x.reshape(x.shape[0], blocks, -1), order, axis=1).reshape(x.shape)


def gather_weight(both):
    cols = both.shape[2]
    held = [both] + [turn(both, d) for d in range(1, lax.axis_size(E) // 4)]
    mine = [jnp.concatenate([h, near_swap(h)], axis=0) for h in held]
    swapped = [core_swap(m) for m in mine]
    whole = jnp.concatenate(mine + swapped, axis=0)
    return whole.reshape(-1, cols), held[-1]


def weight_product(left, right):
    n = lax.axis_size(E)
    half = left.shape[1] // 2
    joined = jnp.concatenate([left[:, :half], core_swap(left[:, half:])], axis=0)
    rights = jnp.concatenate([right, core_swap(right)], axis=0)
    product = dot(joined, rights, 0, 0).astype(b16)
    return product.reshape(n // 4, 2, 2, -1, right.shape[1])


def near_parts(pieces):
    return pieces[:, 0], near_swap(pieces[:, 1])


def turn_parts(sums):
    return sums[0], [
        turn(sums[d].astype(b16), -d) for d in range(1, lax.axis_size(E) // 4)
    ]


def near_sums(parts, *markers):
    kept, got = parts
    return kept.astype(f32) + (after(got, *markers) if markers else got).astype(f32)


def turn_sums(parts, *markers):
    kept, got = parts
    return kept + sum(g.astype(f32) for g in (after(got, *markers) if markers else got))


def pair_columns(total, pair):
    keep = either(pair, total[0], total[1])
    got = pair_swap(either(pair, total[1], total[0]).astype(b16)).astype(f32)
    return ordered(pair, keep, got)


def to_owner(first, second, core):
    received = core_swap(either(core, second, first))
    return ordered(core, either(core, first, second), received)


def head_norm(x):
    inverse = lax.rsqrt(jnp.mean(x * x, axis=-1, keepdims=True) + eps)
    return x * inverse, inverse


def attend(order, normed, w_in, w_out, gains, cosine, sine, allowed, *refs):
    branch, moved, proj, query, key, value, shares, attended, mixed = refs
    rows, head = cosine.shape
    length = allowed.shape[1]
    heads = w_out.shape[1] // head
    move_blocks(order, normed, moved)
    proj[...] = dot(moved[...], w_in[...], 1, 0)

    def prepared(x, gain):
        turned = head_norm(x)[0] * gain
        return (turned * cosine[...] + pltpu.roll(turned, head // 2, 1) * sine[...]).astype(b16)

    for h in range(heads):
        q = prepared(proj[:, h * head : (h + 1) * head], gains[0:1])
        for s in range(rows // length):
            query[s, h * length : (h + 1) * length] = q[s * length : (s + 1) * length]
    key[...] = prepared(proj[:, heads * head : (heads + 1) * head], gains[1:2])
    value[...] = proj[:, (heads + 1) * head :].astype(b16)
    for s in range(rows // length):
        own = slice(s * length, (s + 1) * length)
        scores = dot(query[s], key[own], 1, 1) * head ** (-0.5)
        scores = scores.reshape(heads, length, length)
        scores = jnp.where((allowed[s] > 0)[None], scores, -1e30)
        raised = jnp.exp(scores - jnp.max(scores, axis=-1, keepdims=True))
        weights = raised / jnp.sum(raised, axis=-1, keepdims=True)
        weights = weights.reshape(heads * length, length)
        shares[s] = weights
        result = dot(weights.astype(b16), value[own], 1, 0).astype(b16)
        for h in range(heads):
            attended[own, h * head : (h + 1) * head] = result[h * length : (h + 1) * length]
    mixed[...] = dot(attended[...], w_out[...], 1, 1).astype(b16)
    move_blocks(order, mixed, branch, back=True)


def attend_back(
    order, grads, w_in, w_out, gains, cosine, sine, proj, query, key, value, shares, *refs
):
    back, moved, projected, gain_grads, spread, mixed = refs
    rows, head = cosine.shape
    length = shares.shape[2]
    heads = w_out.shape[1] // head
    scale = head ** (-0.5)
    move_blocks(order, grads, moved)
    attended = dot(moved[...], w_out[...], 1, 0).astype(b16)
    for h in range(heads):
        for s in range(rows // length):
            spread[s, h * length : (h + 1) * length] = attended[
                s * length : (s + 1) * length, h * head : (h + 1) * head
            ]
    query_grads, key_grads = [], []
    for s in range(rows // length):
        own = slice(s * length, (s + 1) * length)
        weights = shares[s]
        given = spread[s]
        value_grad = dot(weights.astype(b16), given, 0, 0).astype(b16)
        projected[own, (heads + 1) * head :] = value_grad
        share_grad = dot(given, value[own], 1, 1)
        delta = jnp.sum(weights * share_grad, axis=-1, keepdims=True)
        score = (weights * (share_grad - delta)).astype(b16)
        query_grads.append((dot(score, key[own], 1, 0) * scale).astype(b16).astype(f32))
        key_grads.append((dot(score, query[s], 0, 0) * scale).astype(b16).astype(f32))

    def prepared_back(grad, x, gain):
        turned = grad * cosine[...] + pltpu.roll(grad * sine[...], head // 2, 1)
        normed, inverse = head_norm(x)
        scaled = turned * gain
        mean = jnp.mean(scaled * normed, axis=-1, keepdims=True)
        gain_grad = jnp.sum(turned * normed, axis=0, keepdims=True)
        return ((scaled - normed * mean) * inverse).astype(b16), gain_grad

    total = jnp.zeros((1, head), f32)
    for h in range(heads):
        grad = jnp.concatenate([g[h * length : (h + 1) * length] for g in query_grads], axis=0)
        at = slice(h * head, (h + 1) * head)
        projected[:, at], gain_grad = prepared_back(grad, proj[:, at], gains[0:1])
        total = total + gain_grad
    at = slice(heads * head, (heads + 1) * head)
    grad = jnp.concatenate(key_grads, axis=0)
    projected[:, at], gain_grad = prepared_back(grad, proj[:, at], gains[1:2])
    gain_grads[0:1] = total
    gain_grads[1:2] = gain_grad
    mixed[...] = dot(projected[...], w_in[...], 1, 1).astype(b16)
    move_blocks(order, mixed, back, back=True)


def in_vmem(kernel, outs, scratch, order, *args):
    whole = pl.BlockSpec(memory_space=pltpu.VMEM)
    return pl.pallas_call(
        kernel,
        out_shape=[jax.ShapeDtypeStruct(*o) for o in outs],
        in_specs=[pl.BlockSpec(memory_space=pltpu.SMEM)] + [whole] * len(args),
        out_specs=[whole] * len(outs),
        scratch_shapes=[pltpu.VMEM(*o) for o in scratch],
        compiler_params=pltpu.CompilerParams(vmem_limit_bytes=48 << 20),
        cost_estimate=pl.CostEstimate(flops=0, bytes_accessed=0, transcendentals=0),
    )(order, *args)


def attention_forward(normed, orders, weights_in, weights_out, gains, tables, allowed):
    rows, width = normed.shape
    cols, heads_cols = weights_in.shape[1], weights_out.shape[1]
    head, length = gains.shape[1], allowed.shape[1]
    stacked = (rows // length, heads_cols // head * length)
    outs = [
        ((rows, width), b16),
        ((rows, width), b16),
        ((rows, cols), f32),
        (stacked + (head,), b16),
        ((rows, head), b16),
        ((rows, head), b16),
        (stacked + (length,), f32),
        ((rows, heads_cols), b16),
    ]
    branch, *saved = in_vmem(
        attend,
        outs,
        [((rows, width), b16)],
        orders[0],
        shuffle_outside(normed, orders[0]),
        weights_in,
        weights_out,
        gains,
        *tables,
        allowed,
    )
    return shuffle_outside(branch, orders[1]), saved


def attention_backward(grads, orders, saved, weights_in, weights_out, gains, tables):
    rows, width = grads.shape
    _, proj, query, key, value, shares, _ = saved
    outs = [
        ((rows, width), b16),
        ((rows, width), b16),
        (proj.shape, b16),
        (gains.shape, f32),
    ]
    back, *others = in_vmem(
        attend_back,
        outs,
        [(query.shape, b16), ((rows, width), b16)],
        orders[0],
        shuffle_outside(grads, orders[0]),
        weights_in,
        weights_out,
        gains,
        *tables,
        proj,
        query,
        key,
        value,
        shares,
    )
    return [shuffle_outside(back, orders[1])] + others


def local_gates(rows, codes, router, first_expert, local):
    gates = gates_of(dot(rows, router, 1, 0), (codes > 0.5).astype(f32))
    gates = jnp.where(codes > 1.5, gates, 0.0)
    ids = jnp.arange(router.shape[1], dtype=jnp.int32)[None, :]
    return [
        jnp.sum(jnp.where(ids == first_expert + j, gates, 0.0), axis=1, keepdims=True)
        for j in range(local)
    ]


def spread(gates, width):
    per = width // len(gates)
    return jnp.concatenate([jnp.broadcast_to(g, (g.shape[0], per)) for g in gates], axis=1)


def experts_forward(rows, codes, router, weights_gu, first_expert, local):
    gates = local_gates(rows, codes, router, first_expert, local)
    hidden = dot(rows, weights_gu, 1, 0)
    cut = hidden.shape[1] // 2
    units = swiglu(hidden[:, :cut], hidden[:, cut:])
    units_b = (units * spread(gates, cut)).astype(b16)
    return rows, gates, hidden, units_b


def experts_backward(grads, saved, weights_gu, weights_down, first_expert, local, experts):
    rows, gates, hidden, units_b = saved
    cut = hidden.shape[1] // 2
    units, swiglu_back = jax.vjp(swiglu, hidden[:, :cut], hidden[:, cut:])
    raw = dot(grads, weights_down, 1, 1)
    gate_grad, up_grad = swiglu_back(raw * spread(gates, cut))
    hidden_b = jnp.concatenate([gate_grad.astype(b16), up_grad.astype(b16)], axis=1)
    part = dot(hidden_b, weights_gu, 1, 1).astype(b16)
    overlap = raw * units
    per = cut // local
    wide = -(-2 * experts // 128) * 128
    ids = jnp.arange(wide, dtype=jnp.int32)[None, :]
    extra = jnp.zeros((grads.shape[0], wide), f32)
    for j in range(local):
        value = jnp.sum(overlap[:, j * per : (j + 1) * per], axis=1, keepdims=True)
        high = value.astype(b16).astype(f32)
        extra = jnp.where(ids == first_expert + j, high, extra)
        extra = jnp.where(ids == experts + first_expert + j, value - high, extra)
    return jnp.concatenate([part, extra.astype(b16)], axis=1), hidden_b


def own_sums(steps, flags, *refs):
    parts = len(steps)
    ins, outs = refs[: 6 * parts], refs[6 * parts :]

    def write(own, side, core):
        total = side[...].astype(f32) + core[...].astype(f32)
        total = total + jnp.where(flags[0] == flags[1], own[...].astype(f32), 0.0)
        if len(outs) == 1:
            outs[0][...] = total
            return
        per = outs[0].shape[2]
        for i, out in enumerate(outs):
            for j in range(out.shape[0]):
                at = (i * out.shape[0] + j) * per
                out[j] = total[:, at : at + per]

    at = pl.program_id(0)
    for l in range(2):
        for k, (first, last) in enumerate(steps):

            @pl.when((flags[0] == l) & (at >= first) & (at < last))
            def _():
                base = 3 * (l * parts + k)
                write(*ins[base : base + 3])


def owned(core, half, by_layer, pieces):
    step = 256
    steps, specs, rows = [], [], 0
    for own, _, _ in by_layer[0]:
        steps.append((rows // step, (rows + own.shape[0]) // step))
        rows += own.shape[0]
    cols = by_layer[0][0][0].shape[1]
    for l in range(2):
        for first, last in steps:

            def where(i, f, l=l, first=first, last=last):
                inside = jnp.clip(i - first, 0, last - first - 1)
                return jnp.where(f[0] == l, inside, 0), 0

            specs += [pl.BlockSpec((step, cols), where)] * 3
    if pieces == 1:
        outs = [jax.ShapeDtypeStruct((rows, cols), f32)]
        out_specs = [pl.BlockSpec((step, cols), lambda i, f: (i, 0))]
    else:
        shape = (pieces // 2, rows, cols // pieces)
        outs = [jax.ShapeDtypeStruct(shape, f32)] * 2
        block = (pieces // 2, step, cols // pieces)
        out_specs = [pl.BlockSpec(block, lambda i, f: (0, i, 0))] * 2
    terms = [t for layer in by_layer for part in layer for t in part]
    return pl.pallas_call(
        functools.partial(own_sums, steps),
        grid_spec=pltpu.PrefetchScalarGridSpec(
            num_scalar_prefetch=1, grid=(rows // step,), in_specs=specs, out_specs=out_specs
        ),
        out_shape=outs,
        compiler_params=pltpu.CompilerParams(vmem_limit_bytes=48 << 20),
        cost_estimate=pl.CostEstimate(flops=0, bytes_accessed=0, transcendentals=0),
    )(jnp.stack([core, half]).astype(jnp.int32), *terms)


def shards(
    inputs,
    cotangent,
    segments,
    routes,
    counts,
    norm_attn,
    norm_ffn,
    q_gain,
    k_gain,
    w_query,
    w_key,
    w_value,
    w_output,
    w_router,
    w_gate,
    w_up,
    w_down,
):
    core, at, half = lax.axis_index(C), lax.axis_index(E), lax.axis_index(H)
    pair = lax.rem(at // 2, 2)
    n = lax.axis_size(E)
    _, tokens, width = inputs.shape
    rows = tokens // 2
    experts = counts.shape[1]
    local = w_gate.shape[1]
    units = w_gate.shape[3]
    first_expert = at * local
    head_size = q_gain.shape[1]

    def by_group(weight):
        return weight[0].reshape(weight.shape[1], 2, -1).transpose(1, 0, 2)

    orders = relative_order(core, at)
    packed = jnp.concatenate([by_group(w) for w in (w_query, w_key, w_value, w_output)], axis=2)
    halves = halves_for_cores(packed, core)
    cut = packed.shape[2] - w_output.shape[2] // 2
    weights_in, weights_out = [None, None], [None, None]
    first = [pair_rows(h, pair) for h in (halves[0][..., :cut], halves[0][..., cut:])]
    (weights_in[0], _), (weights_out[0], arrived) = (gather_weight(h) for h in first)
    second_pair = pair_rows(after(halves[1], arrived), pair)
    second = [second_pair] + [turn(second_pair, d) for d in range(1, n // 4)]
    second[0] = jnp.concatenate([second_pair, near_swap(second_pair)], axis=0)

    def both_layers(own):
        return ordered(core, own, core_swap(own))

    norm_attn, norm_ffn, q_gain, k_gain = (
        both_layers(a[0]) for a in (norm_attn, norm_ffn, q_gain, k_gain)
    )
    counts = both_layers(counts[0])
    chosen = ordered(core, pick(routes[0], core), core_swap(pick(routes[0], 1 - core)))
    block_rows = tokens * chosen.shape[2] // (4 * experts)
    codes = [route_codes(chosen[l], counts[l], block_rows) for l in range(2)]
    codes = jnp.concatenate(codes, axis=1)
    codes_own = lax.dynamic_slice_in_dim(codes, half * rows, rows, 0)
    wide = -(-2 * experts // 128) * 128
    codes_sent = jnp.pad(codes_own.astype(b16), ((0, 0), (0, wide - 2 * experts)))
    router_sent = w_router[0].reshape(-1, wide)
    tables_sent = jnp.concatenate([codes_sent, router_sent], axis=0)
    tables_all = [t.reshape(n, -1, wide) for t in gather_rows(after(tables_sent, first[0]))]
    codes_all = [t[:, :rows].reshape(-1, wide).astype(f32) for t in tables_all]
    routers = [jnp.take(t[:, rows:], position(at), axis=0) for t in tables_all]
    routers = ordered(core, *routers).reshape(2, width, experts)
    codes_own = [codes_own[:, l * experts : (l + 1) * experts] for l in range(2)]
    codes_all = [[c[:, l * experts : (l + 1) * experts] for c in codes_all] for l in range(2)]

    seg_own = pick(segments, core)[0]
    seg_ids = ordered(pair, seg_own, pair_swap(seg_own))
    spots = jnp.arange(tokens)
    allowed = (spots[:, None] >= spots[None, :])[None] & (
        seg_ids[:, :, None] == seg_ids[:, None, :]
    )
    allowed = allowed.astype(f32)
    tables = [jnp.concatenate([t, t], axis=0) for t in rotary_tables(tokens, head_size)]

    at_first = (core == 0) & (half == 0)
    at_last = (core == 1) & (half == 1)
    own_gu = jnp.concatenate([w[0, j] for w in (w_gate, w_up) for j in range(local)], axis=1)
    own_down = w_down[0].reshape(-1, width)

    def experts_sent(layer, own):
        if layer == 0:
            by_side = [((0, 0), (0, 1)), ((0, 1), (1, 0))]
            by_core = [((0, 1), (1, 1))]
        else:
            by_side = [((1, 0), (0, 1)), ((1, 1), (1, 0))]
            by_core = [((1, 0), (0, 0))]
        sent = []
        for w in own:
            if sent:
                w = after(w, sent[-1][0])
            sent.append((send(w, by_side), send(w, by_core)))
        return sent

    def experts_of(layer, sent):
        keeps, takes = (at_first, at_last) if layer == 0 else (at_last, at_first)
        return [
            jnp.where(keeps, own, jnp.where(takes, by_core, by_side))
            for own, (by_side, by_core) in zip((own_gu, own_down), sent)
        ]

    weights_gu, weights_down = [None, None], [None, None]
    sent = experts_sent(0, (own_gu, own_down))

    layer_in = lax.dynamic_slice_in_dim(pick(inputs, core), half * rows, rows, 0)
    whole_in = pick(inputs, core)
    whole_in = ordered(pair, whole_in, pair_swap(whole_in)).reshape(-1, width)
    normed = norm_rows(whole_in.astype(f32), norm_attn[0]).astype(b16)
    normed = after(normed, sent[0][0], sent[1][0])
    gains = jnp.stack([q_gain, k_gain], axis=1)
    outs, kept_attn, kept_rows, kept_experts = [], [], [], []
    for l in range(2):
        if l == 1:
            mine = norm_rows(layer_in.astype(f32), norm_attn[1]).astype(b16)
            mine = after(mine, sent[0][0], sent[1][0])
            grad = lax.dynamic_slice_in_dim(pick(cotangent, core), half * rows, rows, 0)
            grads_all = gather_rows(after(grad, layer_in))
            normed = plane_gather(mine, pair, half)
        branch, saved = attention_forward(
            normed, orders, weights_in[l], weights_out[l], gains[l], tables, allowed
        )
        if l == 1:
            branch = after(branch, *grads_all)
        if l == 0:
            branch = after(branch, *codes_all[0], *codes_all[1], routers)
        hidden = layer_in.astype(f32) + plane_scatter(branch, pair, half)
        normed_two = norm_rows(hidden, norm_ffn[l]).astype(b16)
        if l == 0:
            normed_two = after(normed_two, *second)
            swapped = [core_swap(after(second[0], normed_two))]
        weights_gu[l], weights_down[l] = experts_of(l, after(sent, normed_two))
        if l == 0:
            sent = experts_sent(1, after((own_gu, own_down), normed_two))
        rows_all = gather_rows(normed_two)
        if l == 0:
            late = after(second[1:], rows_all[0])
            late = [jnp.concatenate([p, near_swap(p)], axis=0) for p in late]
        kept_experts.append(
            [
                experts_forward(r, c, routers[l], weights_gu[l], first_expert, local)
                for r, c in zip(rows_all, codes_all[l])
            ]
        )
        kept_attn.append(saved)
        kept_rows.append((layer_in, hidden, normed_two))
        if l == 0:
            parts = [dot(k[3], weights_down[l], 1, 0).astype(b16) for k in kept_experts[l]]
            summed = sum_cores(*parts)
            late = after(late, summed)
            swapped += [core_swap(p) for p in late]
            whole = [second[0]] + late + swapped
            weights_in[1], weights_out[1] = (
                jnp.concatenate([p[..., a:b] for p in whole], axis=0).reshape(-1, b - a)
                for a, b in ((0, cut), (cut, packed.shape[2]))
            )
            layer_in = (hidden + scatter_rows(summed)).astype(b16)

    grads_in, small, grads_experts = ([None] * 2 for _ in range(3))

    def expert_grads(l, marker, grads_all, hidden_b):
        rows_all, units_b = ([k[i] for k in kept_experts[l]] for i in (0, 3))
        units_b, hidden_b = after((units_b, hidden_b), marker)
        cuts = [slice(0, width // 2), slice(width // 2, width)]
        return [
            sum(dot(a[:, c], b, 0, 0) for a, b in zip(rows_all, hidden_b)).astype(b16)
            for c in cuts
        ] + [sum(dot(a, b, 0, 0) for a, b in zip(units_b, grads_all)).astype(b16)]

    def to_owners(l, piece):
        if l == 0:
            by_side = [((0, 1), (0, 0)), ((1, 0), (0, 1))]
            by_core = [((1, 1), (0, 1))]
        else:
            by_side = [((0, 1), (1, 0)), ((1, 0), (1, 1))]
            by_core = [((0, 0), (1, 0))]
        return [send(piece, by_side), send(piece, by_core)]

    late_qkv, late_out, received = None, None, [[], []]
    for l in (1, 0):
        layer_in, hidden, normed_two = kept_rows[l]
        grad_f = grad.astype(f32)
        if l == 0:
            grads_all = gather_rows(grad)
            sent = to_owners(1, after(grads_experts[1][1], grad))
            received[1].append(sent)
            grads_all = after(grads_all, sent[0])
            received[1].append(to_owners(1, after(grads_experts[1][2], sent[0])))
            late_qkv = near_parts(after(late_qkv, grads_all[0]))
            late_out = turn_parts(near_sums(late_out, grads_all[0]))
        backs = [
            experts_backward(
                g, k, weights_gu[l], weights_down[l], first_expert, local, experts
            )
            for g, k in zip(grads_all, kept_experts[l])
        ]
        hidden_b = [b[1] for b in backs]
        summed = sum_cores(*(b[0] for b in backs))
        moved = scatter_rows(summed)
        normed_grad, extra = moved[:, :width], moved[:, width:]
        overlap = extra[:, :experts] + extra[:, experts : 2 * experts]
        chosen_f = (codes_own[l] > 0.5).astype(f32)
        logits = dot(normed_two, routers[l], 1, 0)
        gates_back = jax.vjp(lambda v: gates_of(v, chosen_f), logits)[1]
        logit_b = gates_back(jnp.where(codes_own[l] > 1.5, overlap, 0.0))[0].astype(b16)
        normed_grad = normed_grad + dot(logit_b, routers[l], 1, 1)
        grad_router = dot(logit_b, normed_two, 0, 0)
        hidden_grad, grad_norm_ffn = jax.vjp(norm_rows, hidden, norm_ffn[l])[1](normed_grad)
        hidden_grad = hidden_grad + grad_f
        grads_experts[l] = expert_grads(l, summed, grads_all, hidden_b)
        piece = grads_experts[l][0]
        if l == 0:
            piece = after(piece, received[1][2][0])
        sent = to_owners(l, piece)
        received[l].append(sent)
        branch_b = hidden_grad.astype(b16)
        if l == 1:
            branch_b = after(branch_b, sent[0])
        branch_b = plane_gather(branch_b, pair, half)
        if l == 0:
            late_qkv = turn_parts(near_sums(late_qkv, moved))
            late_out = turn_sums(late_out, moved)
        normed_grad, branch_b, projected_b, gain_grads = attention_backward(
            branch_b, orders, kept_attn[l], weights_in[l], weights_out[l], gains[l], tables
        )
        product_out = weight_product(branch_b, kept_attn[l][6])
        product_qkv = weight_product(kept_attn[l][0], projected_b)
        if l == 1:
            late_out, late_qkv = near_parts(product_out), product_qkv
            units_b = after([k[3] for k in kept_experts[1]], moved)
            parts = [dot(u, weights_down[1], 1, 0).astype(b16) for u in units_b]
            layer_out = hidden + scatter_rows(sum_cores(*parts))
            layer_out = layer_out.astype(b16)
        input_grad, grad_norm_attn = jax.vjp(norm_rows, layer_in.astype(f32), norm_attn[l])[1](
            plane_scatter(normed_grad, pair, half)
        )
        grad = (input_grad + hidden_grad).astype(b16)
        grads_in[l] = grad
        gain_row = jnp.concatenate(
            [g.reshape(n, -1) for g in gain_grads], axis=1
        )
        gain_row = jnp.pad(gain_row, ((0, 0), (0, width // n - gain_row.shape[1])))
        small[l] = jnp.concatenate(
            [grad_router, grad_norm_attn[None], grad_norm_ffn[None], gain_row.reshape(1, -1)],
            axis=0,
        )

    last_out, last_qkv = near_parts(product_out), near_parts(product_qkv)
    last_out = turn_parts(near_sums(last_out))
    last_qkv = turn_parts(near_sums(last_qkv))
    late_qkv = turn_sums(late_qkv, grad)
    late_out = after(late_out, grad)
    grads_out = [pair_columns(turn_sums(last_out), pair), pair_columns(late_out, pair)]
    last_qkv = turn_sums(last_qkv)
    grads_qkv = [pair_columns(last_qkv, pair), pair_columns(late_qkv, pair)]
    for p in grads_experts[0][1:]:
        received[0].append(to_owners(0, after(p, grad, received[0][-1][0])))
    received[1] = after(received[1], grad)

    def of_owner(ks, count):
        return owned(
            core, half, [[(grads_experts[l][k], *received[l][k]) for k in ks] for l in range(2)], count
        )

    grad_gate, grad_up = of_owner((0, 1), 2 * local)
    (grad_down,) = of_owner((2,), 1)
    grad_down = grad_down.reshape(local, units, width)

    def columns(block):
        return block.transpose(0, 2, 1, 3).reshape(width // n, -1)

    qkv = to_owner(grads_qkv[0], grads_qkv[1], core)
    cut = qkv.shape[3] - 2 * head_size
    grad_query = columns(qkv[..., :cut])
    grad_key = columns(qkv[..., cut : cut + head_size])
    grad_value = columns(qkv[..., cut + head_size :])
    grad_output = columns(to_owner(grads_out[0], grads_out[1], core))

    others = core_swap(either(core, small[1], small[0]))
    mine = either(core, small[0], small[1]) + others
    mine = mine.reshape(-1, n, width // n).transpose(1, 0, 2)
    mine = scatter_rows(jnp.take(mine, position(at), axis=0))
    mine = mine + side_swap(mine)
    per = head_size // n

    firsts = jnp.stack([kept_rows[1][0], grads_in[0]])
    seconds = jnp.stack([layer_out, grads_in[1]])
    firsts, seconds = after((firsts, seconds), last_qkv)
    others = core_swap(either(core, seconds, firsts))
    both = ordered(core, either(core, firsts, seconds), others)
    both = ordered(half, both, side_swap(both))
    both = both.transpose(2, 1, 0, 3, 4).reshape(2, 2, tokens, width)
    activations, input_grads = both[0], both[1]
    return (
        activations[None],
        input_grads[None],
        mine[experts][None],
        mine[experts + 1][None],
        mine[experts + 2, :per][None],
        mine[experts + 2, per : 2 * per][None],
        grad_query[None],
        grad_key[None],
        grad_value[None],
        grad_output[None],
        mine[:experts].T[None],
        grad_gate[None],
        grad_up[None],
        grad_down[None],
    )


def solution(mesh):
    by_layer = P(C, None)
    in_specs = (
        P(None, E, None),
        P(None, E, None),
        P(None, E, None),
        P(C, None, E, None),
        by_layer,
        by_layer,
        by_layer,
        by_layer,
        by_layer,
        P(C, E, H),
        P(C, E, H),
        P(C, E, H),
        P(C, E, H),
        P(C, E, None),
        P(C, E, None, H),
        P(C, E, None, H),
        P(C, E, H, None),
    )
    out_specs = (
        P(C, None, E, None),
        P(C, None, E, None),
        P(C, E),
        P(C, E),
        P(C, E),
        P(C, E),
        P(C, E, H),
        P(C, E, H),
        P(C, E, H),
        P(C, E, H),
        P(C, E, None),
        P(C, E, None, H),
        P(C, E, None, H),
        P(C, E, H, None),
    )
    return jax.shard_map(shards, mesh=mesh, in_specs=in_specs, out_specs=out_specs, check_vma=False)
```

```python
import functools

import jax
import jax.numpy as jnp
from jax import lax
from jax.experimental import pallas as pl
from jax.experimental.pallas import tpu as pltpu
from jax.sharding import PartitionSpec as P

C, E, H = "section", "expert", "shard"
f32 = jnp.float32
b16 = jnp.bfloat16

eps = 1e-06
theta = 1000000.0


def core_swap(x):
    return lax.ppermute(x, C, [(0, 1), (1, 0)])


def side_swap(x):
    return lax.ppermute(x, H, [(0, 1), (1, 0)])


def near_swap(x):
    return lax.ppermute(x, E, [(e, e ^ 1) for e in range(lax.axis_size(E))])


def pair_swap(x):
    return lax.ppermute(x, E, [(e, e ^ 2) for e in range(lax.axis_size(E))])


def turn(x, by):
    length = lax.axis_size(E) // 4
    pairs = [(e, (e // 4 + by) % length * 4 + e % 4) for e in range(4 * length)]
    return lax.ppermute(x, E, pairs)


def turns():
    length = lax.axis_size(E) // 4
    return sorted(range(1, length), key=lambda d: (min(d, length - d), d))


def send(x, pairs):
    return lax.ppermute(x, (C, H), [(2 * a + b, 2 * c + d) for (a, b), (c, d) in pairs])


def tie(*refs):
    pass


def after(x, *markers):
    if not markers:
        return x
    leaves, tree = jax.tree.flatten(x)
    here = pl.BlockSpec(memory_space=pl.ANY)
    tied = pl.pallas_call(
        tie,
        out_shape=[jax.ShapeDtypeStruct(a.shape, a.dtype) for a in leaves],
        in_specs=[here] * (len(leaves) + len(markers)),
        out_specs=[here] * len(leaves),
        input_output_aliases={i: i for i in range(len(leaves))},
        cost_estimate=pl.CostEstimate(flops=0, bytes_accessed=0, transcendentals=0),
    )(*leaves, *markers)
    return jax.tree.unflatten(tree, tied)


def pick(x, index, axis=0):
    return lax.dynamic_index_in_dim(x, index, axis, keepdims=False)


def either(flag, first, second):
    return jnp.where(flag == 0, first, second)


def ordered(flag, own, other):
    return jnp.where(flag == 0, jnp.stack([own, other]), jnp.stack([other, own]))


def dot(left, right, at_left, at_right, batch=()):
    return lax.dot_general(
        left, right, (((at_left,), (at_right,)), (batch, batch)), preferred_element_type=f32
    )


def norm_rows(values, weight):
    inverse = lax.rsqrt(jnp.mean(values * values, axis=-1, keepdims=True) + eps)
    return values * inverse * weight


def rotary_tables(length, head_size):
    halfway = head_size // 2
    frequency = theta ** (-jnp.arange(halfway, dtype=f32) * 2.0 / head_size)
    angles = jnp.arange(length, dtype=f32)[:, None] * frequency[None, :]
    cosine, sine = jnp.cos(angles), jnp.sin(angles)
    return (
        jnp.concatenate([cosine, cosine], axis=1),
        jnp.concatenate([-sine, sine], axis=1),
    )


def swiglu(gate_vals, up_vals):
    return gate_vals * jax.nn.sigmoid(gate_vals) * up_vals


def gates_of(logits, chosen):
    largest = jnp.max(logits, axis=-1, keepdims=True)
    raised = jnp.exp(logits - largest)
    picked = raised / jnp.sum(raised, axis=-1, keepdims=True) * chosen
    return picked / jnp.sum(picked, axis=-1, keepdims=True)


def route_codes(chosen, counts, block_rows):
    tokens, experts = chosen.shape[0], counts.shape[0]
    ids = jnp.arange(experts, dtype=jnp.int32)
    member = jnp.any(chosen[:, :, None] == ids[None, None, :], axis=1)
    spots = jnp.arange(tokens)
    earlier = (spots[:, None] > spots[None, :]).astype(b16)
    rank = dot(earlier, member.astype(b16), 1, 0)
    kept = member & (rank < (counts * block_rows).astype(f32)[None, :])
    return member.astype(f32) + kept.astype(f32)


def gather_rows(x, mid=(), end=()):
    length = lax.axis_size(E) // 4
    held = {(0, 0): x}
    for d in turns():
        held[d, 0] = turn(x, d)
    for d in [0] + turns():
        held[d, 1] = pair_swap(held[d, 0])
    keys = sorted(held, key=lambda k: sum(k))
    near = {k: near_swap(held[k]) for k in keys[:-1]}
    near[keys[-1]] = after(near_swap(after(held[keys[-1]], *mid)), *end)
    spots = [(d, p) for d in range(length) for p in range(2)]
    mine = jnp.concatenate([v for k in spots for v in (held[k], near[k])], axis=0)
    return mine, core_swap(mine)


def scatter_rows(pieces, mid=(), last=(), end=()):
    length = lax.axis_size(E) // 4
    pieces = pieces.reshape((length, 2, 2) + pieces.shape[1:])
    far = turns()[::-1] + [0]
    held = {}
    for p in (1, 0):
        for d in far:
            held[d, p] = pieces[d, p, 0].astype(f32)
            held[d, p] += near_swap(pieces[d, p, 1].astype(b16)).astype(f32)
    sent = after([held[d, 1].astype(b16) for d in far], *mid)
    swapped = after([pair_swap(a) for a in sent], *last)
    lined = {d: held[d, 0] + a.astype(f32) for d, a in zip(far, swapped)}
    turned = after([turn(lined[d].astype(b16), -d) for d in far[:-1]], *end)
    total = lined[0]
    for a in turned:
        total = total + a.astype(f32)
    return total


def near_stage(pieces):
    pieces = pieces.reshape((-1, 2, 2) + pieces.shape[1:])
    return pieces[:, :, 0], near_swap(pieces[:, :, 1].astype(b16))


def pair_stage(stage, *markers):
    kept, got = stage
    held = kept.astype(f32) + after(got, *markers).astype(f32)
    return held[:, 0], pair_swap(held[:, 1].astype(b16))


def turn_stage(stage, *markers):
    kept, got = stage
    lined = kept + after(got, *markers).astype(f32)
    return lined[0], [turn(lined[d].astype(b16), -d) for d in range(1, lined.shape[0])]


def last_stage(stage, *markers):
    kept, got = stage
    return kept + sum(g.astype(f32) for g in after(got, *markers))


def sum_cores(own, other):
    summed = own.astype(f32) + core_swap(other).astype(f32)
    return summed.reshape(lax.axis_size(E), -1, own.shape[1])


def position(at):
    length = lax.axis_size(E) // 4
    spots = jnp.arange(4 * length)
    return lax.rem(at // 4 + length - spots // 4, length) * 4 + ((at % 4) ^ (spots % 4))


def plane_pieces(x):
    cut = x.shape[1] // 2
    side, other = side_swap(x), pair_swap(x)
    return x, side, other, pair_swap(side[:, :cut]), side_swap(other[:, cut:])


def plane_whole(pieces, pair, half):
    x, side, other, *across = pieces
    across = jnp.concatenate(across, axis=1)
    own_seq = ordered(half, x, side)
    other_seq = ordered(half, other, across)
    return ordered(pair, own_seq, other_seq).reshape(-1, x.shape[1])


def plane_parts(part, pair, half):
    width = part.shape[1]
    cut = width // 2
    parts = part.reshape(2, 2, -1, width)
    one, two = parts[..., :cut], parts[..., cut:]
    parts = [
        either(pair, one[0], one[1]),
        either(pair, one[1], one[0]),
        either(half, two[:, 0], two[:, 1]),
        either(half, two[:, 1], two[:, 0]),
    ]
    return [p.reshape(-1, cut) for p in parts]


def plane_scatter(parts, pair, half):
    one, one_sent, two, two_sent = parts
    rows = one.shape[0] // 2
    one = one.astype(f32) + pair_swap(one_sent).astype(f32)
    two = two.astype(f32) + side_swap(two_sent).astype(f32)
    one = either(half, one[:rows], one[rows:]) + side_swap(
        either(half, one[rows:], one[:rows]).astype(b16)
    ).astype(f32)
    two = either(pair, two[:rows], two[rows:]) + pair_swap(
        either(pair, two[rows:], two[:rows]).astype(b16)
    ).astype(f32)
    return jnp.concatenate([one, two], axis=1)


def halves_for_cores(packed, core):
    rows = packed.shape[1] // 2
    first, second = packed[:, :rows], packed[:, rows:]
    own, received = either(core, first, second), core_swap(either(core, second, first))
    return either(core, own, received), either(core, received, own)


def pair_rows(half_rows, pair):
    first, second = half_rows[0], half_rows[1]
    return ordered(pair, either(pair, first, second), pair_swap(either(pair, second, first)))


def relative_order(core, at):
    length = lax.axis_size(E) // 4
    spots = jnp.arange(16 * length // 2)
    c, d, y, p = spots // (4 * length), spots // 4 % length, spots // 2 % 2, spots % 2
    line = lax.rem(at // 4 + length - d, length)
    order = ((line * 2 + p) * 2 + (y ^ (at % 2))) * 2 + (c ^ core)
    line, p, y, c = spots // 8, spots // 4 % 2, spots // 2 % 2, spots % 2
    d = lax.rem(at // 4 + length - line, length)
    back = (((c ^ core) * length + d) * 2 + (y ^ (at % 2))) * 2 + p
    return order, back


def move_blocks(order, x, out, back=False):
    wide = x.shape[1] // order.shape[0]
    if wide % 128:
        out[...] = x[...]
        return
    for j in range(order.shape[0]):
        at = pl.multiple_of(order[j] * wide, wide)
        if back:
            out[:, pl.ds(at, wide)] = x[:, j * wide : (j + 1) * wide]
        else:
            out[:, j * wide : (j + 1) * wide] = x[:, pl.ds(at, wide)]


def shuffle_outside(x, order):
    blocks = order.shape[0]
    if x.shape[1] // blocks % 128 == 0:
        return x
    return jnp.take(x.reshape(x.shape[0], blocks, -1), order, axis=1).reshape(x.shape)


def gather_weight(both):
    held = [both] + [turn(both, d) for d in range(1, lax.axis_size(E) // 4)]
    mine = [a for h in held for a in (h, near_swap(h))]
    return [flat(a) for a in mine + [core_swap(m) for m in mine]], held[-1]


def flat(piece):
    return piece.reshape(-1, piece.shape[-1])


def weight_product(left, right):
    n = lax.axis_size(E)
    half = left.shape[1] // 2
    joined = jnp.concatenate([left[:, :half], core_swap(left[:, half:])], axis=0)
    rights = jnp.concatenate([right, core_swap(right)], axis=0)
    product = dot(joined, rights, 0, 0).astype(b16)
    return product.reshape(n // 4, 2, 2, -1, right.shape[1])


def near_parts(pieces):
    return pieces[:, 0], near_swap(pieces[:, 1])


def turn_parts(sums):
    return sums[0], [
        turn(sums[d].astype(b16), -d) for d in range(1, lax.axis_size(E) // 4)
    ]


def near_sums(parts, *markers):
    kept, got = parts
    return kept.astype(f32) + (after(got, *markers) if markers else got).astype(f32)


def turn_sums(parts, *markers):
    kept, got = parts
    return kept + sum(g.astype(f32) for g in (after(got, *markers) if markers else got))


def lay_out(pair, kept, got, query, key, value, output):
    halves, rows, cols = kept.shape
    outs = (query, key, value, output)

    def write(groups):
        for half in range(halves):
            at = slice(half * rows, (half + 1) * rows)
            for g, source in enumerate(groups):
                start = 0
                for out in outs:
                    wide = out.shape[1] // 2
                    out[at, g * wide : (g + 1) * wide] = source[
                        half, :, start : start + wide
                    ].astype(f32)
                    start += wide

    @pl.when(pair[0] == 0)
    def _():
        write((kept, got))

    @pl.when(pair[0] == 1)
    def _():
        write((got, kept))


def to_owner(first, second, core, pair, widths):
    first, second = first.astype(b16), second.astype(b16)
    own, received = either(core, first, second), core_swap(either(core, second, first))
    both = ordered(core, own, received)
    kept = either(pair, both[:, 0], both[:, 1])
    got = pair_swap(either(pair, both[:, 1], both[:, 0]))
    rows = 2 * kept.shape[1]
    outs = [((rows, w), f32) for w in widths]
    return in_vmem(lay_out, outs, [], jnp.stack([pair]).astype(jnp.int32), kept, got)


def head_norm(x):
    inverse = lax.rsqrt(jnp.mean(x * x, axis=-1, keepdims=True) + eps)
    return x * inverse, inverse


def assemble(flags, sources, whole):
    x, side, other, left, right = sources
    rows, cut = left.shape
    pair, half = flags[0], flags[1]

    def at(p, h):
        return pl.ds(pl.multiple_of((p * 2 + h) * rows, rows), rows)

    whole[at(pair, half)] = x[...]
    whole[at(pair, 1 - half)] = side[...]
    whole[at(1 - pair, half)] = other[...]
    whole[at(1 - pair, 1 - half), :cut] = left[...]
    whole[at(1 - pair, 1 - half), cut:] = right[...]


def take_parts(flags, whole, outs):
    one, one_sent, two, two_sent = outs
    rows, cut = one.shape[0] // 2, one.shape[1]
    pair, half = flags[0], flags[1]
    for out, p in ((one, pair), (one_sent, 1 - pair)):
        out[...] = whole[pl.ds(pl.multiple_of(p * 2 * rows, rows), 2 * rows), :cut]
    for out, h in ((two, half), (two_sent, 1 - half)):
        for p in range(2):
            at = pl.ds(pl.multiple_of((p * 2 + h) * rows, rows), rows)
            out[p * rows : (p + 1) * rows] = whole[at, cut:]


def load(flags, order, sources, whole, moved):
    if len(sources) == 1:
        move_blocks(order, sources[0], moved)
        return
    assemble(flags, sources, whole)
    move_blocks(order, whole, moved)


def store(flags, order, mixed, whole, outs):
    if len(outs) == 1:
        move_blocks(order, mixed, outs[0], back=True)
        return
    move_blocks(order, mixed, whole, back=True)
    take_parts(flags, whole, outs)


def attend(counts, starts, flags, order, *refs):
    sources, ins, w_outs, refs = cut_refs(refs, counts[:3])
    w_outs = w_outs or ins
    gains, cosine, sine, allowed, *refs = refs
    outs, refs = refs[: counts[3]], refs[counts[3] :]
    moved, proj, query, key, value, shares, attended, mixed, whole = refs
    rows, head = cosine.shape
    length = allowed.shape[1]
    heads = attended.shape[1] // head
    cols = proj.shape[1]
    load(flags, order, sources, whole, moved)
    depth = ins[0].shape[0]
    total = 0.0
    for i, w in enumerate(ins):
        total = total + dot(moved[:, i * depth : (i + 1) * depth], w[:, :cols], 1, 0)
    proj[...] = total

    def prepared(x, gain):
        turned = head_norm(x)[0] * gain
        return (turned * cosine[...] + pltpu.roll(turned, head // 2, 1) * sine[...]).astype(b16)

    for h in range(heads):
        q = prepared(proj[:, h * head : (h + 1) * head], gains[0:1])
        for s in range(rows // length):
            query[s, h * length : (h + 1) * length] = q[s * length : (s + 1) * length]
    key[...] = prepared(proj[:, heads * head : (heads + 1) * head], gains[1:2])
    value[...] = proj[:, (heads + 1) * head :].astype(b16)
    for s in range(rows // length):
        own = slice(s * length, (s + 1) * length)
        scores = dot(query[s], key[own], 1, 1) * head ** (-0.5)
        scores = scores.reshape(heads, length, length)
        scores = jnp.where((allowed[s] > 0)[None], scores, -1e30)
        raised = jnp.exp(scores - jnp.max(scores, axis=-1, keepdims=True))
        weights = raised / jnp.sum(raised, axis=-1, keepdims=True)
        weights = weights.reshape(heads * length, length)
        shares[s] = weights
        result = dot(weights.astype(b16), value[own], 1, 0).astype(b16)
        for h in range(heads):
            attended[own, h * head : (h + 1) * head] = result[h * length : (h + 1) * length]
    for i, w in enumerate(w_outs):
        at = slice(i * depth, (i + 1) * depth)
        mixed[:, at] = dot(attended[...], w[:, starts:], 1, 1).astype(b16)
    store(flags, order, mixed, whole, outs)


def cut_refs(refs, counts):
    parts = []
    for c in counts:
        parts.append(refs[:c])
        refs = refs[c:]
    return *parts, refs


def attend_back(counts, starts, flags, order, *refs):
    sources, ins, w_outs, refs = cut_refs(refs, counts[:3])
    w_outs = w_outs or ins
    gains, cosine, sine, proj, query, key, value, shares, *refs = refs
    outs, refs = refs[: counts[3]], refs[counts[3] :]
    moved, projected, gain_grads, spread, mixed, whole = refs
    rows, head = cosine.shape
    length = shares.shape[2]
    cols = proj.shape[1]
    heads = cols // head - 2
    scale = head ** (-0.5)
    load(flags, order, sources, whole, moved)
    depth = ins[0].shape[0]
    total = 0.0
    for i, w in enumerate(w_outs):
        total = total + dot(moved[:, i * depth : (i + 1) * depth], w[:, starts:], 1, 0)
    attended = total.astype(b16)
    for h in range(heads):
        for s in range(rows // length):
            spread[s, h * length : (h + 1) * length] = attended[
                s * length : (s + 1) * length, h * head : (h + 1) * head
            ]
    query_grads, key_grads = [], []
    for s in range(rows // length):
        own = slice(s * length, (s + 1) * length)
        weights = shares[s]
        given = spread[s]
        value_grad = dot(weights.astype(b16), given, 0, 0).astype(b16)
        projected[own, (heads + 1) * head :] = value_grad
        share_grad = dot(given, value[own], 1, 1)
        delta = jnp.sum(weights * share_grad, axis=-1, keepdims=True)
        score = (weights * (share_grad - delta)).astype(b16)
        query_grads.append((dot(score, key[own], 1, 0) * scale).astype(b16).astype(f32))
        key_grads.append((dot(score, query[s], 0, 0) * scale).astype(b16).astype(f32))

    def prepared_back(grad, x, gain):
        turned = grad * cosine[...] + pltpu.roll(grad * sine[...], head // 2, 1)
        normed, inverse = head_norm(x)
        scaled = turned * gain
        mean = jnp.mean(scaled * normed, axis=-1, keepdims=True)
        gain_grad = jnp.sum(turned * normed, axis=0, keepdims=True)
        return ((scaled - normed * mean) * inverse).astype(b16), gain_grad

    total = jnp.zeros((1, head), f32)
    for h in range(heads):
        grad = jnp.concatenate([g[h * length : (h + 1) * length] for g in query_grads], axis=0)
        at = slice(h * head, (h + 1) * head)
        projected[:, at], gain_grad = prepared_back(grad, proj[:, at], gains[0:1])
        total = total + gain_grad
    at = slice(heads * head, (heads + 1) * head)
    grad = jnp.concatenate(key_grads, axis=0)
    projected[:, at], gain_grad = prepared_back(grad, proj[:, at], gains[1:2])
    gain_grads[0:1] = total
    gain_grads[1:2] = gain_grad
    for i, w in enumerate(ins):
        at = slice(i * depth, (i + 1) * depth)
        mixed[:, at] = dot(projected[...], w[:, :cols], 1, 1).astype(b16)
    store(flags, order, mixed, whole, outs)


def in_vmem(kernel, outs, scratch, scalars, *args):
    scalars = scalars if isinstance(scalars, tuple) else (scalars,)
    whole = pl.BlockSpec(memory_space=pltpu.VMEM)
    return pl.pallas_call(
        kernel,
        out_shape=[jax.ShapeDtypeStruct(*o) for o in outs],
        in_specs=[pl.BlockSpec(memory_space=pltpu.SMEM)] * len(scalars) + [whole] * len(args),
        out_specs=[whole] * len(outs),
        scratch_shapes=[pltpu.VMEM(*o) for o in scratch],
        compiler_params=pltpu.CompilerParams(vmem_limit_bytes=48 << 20),
        cost_estimate=pl.CostEstimate(flops=0, bytes_accessed=0, transcendentals=0),
    )(*scalars, *args)


def on_plane(kernel, sources, place, weights, start, outs, scratch, *args):
    pair, half, orders = place
    rows, width = 4 * sources[0].shape[0], sources[0].shape[1]
    direct = width // orders[0].shape[0] % 128 != 0
    if len(sources) == 1:
        rows = sources[0].shape[0]
    elif direct:
        sources = [plane_whole(sources, pair, half)]
    if direct:
        sources = [shuffle_outside(sources[0], orders[0])]
    parts = [((rows, width), b16)] if direct else [((rows // 2, width // 2), b16)] * 4
    counts = (len(sources), len(weights[0]), len(weights[1]), len(parts))
    results = in_vmem(
        functools.partial(kernel, counts, start),
        parts + outs,
        scratch + [((rows, width), b16)] * 2,
        (jnp.stack([pair, half]).astype(jnp.int32), orders[0]),
        *sources,
        *weights[0],
        *weights[1],
        *args,
    )
    parts, others = list(results[: len(parts)]), list(results[len(parts) :])
    if direct:
        parts = plane_parts(shuffle_outside(parts[0], orders[1]), pair, half)
    return parts, others


def attention_forward(sources, place, weights, start, sizes, gains, tables, allowed):
    rows, head, length = tables[0].shape[0], gains.shape[1], allowed.shape[1]
    cols, heads_cols = sizes
    stacked = (rows // length, heads_cols // head * length)
    outs = [
        ((rows, sources[0].shape[1]), b16),
        ((rows, cols), f32),
        (stacked + (head,), b16),
        ((rows, head), b16),
        ((rows, head), b16),
        (stacked + (length,), f32),
        ((rows, heads_cols), b16),
    ]
    return on_plane(
        attend, sources, place, weights, start, outs, [], gains, *tables, allowed
    )


def attention_backward(sources, place, saved, weights, start, gains, tables):
    moved, proj, query, key, value, shares, _ = saved
    outs = [(moved.shape, b16), (proj.shape, b16), (gains.shape, f32)]
    return on_plane(
        attend_back,
        sources,
        place,
        weights,
        start,
        outs,
        [(query.shape, b16)],
        gains,
        *tables,
        proj,
        query,
        key,
        value,
        shares,
    )


def spread(gates, local, width):
    per = width // local
    rows = gates.shape[0]
    return jnp.concatenate(
        [jnp.broadcast_to(gates[:, j : j + 1], (rows, per)) for j in range(local)], axis=1
    )


def fetch(which, sizes, refs, target, sem):
    for k, size in enumerate(sizes):
        parts, refs = refs[:size], refs[size:]

        @pl.when(which == k)
        def _():
            start = 0
            for part in parts:
                rows = part.shape[0]
                pltpu.make_async_copy(part, target.at[pl.ds(start, rows)], sem).start()
                start += rows


def fetch_both(which, sizes, refs, targets, sems):
    for k, (size, target) in enumerate(zip(sizes, targets)):
        fetch(which, size, refs, target, sems.at[k])
        refs = refs[sum(size) :]
    for k, target in enumerate(targets):
        pltpu.make_async_copy(target, target, sems.at[k]).wait()


def experts_ahead(
    local, sizes, scalars, rows_own, rows_other, codes_own, codes_other, router, *refs
):
    choices, outs, scratch = refs[: -6 - 3], refs[-6 - 3 : -3], refs[-3:]
    part_own, part_other, rows_all, gates_out, hidden_out, units_out = outs
    weights_gu, weights_down, sems = scratch
    step, half = pl.program_id(0), pl.num_programs(0) // 2

    @pl.when(step == 0)
    def _():
        fetch_both(scalars[0], sizes, choices, (weights_gu, weights_down), sems)

    first = step < half
    rows = jnp.where(first, rows_own[...], rows_other[...])
    codes = jnp.where(first, codes_own[...], codes_other[...])
    rows_all[...] = rows
    gates = gates_of(dot(rows, router[...], 1, 0), (codes > 0.5).astype(f32))
    gates = jnp.where(codes > 1.5, gates, 0.0)
    ids = lax.broadcasted_iota(jnp.int32, gates.shape, 1)
    spots = lax.broadcasted_iota(jnp.int32, gates_out.shape, 1)
    kept = jnp.zeros(gates_out.shape, f32)
    for j in range(local):
        own = jnp.sum(jnp.where(ids == scalars[1] + j, gates, 0.0), axis=1, keepdims=True)
        kept = jnp.where(spots == j, own, kept)
    gates_out[...] = kept
    hidden = dot(rows, weights_gu[...], 1, 0)
    hidden_out[...] = hidden
    cut = hidden.shape[1] // 2
    units = swiglu(hidden[:, :cut], hidden[:, cut:])
    units_b = (units * spread(kept, local, cut)).astype(b16)
    units_out[...] = units_b
    part = dot(units_b, weights_down[...], 1, 0).astype(b16)

    @pl.when(first)
    def _():
        part_own[...] = part

    @pl.when(step >= half)
    def _():
        part_other[...] = part


def experts_back(local, experts, sizes, scalars, grads_own, grads_other, gates, hidden, *refs):
    choices, outs, scratch = refs[: -4 - 3], refs[-4 - 3 : -3], refs[-3:]
    part_own, part_other, grads_all, hidden_out = outs
    weights_gu, weights_down, sems = scratch
    step, half = pl.program_id(0), pl.num_programs(0) // 2

    @pl.when(step == 0)
    def _():
        fetch_both(scalars[0], sizes, choices, (weights_gu, weights_down), sems)

    first = step < half
    grads = jnp.where(first, grads_own[...], grads_other[...])
    grads_all[...] = grads
    raw = dot(grads, weights_down[...], 1, 1)
    cut = raw.shape[1]
    gate, up = hidden[:, :cut], hidden[:, cut:]
    share = jax.nn.sigmoid(gate)
    silu = gate * share
    scaled = raw * spread(gates[...], local, cut)
    gate_grad = (scaled * up * (share + silu * (1.0 - share))).astype(b16)
    up_grad = (scaled * silu).astype(b16)
    hidden_b = jnp.concatenate([gate_grad, up_grad], axis=1)
    hidden_out[...] = hidden_b
    part = dot(hidden_b, weights_gu[...], 1, 1).astype(b16)
    overlap = raw * silu * up
    per = cut // local
    wide = part_own.shape[1] - part.shape[1]
    spots = lax.broadcasted_iota(jnp.int32, (grads.shape[0], wide), 1)
    extra = jnp.zeros(spots.shape, f32)
    for j in range(local):
        value = jnp.sum(overlap[:, j * per : (j + 1) * per], axis=1, keepdims=True)
        high = value.astype(b16).astype(f32)
        extra = jnp.where(spots == scalars[1] + j, high, extra)
        extra = jnp.where(spots == experts + scalars[1] + j, value - high, extra)
    extra = extra.astype(b16)
    width = part.shape[1]

    @pl.when(first)
    def _():
        part_own[:, :width] = part
        part_own[:, width:] = extra

    @pl.when(step >= half)
    def _():
        part_other[:, :width] = part
        part_other[:, width:] = extra


def by_rows(kernel, which, first_expert, halved, whole, fixed, choices, outs_halved, outs):
    rows = halved[0][0].shape[0]
    block = 256
    count = rows // block
    weights = [choice[0][0].shape for choice in choices]

    def spec(a, index):
        return pl.BlockSpec((block, a.shape[1]), index)

    def own(i, *_):
        return jnp.minimum(i, count - 1), 0

    def other(i, *_):
        return jnp.maximum(i - count, 0), 0

    def each(i, *_):
        return i, 0

    in_specs = []
    for first, second in halved:
        in_specs += [spec(first, own), spec(second, other)]
    in_specs += [spec(a, each) for a in whole]
    in_specs += [pl.BlockSpec(a.shape, lambda i, *_: (0, 0)) for a in fixed]
    sizes = [[len(parts) for parts in choice] for choice in choices]
    choices = [a for choice in choices for parts in choice for a in parts]
    in_specs += [pl.BlockSpec(memory_space=pl.ANY)] * len(choices)
    shapes = [jax.ShapeDtypeStruct((rows, w), b16) for w in (outs_halved, outs_halved)]
    shapes += [jax.ShapeDtypeStruct((2 * rows, w), t) for w, t in outs]
    out_specs = [spec(shapes[0], own), spec(shapes[1], other)]
    out_specs += [spec(a, each) for a in shapes[2:]]
    weights = [pltpu.VMEM(a, b16) for a in weights]
    return pl.pallas_call(
        functools.partial(kernel, sizes),
        grid_spec=pltpu.PrefetchScalarGridSpec(
            num_scalar_prefetch=1,
            grid=(2 * count,),
            in_specs=in_specs,
            out_specs=out_specs,
            scratch_shapes=weights + [pltpu.SemaphoreType.DMA((2,))],
        ),
        out_shape=shapes,
        compiler_params=pltpu.CompilerParams(vmem_limit_bytes=48 << 20),
        cost_estimate=pl.CostEstimate(flops=0, bytes_accessed=0, transcendentals=0),
    )(
        jnp.stack([which, first_expert]).astype(jnp.int32),
        *[a for pair in halved for a in pair],
        *whole,
        *fixed,
        *choices,
    )


def experts_forward(rows, codes, router, which, choices, first_expert, local):
    width = rows[0].shape[1]
    hidden = choices[0][0][0].shape[1]
    outs = [(width, b16), (128, f32), (hidden, f32), (hidden // 2, b16)]
    part_own, part_other, *saved = by_rows(
        functools.partial(experts_ahead, local),
        which,
        first_expert,
        [rows, codes],
        [],
        [router],
        choices,
        width,
        outs,
    )
    return (part_own, part_other), saved


def experts_backward(grads, saved, which, choices, first_expert, local, experts):
    _, gates, hidden, _ = saved
    width = grads[0].shape[1]
    wide = -(-2 * experts // 128) * 128
    outs = [(width, b16), (hidden.shape[1], b16)]
    part_own, part_other, *others = by_rows(
        functools.partial(experts_back, local, experts),
        which,
        first_expert,
        [grads],
        [gates, hidden],
        [],
        choices,
        width + wide,
        outs,
    )
    return (part_own, part_other), others


def own_sums(steps, flags, *refs):
    parts = len(steps)
    ins, outs = refs[: 6 * parts], refs[6 * parts :]

    def write(own, side, core):
        total = side[...].astype(f32) + core[...].astype(f32)
        total = total + jnp.where(flags[0] == flags[1], own[...].astype(f32), 0.0)
        if len(outs) == 1:
            outs[0][...] = total
            return
        per = outs[0].shape[2]
        for i, out in enumerate(outs):
            for j in range(out.shape[0]):
                at = (i * out.shape[0] + j) * per
                out[j] = total[:, at : at + per]

    at = pl.program_id(0)
    for l in range(2):
        for k, (first, last) in enumerate(steps):

            @pl.when((flags[0] == l) & (at >= first) & (at < last))
            def _():
                base = 3 * (l * parts + k)
                write(*ins[base : base + 3])


def owned(core, half, by_layer, pieces):
    step = 256
    steps, specs, rows = [], [], 0
    for own, _, _ in by_layer[0]:
        steps.append((rows // step, (rows + own.shape[0]) // step))
        rows += own.shape[0]
    cols = by_layer[0][0][0].shape[1]
    for l in range(2):
        for first, last in steps:

            def where(i, f, l=l, first=first, last=last):
                inside = jnp.clip(i - first, 0, last - first - 1)
                return jnp.where(f[0] == l, inside, 0), 0

            specs += [pl.BlockSpec((step, cols), where)] * 3
    if pieces == 1:
        outs = [jax.ShapeDtypeStruct((rows, cols), f32)]
        out_specs = [pl.BlockSpec((step, cols), lambda i, f: (i, 0))]
    else:
        shape = (pieces // 2, rows, cols // pieces)
        outs = [jax.ShapeDtypeStruct(shape, f32)] * 2
        block = (pieces // 2, step, cols // pieces)
        out_specs = [pl.BlockSpec(block, lambda i, f: (0, i, 0))] * 2
    terms = [t for layer in by_layer for part in layer for t in part]
    return pl.pallas_call(
        functools.partial(own_sums, steps),
        grid_spec=pltpu.PrefetchScalarGridSpec(
            num_scalar_prefetch=1, grid=(rows // step,), in_specs=specs, out_specs=out_specs
        ),
        out_shape=outs,
        compiler_params=pltpu.CompilerParams(vmem_limit_bytes=48 << 20),
        cost_estimate=pl.CostEstimate(flops=0, bytes_accessed=0, transcendentals=0),
    )(jnp.stack([core, half]).astype(jnp.int32), *terms)


def shards(
    inputs,
    cotangent,
    segments,
    routes,
    counts,
    norm_attn,
    norm_ffn,
    q_gain,
    k_gain,
    w_query,
    w_key,
    w_value,
    w_output,
    w_router,
    w_gate,
    w_up,
    w_down,
):
    core, at, half = lax.axis_index(C), lax.axis_index(E), lax.axis_index(H)
    pair = lax.rem(at // 2, 2)
    n = lax.axis_size(E)
    _, tokens, width = inputs.shape
    rows = tokens // 2
    experts = counts.shape[1]
    local = w_gate.shape[1]
    units = w_gate.shape[3]
    first_expert = at * local
    head_size = q_gain.shape[1]
    place = pair, half, relative_order(core, at)

    def by_group(weight):
        return weight[0].reshape(weight.shape[1], 2, -1).transpose(1, 0, 2)

    packed = jnp.concatenate([by_group(w) for w in (w_query, w_key, w_value, w_output)], axis=2)
    halves = halves_for_cores(packed, core)
    heads_cols = w_output.shape[2] // 2
    cut = packed.shape[2] - heads_cols
    sizes = cut, heads_cols
    weights, starts = [None, None], (0, 0)
    first = [pair_rows(h, pair) for h in (halves[0][..., :cut], halves[0][..., cut:])]
    (weights_in, _), (weights_out, arrived) = (gather_weight(h) for h in first)
    weights[0] = weights_in, weights_out
    second_pair = pair_rows(after(halves[1], arrived), pair)
    second_near = near_swap(second_pair)

    def both_layers(own):
        return ordered(core, own, after(core_swap(own), first[0]))

    norm_attn, norm_ffn, q_gain, k_gain = (
        both_layers(a[0]) for a in (norm_attn, norm_ffn, q_gain, k_gain)
    )
    counts = both_layers(counts[0])
    chosen = after(core_swap(pick(routes[0], 1 - core)), first[0])
    chosen = ordered(core, pick(routes[0], core), chosen)
    block_rows = tokens * chosen.shape[2] // (4 * experts)
    codes = [route_codes(chosen[l], counts[l], block_rows) for l in range(2)]
    codes = jnp.concatenate(codes, axis=1)
    codes_own = lax.dynamic_slice_in_dim(codes, half * rows, rows, 0)
    wide = -(-2 * experts // 128) * 128
    codes_sent = jnp.pad(codes_own.astype(b16), ((0, 0), (0, wide - 2 * experts)))
    router_sent = w_router[0].reshape(-1, wide)
    tables_sent = jnp.concatenate([codes_sent, router_sent], axis=0)
    tables_all = [t.reshape(n, -1, wide) for t in gather_rows(after(tables_sent, first[0]))]
    codes_all = [t[:, :rows].reshape(-1, wide).astype(f32) for t in tables_all]
    routers = [jnp.take(t[:, rows:], position(at), axis=0) for t in tables_all]
    routers = ordered(core, *routers).reshape(2, width, experts)
    codes_own = [codes_own[:, l * experts : (l + 1) * experts] for l in range(2)]
    codes_all = [[c[:, l * experts : (l + 1) * experts] for c in codes_all] for l in range(2)]

    seg_own = pick(segments, core)[0]
    seg_ids = ordered(pair, seg_own, after(pair_swap(seg_own), first[0]))
    spots = jnp.arange(tokens)
    allowed = (spots[:, None] >= spots[None, :])[None] & (
        seg_ids[:, :, None] == seg_ids[:, None, :]
    )
    allowed = allowed.astype(f32)
    tables = [jnp.concatenate([t, t], axis=0) for t in rotary_tables(tokens, head_size)]

    at_first = (core == 0) & (half == 0)
    at_last = (core == 1) & (half == 1)
    own_gu = jnp.concatenate([w[0, j] for w in (w_gate, w_up) for j in range(local)], axis=1)
    own_down = w_down[0].reshape(-1, width)
    which = [
        jnp.where(keeps, 0, jnp.where(takes, 2, 1))
        for keeps, takes in ((at_first, at_last), (at_last, at_first))
    ]

    def experts_sent(layer, cuts, *marker):
        if layer == 0:
            by_side = [((0, 0), (0, 1)), ((0, 1), (1, 0))]
            by_core = [((0, 1), (1, 1))]
        else:
            by_side = [((1, 0), (0, 1)), ((1, 1), (1, 0))]
            by_core = [((1, 0), (0, 0))]
        sent = []
        for w, count in zip((own_gu, own_down), cuts):
            step = w.shape[0] // count
            parts = [w[i * step : (i + 1) * step] if count > 1 else w for i in range(count)]
            parts = [send(p, by_side) for p in after(parts, *marker)]
            sent.append(([w], parts, [send(w, by_core)]))
        return sent

    choices = [experts_sent(0, (1, 1)), None]

    layer_in = lax.dynamic_slice_in_dim(pick(inputs, core), half * rows, rows, 0)
    whole_in = pick(inputs, core)
    others_in = after(pair_swap(whole_in), first[0])
    whole_in = ordered(pair, whole_in, others_in).reshape(-1, width)
    sources = [norm_rows(whole_in.astype(f32), norm_attn[0]).astype(b16)]
    sources = after(sources, *choices[0][0][1], *choices[0][1][1], second_pair)
    gains = jnp.stack([q_gain, k_gain], axis=1)
    kept_attn, kept_rows, kept_experts = [], [], []
    for l in range(2):
        if l == 1:
            mine = norm_rows(layer_in.astype(f32), norm_attn[1]).astype(b16)
            sources = plane_pieces(mine)
            grad = lax.dynamic_slice_in_dim(pick(cotangent, core), half * rows, rows, 0)
            grads_all = gather_rows(after(grad, layer_in), sources[1:3])
        parts, saved = attention_forward(
            sources, place, weights[l], starts[l], sizes, gains[l], tables, allowed
        )
        if l == 0:
            parts[0] = after(parts[0], *codes_all[0], *codes_all[1], routers)
        hidden = layer_in.astype(f32) + plane_scatter(parts, pair, half)
        normed_two = norm_rows(hidden, norm_ffn[l]).astype(b16)
        if l == 0:
            normed_two = after(normed_two, second_near)
            choices[1] = experts_sent(1, (2, 2), normed_two)
            gu_parts, down_parts = choices[1][0][1], choices[1][1][1]
            rows_all = gather_rows(normed_two, (), gu_parts[:1])
        else:
            normed_two = after(normed_two, *grads_all)
            rows_all = gather_rows(normed_two, (), down_parts[1:])
        parts, saved_experts = experts_forward(
            rows_all, codes_all[l], routers[l], which[l], choices[l], first_expert, local
        )
        kept_experts.append(saved_experts)
        kept_attn.append(saved)
        kept_rows.append((layer_in, hidden, normed_two))
        if l == 0:
            pieces = after([second_pair[..., :cut], second_pair[..., cut:]], rows_all[0])
            far = [[turn(p, d) for d in range(1, n // 4)] for p in pieces]
            parts = after(parts, *far[0])
            summed = sum_cores(*parts)
            near = [near_swap(p) for p in after(far[0], summed)]
            near = [near, [near_swap(p) for p in after(far[1], *near)]]
            moved = scatter_rows(
                summed, [*far[1], gu_parts[1]], near[0], near[1] + down_parts[:1]
            )
            layer_in = (hidden + moved).astype(b16)
            weights[1] = []
            for k, (a, b) in enumerate(((0, cut), (cut, packed.shape[2]))):
                mine = [second_pair[..., a:b], second_near[..., a:b]]
                for p in zip(far[k], near[k]):
                    mine += p
                mine = [flat(p) for p in mine]
                weights[1].append(mine + [core_swap(p) for p in mine])
    last_parts, last_rows = parts, None

    grads_in, small, grads_experts = ([None] * 2 for _ in range(3))

    def expert_grads(l, marker, grads_all, hidden_b):
        rows_all, _, _, units_b = kept_experts[l]
        units_b, hidden_b = after((units_b, hidden_b), marker)
        cuts = [slice(0, width // 2), slice(width // 2, width)]
        return [dot(rows_all[:, c], hidden_b, 0, 0).astype(b16) for c in cuts] + [
            dot(units_b, grads_all, 0, 0).astype(b16)
        ]

    def to_owners(l, piece):
        if l == 0:
            by_side = [((0, 1), (0, 0)), ((1, 0), (0, 1))]
            by_core = [((1, 1), (0, 1))]
        else:
            by_side = [((0, 1), (1, 0)), ((1, 0), (1, 1))]
            by_core = [((0, 0), (1, 0))]
        return [send(piece, by_side), send(piece, by_core)]

    def both_batches(first, second):
        others = core_swap(either(core, second, first))
        both = ordered(core, either(core, first, second), others)
        swapped = side_swap(both)
        both = ordered(half, both, swapped).transpose(1, 0, 2, 3)
        return both.reshape(2, tokens, width), swapped

    late_qkv, late_out, received = None, None, [[], []]
    for l in (1, 0):
        layer_in, hidden, normed_two = kept_rows[l]
        grad_f = grad.astype(f32)
        if l == 0:
            sent = to_owners(1, after(grads_experts[1][1], grad))
            received[1].append(sent)
            grads_all = gather_rows(grad, (), sent[:1])
            received[1].append(to_owners(1, after(grads_experts[1][2], sent[0])))
        parts, (grads_joined, hidden_b) = experts_backward(
            grads_all, kept_experts[l], which[l], choices[l], first_expert, local, experts
        )
        mid, end = [], []
        if l == 0:
            last_rows = turn_stage(last_rows, grads_all[0])
            late_out = near_parts(late_out)
            parts = after(parts, late_out[1], *last_rows[1])
        summed = sum_cores(*parts)
        grads_experts[l] = expert_grads(l, summed, grads_joined, hidden_b)
        piece = grads_experts[l][0]
        if l == 0:
            piece = after(piece, received[1][2][0])
        sent = to_owners(l, piece)
        received[l].append(sent)
        if l == 0:
            late_out = turn_parts(near_sums((after(late_out[0], summed), late_out[1])))
            late_qkv = near_parts(after(late_qkv, summed))
            mid, end = late_out[1], late_qkv[1:]
        moved = scatter_rows(
            summed, grads_experts[l][:2] + mid, grads_experts[l][2:], sent[:1] + list(end)
        )
        if l == 1:
            last_rows = near_stage(sum_cores(*after(last_parts, moved)))
        normed_grad, extra = moved[:, :width], moved[:, width:]
        overlap = extra[:, :experts] + extra[:, experts : 2 * experts]
        chosen_f = (codes_own[l] > 0.5).astype(f32)
        logits = dot(normed_two, routers[l], 1, 0)
        gates_back = jax.vjp(lambda v: gates_of(v, chosen_f), logits)[1]
        logit_b = gates_back(jnp.where(codes_own[l] > 1.5, overlap, 0.0))[0].astype(b16)
        normed_grad = normed_grad + dot(logit_b, routers[l], 1, 1)
        grad_router = dot(logit_b, normed_two, 0, 0)
        hidden_grad, grad_norm_ffn = jax.vjp(norm_rows, hidden, norm_ffn[l])[1](normed_grad)
        hidden_grad = hidden_grad + grad_f
        branch_b = hidden_grad.astype(b16)
        if l == 0:
            layer_out = kept_rows[1][1] + last_stage(last_rows, moved)
            layer_out = layer_out.astype(b16)
        parts, (branch_b, projected_b, gain_grads) = attention_backward(
            plane_pieces(branch_b), place, kept_attn[l], weights[l], starts[l], gains[l], tables
        )
        product_out = weight_product(branch_b, kept_attn[l][6])
        product_qkv = weight_product(kept_attn[l][0], projected_b)
        if l == 1:
            late_out, late_qkv = product_out, product_qkv
            last_rows = pair_stage(last_rows, projected_b)
        else:
            parts[0] = after(parts[0], product_out, product_qkv)
            late_qkv = turn_parts(near_sums(late_qkv, moved))
            parts[0] = after(parts[0], *late_qkv[1])
            last_out, last_qkv = near_parts(product_out), near_parts(product_qkv)
        input_grad, grad_norm_attn = jax.vjp(norm_rows, layer_in.astype(f32), norm_attn[l])[1](
            plane_scatter(parts, pair, half)
        )
        grad = (input_grad + hidden_grad).astype(b16)
        if l == 0:
            grad = after(grad, last_out[1])
        grads_in[l] = grad
        gain_row = jnp.concatenate([g.reshape(n, -1) for g in gain_grads], axis=1)
        gain_row = jnp.pad(gain_row, ((0, 0), (0, width // n - gain_row.shape[1])))
        small[l] = jnp.concatenate(
            [grad_router, grad_norm_attn[None], grad_norm_ffn[None], gain_row.reshape(1, -1)],
            axis=0,
        )

    input_grads, marker = both_batches(grads_in[0], grads_in[1])
    last_out = turn_parts(near_sums(last_out))
    last_qkv = turn_parts(near_sums(last_qkv))
    for p in grads_experts[0][1:]:
        received[0].append(to_owners(0, after(p, marker, received[0][-1][0])))
    received[1] = after(received[1], grad)
    activations, _ = both_batches(kept_rows[1][0], after(layer_out, received[0][2][0]))

    others = core_swap(either(core, small[1], small[0]))
    mine = either(core, small[0], small[1]) + others
    count = mine.shape[0]
    mine = mine.reshape(count, n, width // n).transpose(1, 0, 2)
    mine = jnp.take(mine, position(at), axis=0)
    mine = turn_stage(pair_stage(near_stage(mine)))
    mine = last_stage(mine, received[0][1][0])
    mine = mine + side_swap(mine)
    per = head_size // n

    weight_grads = [
        jnp.concatenate([turn_sums(a), b], axis=2)
        for a, b in ((last_qkv, turn_sums(last_out)), (late_qkv, turn_sums(late_out)))
    ]
    widths = [w.shape[2] for w in (w_query, w_key, w_value, w_output)]
    weight_grads = to_owner(*weight_grads, core, pair, widths)

    def of_owner(ks, count):
        return owned(
            core, half, [[(grads_experts[l][k], *received[l][k]) for k in ks] for l in range(2)], count
        )

    grad_gate, grad_up = of_owner((0, 1), 2 * local)
    (grad_down,) = of_owner((2,), 1)
    grad_down = grad_down.reshape(local, units, width)
    return (
        activations[None],
        input_grads[None],
        mine[experts][None],
        mine[experts + 1][None],
        mine[experts + 2, :per][None],
        mine[experts + 2, per : 2 * per][None],
        *[w[None] for w in weight_grads],
        mine[:experts].T[None],
        grad_gate[None],
        grad_up[None],
        grad_down[None],
    )


def solution(mesh):
    by_layer = P(C, None)
    in_specs = (
        P(None, E, None),
        P(None, E, None),
        P(None, E, None),
        P(C, None, E, None),
        by_layer,
        by_layer,
        by_layer,
        by_layer,
        by_layer,
        P(C, E, H),
        P(C, E, H),
        P(C, E, H),
        P(C, E, H),
        P(C, E, None),
        P(C, E, None, H),
        P(C, E, None, H),
        P(C, E, H, None),
    )
    out_specs = (
        P(C, None, E, None),
        P(C, None, E, None),
        P(C, E),
        P(C, E),
        P(C, E),
        P(C, E),
        P(C, E, H),
        P(C, E, H),
        P(C, E, H),
        P(C, E, H),
        P(C, E, None),
        P(C, E, None, H),
        P(C, E, None, H),
        P(C, E, H, None),
    )
    return jax.shard_map(shards, mesh=mesh, in_specs=in_specs, out_specs=out_specs, check_vma=False)
```

```python
import functools

import jax
import jax.numpy as jnp
from jax import lax
from jax.experimental import pallas as pl
from jax.experimental.pallas import tpu as pltpu
from jax.sharding import PartitionSpec as P

C, E, H = "section", "expert", "shard"
f32 = jnp.float32
b16 = jnp.bfloat16

eps = 1e-06
theta = 1000000.0


def core_swap(x):
    return lax.ppermute(x, C, [(0, 1), (1, 0)])


def side_swap(x):
    return lax.ppermute(x, H, [(0, 1), (1, 0)])


def near_swap(x):
    return lax.ppermute(x, E, [(e, e ^ 1) for e in range(lax.axis_size(E))])


def pair_swap(x):
    return lax.ppermute(x, E, [(e, e ^ 2) for e in range(lax.axis_size(E))])


def turn(x, by):
    length = lax.axis_size(E) // 4
    pairs = [(e, (e // 4 + by) % length * 4 + e % 4) for e in range(4 * length)]
    return lax.ppermute(x, E, pairs)


def turns():
    length = lax.axis_size(E) // 4
    return sorted(range(1, length), key=lambda d: (min(d, length - d), d))


def send(x, pairs):
    return lax.ppermute(x, (C, H), [(2 * a + b, 2 * c + d) for (a, b), (c, d) in pairs])


def tie(*refs):
    pass


def after(x, *markers):
    if not markers:
        return x
    leaves, tree = jax.tree.flatten(x)
    here = pl.BlockSpec(memory_space=pl.ANY)
    tied = pl.pallas_call(
        tie,
        out_shape=[jax.ShapeDtypeStruct(a.shape, a.dtype) for a in leaves],
        in_specs=[here] * (len(leaves) + len(markers)),
        out_specs=[here] * len(leaves),
        input_output_aliases={i: i for i in range(len(leaves))},
        cost_estimate=pl.CostEstimate(flops=0, bytes_accessed=0, transcendentals=0),
    )(*leaves, *markers)
    return jax.tree.unflatten(tree, tied)


def pick(x, index, axis=0):
    return lax.dynamic_index_in_dim(x, index, axis, keepdims=False)


def either(flag, first, second):
    return jnp.where(flag == 0, first, second)


def ordered(flag, own, other):
    return jnp.where(flag == 0, jnp.stack([own, other]), jnp.stack([other, own]))


def dot(left, right, at_left, at_right, batch=()):
    return lax.dot_general(
        left, right, (((at_left,), (at_right,)), (batch, batch)), preferred_element_type=f32
    )


def norm_rows(values, weight):
    inverse = lax.rsqrt(jnp.mean(values * values, axis=-1, keepdims=True) + eps)
    return values * inverse * weight


def rotary_tables(length, head_size):
    halfway = head_size // 2
    frequency = theta ** (-jnp.arange(halfway, dtype=f32) * 2.0 / head_size)
    angles = jnp.arange(length, dtype=f32)[:, None] * frequency[None, :]
    cosine, sine = jnp.cos(angles), jnp.sin(angles)
    return (
        jnp.concatenate([cosine, cosine], axis=1),
        jnp.concatenate([-sine, sine], axis=1),
    )


def swiglu(gate_vals, up_vals):
    return gate_vals * jax.nn.sigmoid(gate_vals) * up_vals


def gates_of(logits, chosen):
    largest = jnp.max(logits, axis=-1, keepdims=True)
    raised = jnp.exp(logits - largest)
    picked = raised / jnp.sum(raised, axis=-1, keepdims=True) * chosen
    return picked / jnp.sum(picked, axis=-1, keepdims=True)


def route_codes(chosen, counts, block_rows):
    tokens, experts = chosen.shape[0], counts.shape[0]
    ids = jnp.arange(experts, dtype=jnp.int32)
    member = jnp.any(chosen[:, :, None] == ids[None, None, :], axis=1)
    spots = jnp.arange(tokens)
    earlier = (spots[:, None] > spots[None, :]).astype(b16)
    rank = dot(earlier, member.astype(b16), 1, 0)
    kept = member & (rank < (counts * block_rows).astype(f32)[None, :])
    return member.astype(f32) + kept.astype(f32)


def gather_rows(x, mid=(), end=()):
    length = lax.axis_size(E) // 4
    held = {(0, 0): x}
    for d in turns():
        held[d, 0] = turn(x, d)
    for d in [0] + turns():
        held[d, 1] = pair_swap(held[d, 0])
    keys = sorted(held, key=lambda k: sum(k))
    near = {k: near_swap(held[k]) for k in keys[:-1]}
    near[keys[-1]] = after(near_swap(after(held[keys[-1]], *mid)), *end)
    spots = [(d, p) for d in range(length) for p in range(2)]
    mine = jnp.concatenate([v for k in spots for v in (held[k], near[k])], axis=0)
    return mine, core_swap(mine)


def scatter_rows(pieces, mid=(), last=(), end=()):
    length = lax.axis_size(E) // 4
    pieces = pieces.reshape((length, 2, 2) + pieces.shape[1:])
    far = turns()[::-1] + [0]
    held = {}
    for p in (1, 0):
        for d in far:
            held[d, p] = pieces[d, p, 0].astype(f32)
            held[d, p] += near_swap(pieces[d, p, 1].astype(b16)).astype(f32)
    sent = after([held[d, 1].astype(b16) for d in far], *mid)
    swapped = after([pair_swap(a) for a in sent], *last)
    lined = {d: held[d, 0] + a.astype(f32) for d, a in zip(far, swapped)}
    turned = after([turn(lined[d].astype(b16), -d) for d in far[:-1]], *end)
    total = lined[0]
    for a in turned:
        total = total + a.astype(f32)
    return total


def near_pieces(pieces):
    pieces = pieces.reshape((-1, 2, 2) + pieces.shape[1:])
    return pieces[:, :, 0], pieces[:, :, 1].astype(b16)


def near_stage(pieces):
    kept, sent = near_pieces(pieces)
    return kept, near_swap(sent)


def pair_stage(stage, *markers):
    kept, got = stage
    held = kept.astype(f32) + after(got, *markers).astype(f32)
    return held[:, 0], pair_swap(held[:, 1].astype(b16))


def turn_stage(stage, *markers):
    kept, got = stage
    lined = kept + after(got, *markers).astype(f32)
    return lined[0], [turn(lined[d].astype(b16), -d) for d in range(1, lined.shape[0])]


def last_stage(stage, *markers):
    kept, got = stage
    return kept + sum(g.astype(f32) for g in after(got, *markers))


def sum_cores(own, other):
    summed = own.astype(f32) + core_swap(other).astype(f32)
    return summed.reshape(lax.axis_size(E), -1, own.shape[1])


def position(at):
    length = lax.axis_size(E) // 4
    spots = jnp.arange(4 * length)
    return lax.rem(at // 4 + length - spots // 4, length) * 4 + ((at % 4) ^ (spots % 4))


def plane_pieces(x):
    cut = x.shape[1] // 2
    side, other = side_swap(x), pair_swap(x)
    return x, side, other, pair_swap(side[:, :cut]), side_swap(other[:, cut:])


def plane_whole(pieces, pair, half):
    x, side, other, *across = pieces
    across = jnp.concatenate(across, axis=1)
    own_seq = ordered(half, x, side)
    other_seq = ordered(half, other, across)
    return ordered(pair, own_seq, other_seq).reshape(-1, x.shape[1])


def plane_parts(part, pair, half):
    width = part.shape[1]
    cut = width // 2
    parts = part.reshape(2, 2, -1, width)
    one, two = parts[..., :cut], parts[..., cut:]
    parts = [
        either(pair, one[0], one[1]),
        either(pair, one[1], one[0]),
        either(half, two[:, 0], two[:, 1]),
        either(half, two[:, 1], two[:, 0]),
    ]
    return [p.reshape(-1, cut) for p in parts]


def plane_scatter(parts, pair, half):
    one, one_sent, two, two_sent = parts
    rows = one.shape[0] // 2
    one = one.astype(f32) + pair_swap(one_sent).astype(f32)
    two = two.astype(f32) + side_swap(two_sent).astype(f32)
    one = either(half, one[:rows], one[rows:]) + side_swap(
        either(half, one[rows:], one[:rows]).astype(b16)
    ).astype(f32)
    two = either(pair, two[:rows], two[rows:]) + pair_swap(
        either(pair, two[rows:], two[:rows]).astype(b16)
    ).astype(f32)
    return jnp.concatenate([one, two], axis=1)


def halves_for_cores(packed, core):
    rows = packed.shape[1] // 2
    first, second = packed[:, :rows], packed[:, rows:]
    own, received = either(core, first, second), core_swap(either(core, second, first))
    return either(core, own, received), either(core, received, own)


def pair_rows(half_rows, pair):
    first, second = half_rows[0], half_rows[1]
    return ordered(pair, either(pair, first, second), pair_swap(either(pair, second, first)))


def relative_order(core, at):
    length = lax.axis_size(E) // 4
    spots = jnp.arange(16 * length // 2)
    c, d, y, p = spots // (4 * length), spots // 4 % length, spots // 2 % 2, spots % 2
    line = lax.rem(at // 4 + length - d, length)
    order = ((line * 2 + p) * 2 + (y ^ (at % 2))) * 2 + (c ^ core)
    line, p, y, c = spots // 8, spots // 4 % 2, spots // 2 % 2, spots % 2
    d = lax.rem(at // 4 + length - line, length)
    back = (((c ^ core) * length + d) * 2 + (y ^ (at % 2))) * 2 + p
    return order, back


def move_blocks(order, x, out, back=False):
    wide = x.shape[1] // order.shape[0]
    if wide % 128:
        out[...] = x[...]
        return
    for j in range(order.shape[0]):
        at = pl.multiple_of(order[j] * wide, wide)
        if back:
            out[:, pl.ds(at, wide)] = x[:, j * wide : (j + 1) * wide]
        else:
            out[:, j * wide : (j + 1) * wide] = x[:, pl.ds(at, wide)]


def shuffle_outside(x, order):
    blocks = order.shape[0]
    if x.shape[1] // blocks % 128 == 0:
        return x
    return jnp.take(x.reshape(x.shape[0], blocks, -1), order, axis=1).reshape(x.shape)


def gather_weight(both):
    held = [both] + [turn(both, d) for d in range(1, lax.axis_size(E) // 4)]
    mine = [a for h in held for a in (h, near_swap(h))]
    return [flat(a) for a in mine + [core_swap(m) for m in mine]], held[-1]


def flat(piece):
    return piece.reshape(-1, piece.shape[-1])


def weight_product(left, right):
    n = lax.axis_size(E)
    half = left.shape[1] // 2
    joined = jnp.concatenate([left[:, :half], core_swap(left[:, half:])], axis=0)
    rights = jnp.concatenate([right, core_swap(right)], axis=0)
    product = dot(joined, rights, 0, 0).astype(b16)
    return product.reshape(n // 4, 2, 2, -1, right.shape[1])


def near_parts(pieces):
    return pieces[:, 0], near_swap(pieces[:, 1])


def turn_parts(sums):
    return sums[0], [
        turn(sums[d].astype(b16), -d) for d in range(1, lax.axis_size(E) // 4)
    ]


def near_sums(parts, *markers):
    kept, got = parts
    return kept.astype(f32) + (after(got, *markers) if markers else got).astype(f32)


def turn_sums(parts, *markers):
    kept, got = parts
    return kept + sum(g.astype(f32) for g in (after(got, *markers) if markers else got))


def lay_out(flags, own, received, query, key, value, output):
    _, rows, _ = own.shape
    outs = (query, key, value, output)

    def write(core, pair):
        for source, half in ((own, core), (received, 1 - core)):
            at = slice(half * rows, (half + 1) * rows)
            for k, g in ((0, pair), (1, 1 - pair)):
                start = 0
                for out in outs:
                    wide = out.shape[1] // 2
                    columns = slice(g * wide, (g + 1) * wide)
                    out[at, columns] = source[k, :, start : start + wide].astype(f32)
                    start += wide

    for core in range(2):
        for pair in range(2):

            @pl.when((flags[0] == core) & (flags[1] == pair))
            def _():
                write(core, pair)


def pair_columns(total, pair):
    kept = either(pair, total[0], total[1]).astype(b16)
    return jnp.stack([kept, pair_swap(either(pair, total[1], total[0]).astype(b16))])


def to_owner(first, second, core, widths, pair):
    own, received = either(core, first, second), core_swap(either(core, second, first))
    outs = [((2 * own.shape[1], w), f32) for w in widths]
    flags = jnp.stack([core, pair]).astype(jnp.int32)
    return in_vmem(lay_out, outs, [], flags, own, received)


def head_norm(x):
    inverse = lax.rsqrt(jnp.mean(x * x, axis=-1, keepdims=True) + eps)
    return x * inverse, inverse


def assemble(flags, sources, whole):
    x, side, other, left, right = sources
    rows, cut = left.shape
    pair, half = flags[0], flags[1]

    def at(p, h):
        return pl.ds(pl.multiple_of((p * 2 + h) * rows, rows), rows)

    whole[at(pair, half)] = x[...]
    whole[at(pair, 1 - half)] = side[...]
    whole[at(1 - pair, half)] = other[...]
    whole[at(1 - pair, 1 - half), :cut] = left[...]
    whole[at(1 - pair, 1 - half), cut:] = right[...]


def take_parts(flags, whole, outs):
    one, one_sent, two, two_sent = outs
    rows, cut = one.shape[0] // 2, one.shape[1]
    pair, half = flags[0], flags[1]
    for out, p in ((one, pair), (one_sent, 1 - pair)):
        out[...] = whole[pl.ds(pl.multiple_of(p * 2 * rows, rows), 2 * rows), :cut]
    for out, h in ((two, half), (two_sent, 1 - half)):
        for p in range(2):
            at = pl.ds(pl.multiple_of((p * 2 + h) * rows, rows), rows)
            out[p * rows : (p + 1) * rows] = whole[at, cut:]


def load(flags, order, sources, whole, moved):
    if len(sources) == 1:
        move_blocks(order, sources[0], moved)
        return
    assemble(flags, sources, whole)
    move_blocks(order, whole, moved)


def store(flags, order, mixed, whole, outs):
    if len(outs) == 1:
        move_blocks(order, mixed, outs[0], back=True)
        return
    move_blocks(order, mixed, whole, back=True)
    take_parts(flags, whole, outs)


def attend(counts, starts, flags, order, *refs):
    sources, ins, w_outs, refs = cut_refs(refs, counts[:3])
    w_outs = w_outs or ins
    gains, cosine, sine, allowed, *refs = refs
    outs, refs = refs[: counts[3]], refs[counts[3] :]
    moved, proj, query, key, value, shares, attended, mixed, whole = refs
    rows, head = cosine.shape
    length = allowed.shape[1]
    heads = attended.shape[1] // head
    cols = proj.shape[1]
    load(flags, order, sources, whole, moved)
    depth = ins[0].shape[0]
    total = 0.0
    for i, w in enumerate(ins):
        total = total + dot(moved[:, i * depth : (i + 1) * depth], w[:, :cols], 1, 0)
    proj[...] = total

    def prepared(x, gain):
        turned = head_norm(x)[0] * gain
        return (turned * cosine[...] + pltpu.roll(turned, head // 2, 1) * sine[...]).astype(b16)

    for h in range(heads):
        q = prepared(proj[:, h * head : (h + 1) * head], gains[0:1])
        for s in range(rows // length):
            query[s, h * length : (h + 1) * length] = q[s * length : (s + 1) * length]
    key[...] = prepared(proj[:, heads * head : (heads + 1) * head], gains[1:2])
    value[...] = proj[:, (heads + 1) * head :].astype(b16)
    for s in range(rows // length):
        own = slice(s * length, (s + 1) * length)
        scores = dot(query[s], key[own], 1, 1) * head ** (-0.5)
        scores = scores.reshape(heads, length, length)
        scores = jnp.where((allowed[s] > 0)[None], scores, -1e30)
        raised = jnp.exp(scores - jnp.max(scores, axis=-1, keepdims=True))
        weights = raised / jnp.sum(raised, axis=-1, keepdims=True)
        weights = weights.reshape(heads * length, length)
        shares[s] = weights
        result = dot(weights.astype(b16), value[own], 1, 0).astype(b16)
        for h in range(heads):
            attended[own, h * head : (h + 1) * head] = result[h * length : (h + 1) * length]
    for i, w in enumerate(w_outs):
        at = slice(i * depth, (i + 1) * depth)
        mixed[:, at] = dot(attended[...], w[:, starts:], 1, 1).astype(b16)
    store(flags, order, mixed, whole, outs)


def cut_refs(refs, counts):
    parts = []
    for c in counts:
        parts.append(refs[:c])
        refs = refs[c:]
    return *parts, refs


def attend_back(counts, starts, flags, order, *refs):
    sources, ins, w_outs, refs = cut_refs(refs, counts[:3])
    w_outs = w_outs or ins
    gains, cosine, sine, proj, query, key, value, shares, *refs = refs
    outs, refs = refs[: counts[3]], refs[counts[3] :]
    moved, projected, gain_grads, spread, mixed, whole = refs
    rows, head = cosine.shape
    length = shares.shape[2]
    cols = proj.shape[1]
    heads = cols // head - 2
    scale = head ** (-0.5)
    load(flags, order, sources, whole, moved)
    depth = ins[0].shape[0]
    total = 0.0
    for i, w in enumerate(w_outs):
        total = total + dot(moved[:, i * depth : (i + 1) * depth], w[:, starts:], 1, 0)
    attended = total.astype(b16)
    for h in range(heads):
        for s in range(rows // length):
            spread[s, h * length : (h + 1) * length] = attended[
                s * length : (s + 1) * length, h * head : (h + 1) * head
            ]
    query_grads, key_grads = [], []
    for s in range(rows // length):
        own = slice(s * length, (s + 1) * length)
        weights = shares[s]
        given = spread[s]
        value_grad = dot(weights.astype(b16), given, 0, 0).astype(b16)
        projected[own, (heads + 1) * head :] = value_grad
        share_grad = dot(given, value[own], 1, 1)
        delta = jnp.sum(weights * share_grad, axis=-1, keepdims=True)
        score = (weights * (share_grad - delta)).astype(b16)
        query_grads.append((dot(score, key[own], 1, 0) * scale).astype(b16).astype(f32))
        key_grads.append((dot(score, query[s], 0, 0) * scale).astype(b16).astype(f32))

    def prepared_back(grad, x, gain):
        turned = grad * cosine[...] + pltpu.roll(grad * sine[...], head // 2, 1)
        normed, inverse = head_norm(x)
        scaled = turned * gain
        mean = jnp.mean(scaled * normed, axis=-1, keepdims=True)
        gain_grad = jnp.sum(turned * normed, axis=0, keepdims=True)
        return ((scaled - normed * mean) * inverse).astype(b16), gain_grad

    total = jnp.zeros((1, head), f32)
    for h in range(heads):
        grad = jnp.concatenate([g[h * length : (h + 1) * length] for g in query_grads], axis=0)
        at = slice(h * head, (h + 1) * head)
        projected[:, at], gain_grad = prepared_back(grad, proj[:, at], gains[0:1])
        total = total + gain_grad
    at = slice(heads * head, (heads + 1) * head)
    grad = jnp.concatenate(key_grads, axis=0)
    projected[:, at], gain_grad = prepared_back(grad, proj[:, at], gains[1:2])
    gain_grads[0:1] = total
    gain_grads[1:2] = gain_grad
    for i, w in enumerate(ins):
        at = slice(i * depth, (i + 1) * depth)
        mixed[:, at] = dot(projected[...], w[:, :cols], 1, 1).astype(b16)
    store(flags, order, mixed, whole, outs)


def in_vmem(kernel, outs, scratch, scalars, *args):
    scalars = scalars if isinstance(scalars, tuple) else (scalars,)
    whole = pl.BlockSpec(memory_space=pltpu.VMEM)
    return pl.pallas_call(
        kernel,
        out_shape=[jax.ShapeDtypeStruct(*o) for o in outs],
        in_specs=[pl.BlockSpec(memory_space=pltpu.SMEM)] * len(scalars) + [whole] * len(args),
        out_specs=[whole] * len(outs),
        scratch_shapes=[pltpu.VMEM(*o) for o in scratch],
        compiler_params=pltpu.CompilerParams(vmem_limit_bytes=48 << 20),
        cost_estimate=pl.CostEstimate(flops=0, bytes_accessed=0, transcendentals=0),
    )(*scalars, *args)


def on_plane(kernel, sources, place, weights, start, outs, scratch, *args):
    pair, half, orders = place
    rows, width = 4 * sources[0].shape[0], sources[0].shape[1]
    direct = width // orders[0].shape[0] % 128 != 0
    if len(sources) == 1:
        rows = sources[0].shape[0]
    elif direct:
        sources = [plane_whole(sources, pair, half)]
    if direct:
        sources = [shuffle_outside(sources[0], orders[0])]
    parts = [((rows, width), b16)] if direct else [((rows // 2, width // 2), b16)] * 4
    counts = (len(sources), len(weights[0]), len(weights[1]), len(parts))
    results = in_vmem(
        functools.partial(kernel, counts, start),
        parts + outs,
        scratch + [((rows, width), b16)] * 2,
        (jnp.stack([pair, half]).astype(jnp.int32), orders[0]),
        *sources,
        *weights[0],
        *weights[1],
        *args,
    )
    parts, others = list(results[: len(parts)]), list(results[len(parts) :])
    if direct:
        parts = plane_parts(shuffle_outside(parts[0], orders[1]), pair, half)
    return parts, others


def attention_forward(sources, place, weights, start, sizes, gains, tables, allowed):
    rows, head, length = tables[0].shape[0], gains.shape[1], allowed.shape[1]
    cols, heads_cols = sizes
    stacked = (rows // length, heads_cols // head * length)
    outs = [
        ((rows, sources[0].shape[1]), b16),
        ((rows, cols), f32),
        (stacked + (head,), b16),
        ((rows, head), b16),
        ((rows, head), b16),
        (stacked + (length,), f32),
        ((rows, heads_cols), b16),
    ]
    return on_plane(
        attend, sources, place, weights, start, outs, [], gains, *tables, allowed
    )


def attention_backward(sources, place, saved, weights, start, gains, tables):
    moved, proj, query, key, value, shares, _ = saved
    outs = [(moved.shape, b16), (proj.shape, b16), (gains.shape, f32)]
    return on_plane(
        attend_back,
        sources,
        place,
        weights,
        start,
        outs,
        [(query.shape, b16)],
        gains,
        *tables,
        proj,
        query,
        key,
        value,
        shares,
    )


def spread(gates, local, width):
    per = width // local
    rows = gates.shape[0]
    return jnp.concatenate(
        [jnp.broadcast_to(gates[:, j : j + 1], (rows, per)) for j in range(local)], axis=1
    )


def fetch(which, sizes, refs, target, sem):
    for k, size in enumerate(sizes):
        parts, refs = refs[:size], refs[size:]

        @pl.when(which == k)
        def _():
            start = 0
            for part in parts:
                rows = part.shape[0]
                pltpu.make_async_copy(part, target.at[pl.ds(start, rows)], sem).start()
                start += rows


def fetch_both(which, sizes, refs, targets, sems):
    for k, (size, target) in enumerate(zip(sizes, targets)):
        fetch(which, size, refs, target, sems.at[k])
        refs = refs[sum(size) :]
    for k, target in enumerate(targets):
        pltpu.make_async_copy(target, target, sems.at[k]).wait()


def experts_ahead(
    local, sizes, scalars, rows_own, rows_other, codes_own, codes_other, router, *refs
):
    choices, outs, scratch = refs[: -6 - 3], refs[-6 - 3 : -3], refs[-3:]
    part_own, part_other, rows_all, gates_out, hidden_out, units_out = outs
    weights_gu, weights_down, sems = scratch
    step, half = pl.program_id(0), pl.num_programs(0) // 2

    @pl.when(step == 0)
    def _():
        fetch_both(scalars[0], sizes, choices, (weights_gu, weights_down), sems)

    first = step < half
    rows = jnp.where(first, rows_own[...], rows_other[...])
    codes = jnp.where(first, codes_own[...], codes_other[...])
    rows_all[...] = rows
    gates = gates_of(dot(rows, router[...], 1, 0), (codes > 0.5).astype(f32))
    gates = jnp.where(codes > 1.5, gates, 0.0)
    ids = lax.broadcasted_iota(jnp.int32, gates.shape, 1)
    spots = lax.broadcasted_iota(jnp.int32, gates_out.shape, 1)
    kept = jnp.zeros(gates_out.shape, f32)
    for j in range(local):
        own = jnp.sum(jnp.where(ids == scalars[1] + j, gates, 0.0), axis=1, keepdims=True)
        kept = jnp.where(spots == j, own, kept)
    gates_out[...] = kept
    hidden = dot(rows, weights_gu[...], 1, 0)
    hidden_out[...] = hidden
    cut = hidden.shape[1] // 2
    units = swiglu(hidden[:, :cut], hidden[:, cut:])
    units_b = (units * spread(kept, local, cut)).astype(b16)
    units_out[...] = units_b
    part = dot(units_b, weights_down[...], 1, 0).astype(b16)

    @pl.when(first)
    def _():
        part_own[...] = part

    @pl.when(step >= half)
    def _():
        part_other[...] = part


def experts_back(local, experts, sizes, scalars, grads_own, grads_other, gates, hidden, *refs):
    choices, outs, scratch = refs[: -4 - 3], refs[-4 - 3 : -3], refs[-3:]
    part_own, part_other, grads_all, hidden_out = outs
    weights_gu, weights_down, sems = scratch
    step, half = pl.program_id(0), pl.num_programs(0) // 2

    @pl.when(step == 0)
    def _():
        fetch_both(scalars[0], sizes, choices, (weights_gu, weights_down), sems)

    first = step < half
    grads = jnp.where(first, grads_own[...], grads_other[...])
    grads_all[...] = grads
    raw = dot(grads, weights_down[...], 1, 1)
    cut = raw.shape[1]
    gate, up = hidden[:, :cut], hidden[:, cut:]
    share = jax.nn.sigmoid(gate)
    silu = gate * share
    scaled = raw * spread(gates[...], local, cut)
    gate_grad = (scaled * up * (share + silu * (1.0 - share))).astype(b16)
    up_grad = (scaled * silu).astype(b16)
    hidden_b = jnp.concatenate([gate_grad, up_grad], axis=1)
    hidden_out[...] = hidden_b
    part = dot(hidden_b, weights_gu[...], 1, 1).astype(b16)
    overlap = raw * silu * up
    per = cut // local
    wide = part_own.shape[1] - part.shape[1]
    spots = lax.broadcasted_iota(jnp.int32, (grads.shape[0], wide), 1)
    extra = jnp.zeros(spots.shape, f32)
    for j in range(local):
        value = jnp.sum(overlap[:, j * per : (j + 1) * per], axis=1, keepdims=True)
        high = value.astype(b16).astype(f32)
        extra = jnp.where(spots == scalars[1] + j, high, extra)
        extra = jnp.where(spots == experts + scalars[1] + j, value - high, extra)
    extra = extra.astype(b16)
    width = part.shape[1]

    @pl.when(first)
    def _():
        part_own[:, :width] = part
        part_own[:, width:] = extra

    @pl.when(step >= half)
    def _():
        part_other[:, :width] = part
        part_other[:, width:] = extra


def by_rows(kernel, which, first_expert, halved, whole, fixed, choices, outs_halved, outs):
    rows = halved[0][0].shape[0]
    block = 256
    count = rows // block
    weights = [choice[0][0].shape for choice in choices]

    def spec(a, index):
        return pl.BlockSpec((block, a.shape[1]), index)

    def own(i, *_):
        return jnp.minimum(i, count - 1), 0

    def other(i, *_):
        return jnp.maximum(i - count, 0), 0

    def each(i, *_):
        return i, 0

    in_specs = []
    for first, second in halved:
        in_specs += [spec(first, own), spec(second, other)]
    in_specs += [spec(a, each) for a in whole]
    in_specs += [pl.BlockSpec(a.shape, lambda i, *_: (0, 0)) for a in fixed]
    sizes = [[len(parts) for parts in choice] for choice in choices]
    choices = [a for choice in choices for parts in choice for a in parts]
    in_specs += [pl.BlockSpec(memory_space=pl.ANY)] * len(choices)
    shapes = [jax.ShapeDtypeStruct((rows, w), b16) for w in (outs_halved, outs_halved)]
    shapes += [jax.ShapeDtypeStruct((2 * rows, w), t) for w, t in outs]
    out_specs = [spec(shapes[0], own), spec(shapes[1], other)]
    out_specs += [spec(a, each) for a in shapes[2:]]
    weights = [pltpu.VMEM(a, b16) for a in weights]
    return pl.pallas_call(
        functools.partial(kernel, sizes),
        grid_spec=pltpu.PrefetchScalarGridSpec(
            num_scalar_prefetch=1,
            grid=(2 * count,),
            in_specs=in_specs,
            out_specs=out_specs,
            scratch_shapes=weights + [pltpu.SemaphoreType.DMA((2,))],
        ),
        out_shape=shapes,
        compiler_params=pltpu.CompilerParams(vmem_limit_bytes=48 << 20),
        cost_estimate=pl.CostEstimate(flops=0, bytes_accessed=0, transcendentals=0),
    )(
        jnp.stack([which, first_expert]).astype(jnp.int32),
        *[a for pair in halved for a in pair],
        *whole,
        *fixed,
        *choices,
    )


def experts_forward(rows, codes, router, which, choices, first_expert, local):
    width = rows[0].shape[1]
    hidden = choices[0][0][0].shape[1]
    outs = [(width, b16), (128, f32), (hidden, f32), (hidden // 2, b16)]
    part_own, part_other, *saved = by_rows(
        functools.partial(experts_ahead, local),
        which,
        first_expert,
        [rows, codes],
        [],
        [router],
        choices,
        width,
        outs,
    )
    return (part_own, part_other), saved


def experts_backward(grads, saved, which, choices, first_expert, local, experts):
    _, gates, hidden, _ = saved
    width = grads[0].shape[1]
    wide = -(-2 * experts // 128) * 128
    outs = [(width, b16), (hidden.shape[1], b16)]
    part_own, part_other, *others = by_rows(
        functools.partial(experts_back, local, experts),
        which,
        first_expert,
        [grads],
        [gates, hidden],
        [],
        choices,
        width + wide,
        outs,
    )
    return (part_own, part_other), others


def own_sums(steps, flags, *refs):
    parts = len(steps)
    ins, outs = refs[: 6 * parts], refs[6 * parts :]

    def write(own, side, core):
        total = side[...].astype(f32) + core[...].astype(f32)
        total = total + jnp.where(flags[0] == flags[1], own[...].astype(f32), 0.0)
        if len(outs) == 1:
            outs[0][...] = total
            return
        per = outs[0].shape[2]
        for i, out in enumerate(outs):
            for j in range(out.shape[0]):
                at = (i * out.shape[0] + j) * per
                out[j] = total[:, at : at + per]

    at = pl.program_id(0)
    for l in range(2):
        for k, (first, last) in enumerate(steps):

            @pl.when((flags[0] == l) & (at >= first) & (at < last))
            def _():
                base = 3 * (l * parts + k)
                write(*ins[base : base + 3])


def owned(core, half, by_layer, pieces):
    step = 256
    steps, specs, rows = [], [], 0
    for own, _, _ in by_layer[0]:
        steps.append((rows // step, (rows + own.shape[0]) // step))
        rows += own.shape[0]
    cols = by_layer[0][0][0].shape[1]
    for l in range(2):
        for first, last in steps:

            def where(i, f, l=l, first=first, last=last):
                inside = jnp.clip(i - first, 0, last - first - 1)
                return jnp.where(f[0] == l, inside, 0), 0

            specs += [pl.BlockSpec((step, cols), where)] * 3
    if pieces == 1:
        outs = [jax.ShapeDtypeStruct((rows, cols), f32)]
        out_specs = [pl.BlockSpec((step, cols), lambda i, f: (i, 0))]
    else:
        shape = (pieces // 2, rows, cols // pieces)
        outs = [jax.ShapeDtypeStruct(shape, f32)] * 2
        block = (pieces // 2, step, cols // pieces)
        out_specs = [pl.BlockSpec(block, lambda i, f: (0, i, 0))] * 2
    terms = [t for layer in by_layer for part in layer for t in part]
    return pl.pallas_call(
        functools.partial(own_sums, steps),
        grid_spec=pltpu.PrefetchScalarGridSpec(
            num_scalar_prefetch=1, grid=(rows // step,), in_specs=specs, out_specs=out_specs
        ),
        out_shape=outs,
        compiler_params=pltpu.CompilerParams(vmem_limit_bytes=48 << 20),
        cost_estimate=pl.CostEstimate(flops=0, bytes_accessed=0, transcendentals=0),
    )(jnp.stack([core, half]).astype(jnp.int32), *terms)


def shards(
    inputs,
    cotangent,
    segments,
    routes,
    counts,
    norm_attn,
    norm_ffn,
    q_gain,
    k_gain,
    w_query,
    w_key,
    w_value,
    w_output,
    w_router,
    w_gate,
    w_up,
    w_down,
):
    core, at, half = lax.axis_index(C), lax.axis_index(E), lax.axis_index(H)
    pair = lax.rem(at // 2, 2)
    n = lax.axis_size(E)
    _, tokens, width = inputs.shape
    rows = tokens // 2
    experts = counts.shape[1]
    local = w_gate.shape[1]
    units = w_gate.shape[3]
    first_expert = at * local
    head_size = q_gain.shape[1]
    place = pair, half, relative_order(core, at)

    def by_group(weight):
        return weight[0].reshape(weight.shape[1], 2, -1).transpose(1, 0, 2)

    packed = jnp.concatenate([by_group(w) for w in (w_query, w_key, w_value, w_output)], axis=2)
    halves = halves_for_cores(packed, core)
    heads_cols = w_output.shape[2] // 2
    cut = packed.shape[2] - heads_cols
    sizes = cut, heads_cols
    weights, starts = [None, None], (0, 0)
    first = [pair_rows(h, pair) for h in (halves[0][..., :cut], halves[0][..., cut:])]
    (weights_in, _), (weights_out, arrived) = (gather_weight(h) for h in first)
    weights[0] = weights_in, weights_out
    grad = lax.dynamic_slice_in_dim(pick(cotangent, core), half * rows, rows, 0)
    grads_all = gather_rows(after(grad, *first))

    def both_layers(own):
        return ordered(core, own, after(core_swap(own), first[0]))

    norm_attn, norm_ffn, q_gain, k_gain = (
        both_layers(a[0]) for a in (norm_attn, norm_ffn, q_gain, k_gain)
    )
    counts = both_layers(counts[0])
    chosen = after(core_swap(pick(routes[0], 1 - core)), first[0])
    chosen = ordered(core, pick(routes[0], core), chosen)
    block_rows = tokens * chosen.shape[2] // (4 * experts)
    codes = [route_codes(chosen[l], counts[l], block_rows) for l in range(2)]
    codes = jnp.concatenate(codes, axis=1)
    codes_own = lax.dynamic_slice_in_dim(codes, half * rows, rows, 0)
    wide = -(-2 * experts // 128) * 128
    codes_sent = jnp.pad(codes_own.astype(b16), ((0, 0), (0, wide - 2 * experts)))
    router_sent = w_router[0].reshape(-1, wide)
    tables_sent = jnp.concatenate([codes_sent, router_sent], axis=0)
    codes_own = [codes_own[:, l * experts : (l + 1) * experts] for l in range(2)]

    seg_own = pick(segments, core)[0]
    seg_ids = ordered(pair, seg_own, after(pair_swap(seg_own), first[0]))
    spots = jnp.arange(tokens)
    allowed = (spots[:, None] >= spots[None, :])[None] & (
        seg_ids[:, :, None] == seg_ids[:, None, :]
    )
    allowed = allowed.astype(f32)
    tables = [jnp.concatenate([t, t], axis=0) for t in rotary_tables(tokens, head_size)]

    at_first = (core == 0) & (half == 0)
    at_last = (core == 1) & (half == 1)
    own_gu = jnp.concatenate([w[0, j] for w in (w_gate, w_up) for j in range(local)], axis=1)
    own_down = w_down[0].reshape(-1, width)
    which = [
        jnp.where(keeps, 0, jnp.where(takes, 2, 1))
        for keeps, takes in ((at_first, at_last), (at_last, at_first))
    ]

    def experts_sent(layer, cuts, *marker):
        if layer == 0:
            by_side = [((0, 0), (0, 1)), ((0, 1), (1, 0))]
            by_core = [((0, 1), (1, 1))]
        else:
            by_side = [((1, 0), (0, 1)), ((1, 1), (1, 0))]
            by_core = [((1, 0), (0, 0))]
        sent = []
        for w, count in zip((own_gu, own_down), cuts):
            step = w.shape[0] // count
            parts = [w[i * step : (i + 1) * step] if count > 1 else w for i in range(count)]
            parts = [send(p, by_side) for p in after(parts, *marker)]
            sent.append(([w], parts, [send(w, by_core)]))
        return sent

    choices = [experts_sent(0, (1, 1)), None]

    layer_in = lax.dynamic_slice_in_dim(pick(inputs, core), half * rows, rows, 0)
    whole_in = pick(inputs, core)
    others_in = after(pair_swap(whole_in), first[0])
    whole_in = ordered(pair, whole_in, others_in).reshape(-1, width)
    sources = [norm_rows(whole_in.astype(f32), norm_attn[0]).astype(b16)]
    sources = after(sources, *choices[0][0][1], *choices[0][1][1], *grads_all)
    gains = jnp.stack([q_gain, k_gain], axis=1)
    kept_attn, kept_rows, kept_experts = [], [], []
    for l in range(2):
        if l == 1:
            mine = norm_rows(layer_in.astype(f32), norm_attn[1]).astype(b16)
            sources = plane_pieces(mine)
        parts, saved = attention_forward(
            sources, place, weights[l], starts[l], sizes, gains[l], tables, allowed
        )
        if l == 0:
            tables_all = [t.reshape(n, -1, wide) for t in gather_rows(after(tables_sent, saved[6]))]
            codes_all = [t[:, :rows].reshape(-1, wide).astype(f32) for t in tables_all]
            routers = [jnp.take(t[:, rows:], position(at), axis=0) for t in tables_all]
            routers = ordered(core, *routers).reshape(2, width, experts)
            codes_all = [[c[:, l * experts : (l + 1) * experts] for c in codes_all] for l in range(2)]
            second_pair = pair_rows(after(halves[1], arrived), pair)
            second_near = near_swap(second_pair)
            parts[0] = after(parts[0], second_pair)
        hidden = layer_in.astype(f32) + plane_scatter(parts, pair, half)
        normed_two = norm_rows(hidden, norm_ffn[l]).astype(b16)
        if l == 0:
            normed_two = after(normed_two, second_near, *codes_all[0], *codes_all[1], routers)
            choices[1] = experts_sent(1, (2, 2), normed_two)
            gu_parts, down_parts = choices[1][0][1], choices[1][1][1]
            rows_all = gather_rows(normed_two, (), gu_parts[:1])
        else:
            rows_all = gather_rows(normed_two, (), down_parts[1:])
        parts, saved_experts = experts_forward(
            rows_all, codes_all[l], routers[l], which[l], choices[l], first_expert, local
        )
        kept_experts.append(saved_experts)
        kept_attn.append(saved)
        kept_rows.append((layer_in, hidden, normed_two))
        if l == 0:
            pieces = after([second_pair[..., :cut], second_pair[..., cut:]], rows_all[0])
            far = [[turn(p, d) for d in range(1, n // 4)] for p in pieces]
            parts = after(parts, *far[0])
            summed = sum_cores(*parts)
            near = [near_swap(p) for p in after(far[0], summed)]
            near = [near, [near_swap(p) for p in after(far[1], *near)]]
            moved = scatter_rows(
                summed, [*far[1], gu_parts[1]], near[0], near[1] + down_parts[:1]
            )
            layer_in = (hidden + moved).astype(b16)
            weights[1] = []
            for k, (a, b) in enumerate(((0, cut), (cut, packed.shape[2]))):
                mine = [second_pair[..., a:b], second_near[..., a:b]]
                for p in zip(far[k], near[k]):
                    mine += p
                mine = [flat(p) for p in mine]
                weights[1].append(mine + [core_swap(p) for p in mine])
    last_parts, last_rows = parts, None

    grads_in, small, grads_experts = ([None] * 2 for _ in range(3))

    def expert_grads(l, marker, grads_all, hidden_b):
        rows_all, _, _, units_b = kept_experts[l]
        units_b, hidden_b = after((units_b, hidden_b), marker)
        cuts = [slice(0, width // 2), slice(width // 2, width)]
        return [dot(rows_all[:, c], hidden_b, 0, 0).astype(b16) for c in cuts] + [
            dot(units_b, grads_all, 0, 0).astype(b16)
        ]

    def to_owners(l, piece):
        if l == 0:
            by_side = [((0, 1), (0, 0)), ((1, 0), (0, 1))]
            by_core = [((1, 1), (0, 1))]
        else:
            by_side = [((0, 1), (1, 0)), ((1, 0), (1, 1))]
            by_core = [((0, 0), (1, 0))]
        return [send(piece, by_side), send(piece, by_core)]

    def both_batches(first, second):
        others = core_swap(either(core, second, first))
        both = ordered(core, either(core, first, second), others)
        swapped = side_swap(both)
        both = ordered(half, both, swapped).transpose(1, 0, 2, 3)
        return both.reshape(2, tokens, width), swapped

    late_qkv, late_out, received = None, None, [[], []]
    for l in (1, 0):
        layer_in, hidden, normed_two = kept_rows[l]
        grad_f = grad.astype(f32)
        if l == 0:
            sent = to_owners(1, after(grads_experts[1][1], grad))
            received[1].append(sent)
            grads_all = gather_rows(grad, (), sent[:1])
            received[1].append(to_owners(1, after(grads_experts[1][2], sent[0])))
        parts, (grads_joined, hidden_b) = experts_backward(
            grads_all, kept_experts[l], which[l], choices[l], first_expert, local, experts
        )
        mid, last, end = [], [], []
        if l == 0:
            late_out = near_parts(late_out)
            last_rows = pair_stage(last_rows)
            parts = after(parts, late_out[1], last_rows[1])
        summed = sum_cores(*parts)
        grads_experts[l] = expert_grads(l, summed, grads_joined, hidden_b)
        piece = grads_experts[l][0]
        if l == 0:
            piece = after(piece, received[1][2][0])
        sent = to_owners(l, piece)
        received[l].append(sent)
        if l == 0:
            late_out = turn_parts(near_sums((after(late_out[0], summed), late_out[1])))
            late_qkv = near_parts(after(late_qkv, summed))
            last_rows = turn_stage((after(last_rows[0], summed), last_rows[1]))
            mid, last, end = late_out[1], last_rows[1], late_qkv[1:]
        else:
            rows_kept, rows_sent = near_pieces(sum_cores(*after(last_parts, parts[0])))
            rows_got = [near_swap(rows_sent[..., : width // 2])]
            end = rows_got
        moved = scatter_rows(
            summed, grads_experts[l][:2] + mid, grads_experts[l][2:] + last, sent[:1] + list(end)
        )
        normed_grad, extra = moved[:, :width], moved[:, width:]
        overlap = extra[:, :experts] + extra[:, experts : 2 * experts]
        chosen_f = (codes_own[l] > 0.5).astype(f32)
        logits = dot(normed_two, routers[l], 1, 0)
        gates_back = jax.vjp(lambda v: gates_of(v, chosen_f), logits)[1]
        logit_b = gates_back(jnp.where(codes_own[l] > 1.5, overlap, 0.0))[0].astype(b16)
        normed_grad = normed_grad + dot(logit_b, routers[l], 1, 1)
        grad_router = dot(logit_b, normed_two, 0, 0)
        hidden_grad, grad_norm_ffn = jax.vjp(norm_rows, hidden, norm_ffn[l])[1](normed_grad)
        hidden_grad = hidden_grad + grad_f
        branch_b = hidden_grad.astype(b16)
        sources = plane_pieces(branch_b)
        parts, (branch_b, projected_b, gain_grads) = attention_backward(
            sources, place, kept_attn[l], weights[l], starts[l], gains[l], tables
        )
        product_out = weight_product(branch_b, kept_attn[l][6])
        product_qkv = weight_product(kept_attn[l][0], projected_b)
        if l == 1:
            late_out, late_qkv = product_out, product_qkv
            rows_got.append(near_swap(after(rows_sent[..., width // 2 :], moved)))
            parts[0] = after(parts[0], rows_got[1])
            last_rows = rows_kept, jnp.concatenate(rows_got, axis=-1)
        else:
            parts[0] = after(parts[0], product_out, product_qkv)
            late_qkv = turn_parts(near_sums(late_qkv, moved))
            layer_out = kept_rows[1][1] + last_stage(last_rows)
            activations, marker = both_batches(kept_rows[1][0], layer_out.astype(b16))
            parts[0] = after(parts[0], *late_qkv[1], marker)
            last_out, last_qkv = near_parts(product_out), near_parts(product_qkv)
        input_grad, grad_norm_attn = jax.vjp(norm_rows, layer_in.astype(f32), norm_attn[l])[1](
            plane_scatter(parts, pair, half)
        )
        grad = (input_grad + hidden_grad).astype(b16)
        if l == 0:
            grad = after(grad, last_out[1])
        grads_in[l] = grad
        gain_row = jnp.concatenate([g.reshape(n, -1) for g in gain_grads], axis=1)
        gain_row = jnp.pad(gain_row, ((0, 0), (0, width // n - gain_row.shape[1])))
        small[l] = jnp.concatenate(
            [grad_router, grad_norm_attn[None], grad_norm_ffn[None], gain_row.reshape(1, -1)],
            axis=0,
        )

    input_grads, marker = both_batches(grads_in[0], grads_in[1])
    last_out = turn_parts(near_sums(last_out))
    late = pair_columns(jnp.concatenate([turn_sums(late_qkv), turn_sums(late_out)], axis=2), pair)
    for p in grads_experts[0][1:]:
        received[0].append(to_owners(0, after(p, marker, received[0][-1][0])))
    received[1] = after(received[1], grad)
    last_qkv = near_sums((last_qkv[0], after(last_qkv[1], *last_out[1], late, marker)))
    last_qkv = turn_parts(last_qkv)

    def of_owner(ks, count):
        return owned(
            core, half, [[(grads_experts[l][k], *received[l][k]) for k in ks] for l in range(2)], count
        )

    grad_gate, grad_up = of_owner((0, 1), 2 * local)
    last_qkv = last_qkv[0], after(last_qkv[1], grad_gate)

    others = core_swap(either(core, small[1], small[0]))
    mine = either(core, small[0], small[1]) + others
    count = mine.shape[0]
    mine = mine.reshape(count, n, width // n).transpose(1, 0, 2)
    mine = jnp.take(mine, position(at), axis=0)
    mine = turn_stage(pair_stage(near_stage(mine)))
    mine = last_stage(mine)
    mine = mine + side_swap(mine)
    per = head_size // n

    widths = [w.shape[2] for w in (w_query, w_key, w_value, w_output)]
    last = [pair_columns(turn_sums(t), pair) for t in (last_out, last_qkv)]
    weight_grads = to_owner(jnp.concatenate(last[::-1], axis=2), late, core, widths, pair)

    (grad_down,) = of_owner((2,), 1)
    grad_down = grad_down.reshape(local, units, width)
    return (
        activations[None],
        input_grads[None],
        mine[experts][None],
        mine[experts + 1][None],
        mine[experts + 2, :per][None],
        mine[experts + 2, per : 2 * per][None],
        *[w[None] for w in weight_grads],
        mine[:experts].T[None],
        grad_gate[None],
        grad_up[None],
        grad_down[None],
    )


def solution(mesh):
    by_layer = P(C, None)
    in_specs = (
        P(None, E, None),
        P(None, E, None),
        P(None, E, None),
        P(C, None, E, None),
        by_layer,
        by_layer,
        by_layer,
        by_layer,
        by_layer,
        P(C, E, H),
        P(C, E, H),
        P(C, E, H),
        P(C, E, H),
        P(C, E, None),
        P(C, E, None, H),
        P(C, E, None, H),
        P(C, E, H, None),
    )
    out_specs = (
        P(C, None, E, None),
        P(C, None, E, None),
        P(C, E),
        P(C, E),
        P(C, E),
        P(C, E),
        P(C, E, H),
        P(C, E, H),
        P(C, E, H),
        P(C, E, H),
        P(C, E, None),
        P(C, E, None, H),
        P(C, E, None, H),
        P(C, E, H, None),
    )
    return jax.shard_map(shards, mesh=mesh, in_specs=in_specs, out_specs=out_specs, check_vma=False)
```

```python
import functools

import jax
import jax.numpy as jnp
from jax import lax
from jax.experimental import pallas as pl
from jax.experimental.pallas import tpu as pltpu
from jax.sharding import PartitionSpec as P

C, E, H = "section", "expert", "shard"
f32 = jnp.float32
b16 = jnp.bfloat16

eps = 1e-06
theta = 1000000.0


def core_swap(x):
    return lax.ppermute(x, C, [(0, 1), (1, 0)])


def side_swap(x):
    return lax.ppermute(x, H, [(0, 1), (1, 0)])


def near_swap(x):
    return lax.ppermute(x, E, [(e, e ^ 1) for e in range(lax.axis_size(E))])


def pair_swap(x):
    return lax.ppermute(x, E, [(e, e ^ 2) for e in range(lax.axis_size(E))])


def turn(x, by):
    length = lax.axis_size(E) // 4
    pairs = [(e, (e // 4 + by) % length * 4 + e % 4) for e in range(4 * length)]
    return lax.ppermute(x, E, pairs)


def turns():
    length = lax.axis_size(E) // 4
    return sorted(range(1, length), key=lambda d: (min(d, length - d), d))


def send(x, pairs):
    return lax.ppermute(x, (C, H), [(2 * a + b, 2 * c + d) for (a, b), (c, d) in pairs])


def tie(*refs):
    pass


def after(x, *markers):
    if not markers:
        return x
    leaves, tree = jax.tree.flatten(x)
    here = pl.BlockSpec(memory_space=pl.ANY)
    tied = pl.pallas_call(
        tie,
        out_shape=[jax.ShapeDtypeStruct(a.shape, a.dtype) for a in leaves],
        in_specs=[here] * (len(leaves) + len(markers)),
        out_specs=[here] * len(leaves),
        input_output_aliases={i: i for i in range(len(leaves))},
        cost_estimate=pl.CostEstimate(flops=0, bytes_accessed=0, transcendentals=0),
    )(*leaves, *markers)
    return jax.tree.unflatten(tree, tied)


def pick(x, index, axis=0):
    return lax.dynamic_index_in_dim(x, index, axis, keepdims=False)


def either(flag, first, second):
    return jnp.where(flag == 0, first, second)


def ordered(flag, own, other):
    return jnp.where(flag == 0, jnp.stack([own, other]), jnp.stack([other, own]))


def dot(left, right, at_left, at_right, batch=()):
    return lax.dot_general(
        left, right, (((at_left,), (at_right,)), (batch, batch)), preferred_element_type=f32
    )


def norm_rows(values, weight):
    inverse = lax.rsqrt(jnp.mean(values * values, axis=-1, keepdims=True) + eps)
    return values * inverse * weight


def rotary_tables(length, head_size):
    halfway = head_size // 2
    frequency = theta ** (-jnp.arange(halfway, dtype=f32) * 2.0 / head_size)
    angles = jnp.arange(length, dtype=f32)[:, None] * frequency[None, :]
    cosine, sine = jnp.cos(angles), jnp.sin(angles)
    return (
        jnp.concatenate([cosine, cosine], axis=1),
        jnp.concatenate([-sine, sine], axis=1),
    )


def swiglu(gate_vals, up_vals):
    return gate_vals * jax.nn.sigmoid(gate_vals) * up_vals


def gates_of(logits, chosen):
    largest = jnp.max(logits, axis=-1, keepdims=True)
    raised = jnp.exp(logits - largest)
    picked = raised / jnp.sum(raised, axis=-1, keepdims=True) * chosen
    return picked / jnp.sum(picked, axis=-1, keepdims=True)


def route_codes(chosen, counts, block_rows):
    tokens, experts = chosen.shape[0], counts.shape[0]
    ids = jnp.arange(experts, dtype=jnp.int32)
    member = jnp.any(chosen[:, :, None] == ids[None, None, :], axis=1)
    spots = jnp.arange(tokens)
    earlier = (spots[:, None] > spots[None, :]).astype(b16)
    rank = dot(earlier, member.astype(b16), 1, 0)
    kept = member & (rank < (counts * block_rows).astype(f32)[None, :])
    return member.astype(f32) + kept.astype(f32)


def gather_rows(x, mid=(), end=()):
    length = lax.axis_size(E) // 4
    held = {(0, 0): x}
    for d in turns():
        held[d, 0] = turn(x, d)
    for d in [0] + turns():
        held[d, 1] = pair_swap(held[d, 0])
    keys = sorted(held, key=lambda k: sum(k))
    near = {k: near_swap(held[k]) for k in keys[:-1]}
    near[keys[-1]] = after(near_swap(after(held[keys[-1]], *mid)), *end)
    spots = [(d, p) for d in range(length) for p in range(2)]
    mine = jnp.concatenate([v for k in spots for v in (held[k], near[k])], axis=0)
    return mine, core_swap(mine)


def scatter_rows(pieces, mid=(), last=(), end=()):
    length = lax.axis_size(E) // 4
    pieces = pieces.reshape((length, 2, 2) + pieces.shape[1:])
    far = turns()[::-1] + [0]
    held = {}
    for p in (1, 0):
        for d in far:
            held[d, p] = pieces[d, p, 0].astype(f32)
            held[d, p] += near_swap(pieces[d, p, 1].astype(b16)).astype(f32)
    sent = after([held[d, 1].astype(b16) for d in far], *mid)
    swapped = after([pair_swap(a) for a in sent], *last)
    lined = {d: held[d, 0] + a.astype(f32) for d, a in zip(far, swapped)}
    turned = after([turn(lined[d].astype(b16), -d) for d in far[:-1]], *end)
    total = lined[0]
    for a in turned:
        total = total + a.astype(f32)
    return total


def near_pieces(pieces):
    pieces = pieces.reshape((-1, 2, 2) + pieces.shape[1:])
    return pieces[:, :, 0], pieces[:, :, 1].astype(b16)


def near_stage(pieces):
    kept, sent = near_pieces(pieces)
    return kept, near_swap(sent)


def pair_stage(stage, *markers):
    kept, got = stage
    held = kept.astype(f32) + after(got, *markers).astype(f32)
    return held[:, 0], pair_swap(held[:, 1].astype(b16))


def turn_stage(stage, *markers):
    kept, got = stage
    lined = kept + after(got, *markers).astype(f32)
    return lined[0], [turn(lined[d].astype(b16), -d) for d in range(1, lined.shape[0])]


def last_stage(stage, *markers):
    kept, got = stage
    return kept + sum(g.astype(f32) for g in after(got, *markers))


def sum_cores(own, other):
    summed = (own.astype(f32) + core_swap(other).astype(f32)).astype(b16)
    return summed.reshape(lax.axis_size(E), -1, own.shape[1])


def position(at):
    length = lax.axis_size(E) // 4
    spots = jnp.arange(4 * length)
    return lax.rem(at // 4 + length - spots // 4, length) * 4 + ((at % 4) ^ (spots % 4))


def plane_pieces(x):
    cut = x.shape[1] // 2
    side, other = side_swap(x), pair_swap(x)
    return x, side, other, pair_swap(side[:, :cut]), side_swap(other[:, cut:])


def plane_whole(pieces, pair, half):
    x, side, other, *across = pieces
    across = jnp.concatenate(across, axis=1)
    own_seq = ordered(half, x, side)
    other_seq = ordered(half, other, across)
    return ordered(pair, own_seq, other_seq).reshape(-1, x.shape[1])


def plane_parts(part, pair, half):
    width = part.shape[1]
    cut = width // 2
    parts = part.reshape(2, 2, -1, width)
    one, two = parts[..., :cut], parts[..., cut:]
    parts = [
        either(pair, one[0], one[1]),
        either(pair, one[1], one[0]),
        either(half, two[:, 0], two[:, 1]),
        either(half, two[:, 1], two[:, 0]),
    ]
    return [p.reshape(-1, cut) for p in parts]


def plane_scatter(parts, pair, half):
    one, one_sent, two, two_sent = parts
    rows = one.shape[0] // 2
    one = one.astype(f32) + pair_swap(one_sent).astype(f32)
    two = two.astype(f32) + side_swap(two_sent).astype(f32)
    one = either(half, one[:rows], one[rows:]) + side_swap(
        either(half, one[rows:], one[:rows]).astype(b16)
    ).astype(f32)
    two = either(pair, two[:rows], two[rows:]) + pair_swap(
        either(pair, two[rows:], two[:rows]).astype(b16)
    ).astype(f32)
    return jnp.concatenate([one, two], axis=1)


def halves_for_cores(packed, core):
    rows = packed.shape[1] // 2
    first, second = packed[:, :rows], packed[:, rows:]
    own, received = either(core, first, second), core_swap(either(core, second, first))
    return either(core, own, received), either(core, received, own)


def pair_rows(half_rows, pair):
    first, second = half_rows[0], half_rows[1]
    return ordered(pair, either(pair, first, second), pair_swap(either(pair, second, first)))


def relative_order(core, at):
    length = lax.axis_size(E) // 4
    spots = jnp.arange(16 * length // 2)
    c, d, y, p = spots // (4 * length), spots // 4 % length, spots // 2 % 2, spots % 2
    line = lax.rem(at // 4 + length - d, length)
    order = ((line * 2 + p) * 2 + (y ^ (at % 2))) * 2 + (c ^ core)
    line, p, y, c = spots // 8, spots // 4 % 2, spots // 2 % 2, spots % 2
    d = lax.rem(at // 4 + length - line, length)
    back = (((c ^ core) * length + d) * 2 + (y ^ (at % 2))) * 2 + p
    return order, back


def move_blocks(order, x, out, back=False):
    wide = x.shape[1] // order.shape[0]
    if wide % 128:
        out[...] = x[...]
        return
    for j in range(order.shape[0]):
        at = pl.multiple_of(order[j] * wide, wide)
        if back:
            out[:, pl.ds(at, wide)] = x[:, j * wide : (j + 1) * wide]
        else:
            out[:, j * wide : (j + 1) * wide] = x[:, pl.ds(at, wide)]


def shuffle_outside(x, order):
    blocks = order.shape[0]
    if x.shape[1] // blocks % 128 == 0:
        return x
    return jnp.take(x.reshape(x.shape[0], blocks, -1), order, axis=1).reshape(x.shape)


def gather_weight(both):
    held = [both] + [turn(both, d) for d in range(1, lax.axis_size(E) // 4)]
    mine = [a for h in held for a in (h, near_swap(h))]
    return [flat(a) for a in mine + [core_swap(m) for m in mine]], held[-1]


def flat(piece):
    return piece.reshape(-1, piece.shape[-1])


def weight_product(left, right):
    n = lax.axis_size(E)
    half = left.shape[1] // 2
    joined = jnp.concatenate([left[:, :half], core_swap(left[:, half:])], axis=0)
    rights = jnp.concatenate([right, core_swap(right)], axis=0)
    product = dot(joined, rights, 0, 0).astype(b16)
    return product.reshape(n // 4, 2, 2, -1, right.shape[1])


def near_parts(pieces):
    return pieces[:, 0], near_swap(pieces[:, 1])


def turn_parts(sums):
    return sums[0], [
        turn(sums[d].astype(b16), -d) for d in range(1, lax.axis_size(E) // 4)
    ]


def near_sums(parts, *markers):
    kept, got = parts
    return kept.astype(f32) + (after(got, *markers) if markers else got).astype(f32)


def turn_sums(parts, *markers):
    kept, got = parts
    return kept + sum(g.astype(f32) for g in (after(got, *markers) if markers else got))


def lay_out(flags, own, received, query, key, value, output):
    _, rows, _ = own.shape
    outs = (query, key, value, output)

    def write(core, pair):
        for source, half in ((own, core), (received, 1 - core)):
            at = slice(half * rows, (half + 1) * rows)
            for k, g in ((0, pair), (1, 1 - pair)):
                start = 0
                for out in outs:
                    wide = out.shape[1] // 2
                    columns = slice(g * wide, (g + 1) * wide)
                    out[at, columns] = source[k, :, start : start + wide].astype(f32)
                    start += wide

    for core in range(2):
        for pair in range(2):

            @pl.when((flags[0] == core) & (flags[1] == pair))
            def _():
                write(core, pair)


def pair_columns(total, pair):
    kept = either(pair, total[0], total[1]).astype(b16)
    return jnp.stack([kept, pair_swap(either(pair, total[1], total[0]).astype(b16))])


def to_owner(first, second, core, widths, pair):
    own, received = either(core, first, second), core_swap(either(core, second, first))
    outs = [((2 * own.shape[1], w), f32) for w in widths]
    flags = jnp.stack([core, pair]).astype(jnp.int32)
    return in_vmem(lay_out, outs, [], flags, own, received)


def head_norm(x):
    inverse = lax.rsqrt(jnp.mean(x * x, axis=-1, keepdims=True) + eps)
    return x * inverse, inverse


def assemble(flags, sources, whole):
    x, side, other, left, right = sources
    rows, cut = left.shape
    pair, half = flags[0], flags[1]

    def at(p, h):
        return pl.ds(pl.multiple_of((p * 2 + h) * rows, rows), rows)

    whole[at(pair, half)] = x[...]
    whole[at(pair, 1 - half)] = side[...]
    whole[at(1 - pair, half)] = other[...]
    whole[at(1 - pair, 1 - half), :cut] = left[...]
    whole[at(1 - pair, 1 - half), cut:] = right[...]


def take_parts(flags, whole, outs):
    one, one_sent, two, two_sent = outs
    rows, cut = one.shape[0] // 2, one.shape[1]
    pair, half = flags[0], flags[1]
    for out, p in ((one, pair), (one_sent, 1 - pair)):
        out[...] = whole[pl.ds(pl.multiple_of(p * 2 * rows, rows), 2 * rows), :cut]
    for out, h in ((two, half), (two_sent, 1 - half)):
        for p in range(2):
            at = pl.ds(pl.multiple_of((p * 2 + h) * rows, rows), rows)
            out[p * rows : (p + 1) * rows] = whole[at, cut:]


def load(flags, order, sources, whole, moved):
    if len(sources) == 1:
        move_blocks(order, sources[0], moved)
        return
    assemble(flags, sources, whole)
    move_blocks(order, whole, moved)


def store(flags, order, mixed, whole, outs):
    if len(outs) == 1:
        move_blocks(order, mixed, outs[0], back=True)
        return
    move_blocks(order, mixed, whole, back=True)
    take_parts(flags, whole, outs)


def attend(counts, starts, flags, order, *refs):
    sources, ins, w_outs, refs = cut_refs(refs, counts[:3])
    w_outs = w_outs or ins
    gains, cosine, sine, allowed, *refs = refs
    outs, refs = refs[: counts[3]], refs[counts[3] :]
    moved, proj, query, key, value, shares, attended, mixed, whole = refs
    rows, head = cosine.shape
    length = allowed.shape[1]
    heads = attended.shape[1] // head
    cols = proj.shape[1]
    load(flags, order, sources, whole, moved)
    depth = ins[0].shape[0]
    total = 0.0
    for i, w in enumerate(ins):
        total = total + dot(moved[:, i * depth : (i + 1) * depth], w[:, :cols], 1, 0)
    proj[...] = total

    def prepared(x, gain):
        turned = head_norm(x)[0] * gain
        return (turned * cosine[...] + pltpu.roll(turned, head // 2, 1) * sine[...]).astype(b16)

    for h in range(heads):
        q = prepared(proj[:, h * head : (h + 1) * head], gains[0:1])
        for s in range(rows // length):
            query[s, h * length : (h + 1) * length] = q[s * length : (s + 1) * length]
    key[...] = prepared(proj[:, heads * head : (heads + 1) * head], gains[1:2])
    value[...] = proj[:, (heads + 1) * head :].astype(b16)
    for s in range(rows // length):
        own = slice(s * length, (s + 1) * length)
        scores = dot(query[s], key[own], 1, 1) * head ** (-0.5)
        scores = scores.reshape(heads, length, length)
        scores = jnp.where((allowed[s] > 0)[None], scores, -1e30)
        raised = jnp.exp(scores - jnp.max(scores, axis=-1, keepdims=True))
        weights = raised / jnp.sum(raised, axis=-1, keepdims=True)
        weights = weights.reshape(heads * length, length)
        shares[s] = weights
        result = dot(weights.astype(b16), value[own], 1, 0).astype(b16)
        for h in range(heads):
            attended[own, h * head : (h + 1) * head] = result[h * length : (h + 1) * length]
    for i, w in enumerate(w_outs):
        at = slice(i * depth, (i + 1) * depth)
        mixed[:, at] = dot(attended[...], w[:, starts:], 1, 1).astype(b16)
    store(flags, order, mixed, whole, outs)


def cut_refs(refs, counts):
    parts = []
    for c in counts:
        parts.append(refs[:c])
        refs = refs[c:]
    return *parts, refs


def attend_back(counts, starts, flags, order, *refs):
    sources, ins, w_outs, refs = cut_refs(refs, counts[:3])
    w_outs = w_outs or ins
    gains, cosine, sine, proj, query, key, value, shares, *refs = refs
    outs, refs = refs[: counts[3]], refs[counts[3] :]
    moved, projected, gain_grads, spread, mixed, whole = refs
    rows, head = cosine.shape
    length = shares.shape[2]
    cols = proj.shape[1]
    heads = cols // head - 2
    scale = head ** (-0.5)
    load(flags, order, sources, whole, moved)
    depth = ins[0].shape[0]
    total = 0.0
    for i, w in enumerate(w_outs):
        total = total + dot(moved[:, i * depth : (i + 1) * depth], w[:, starts:], 1, 0)
    attended = total.astype(b16)
    for h in range(heads):
        for s in range(rows // length):
            spread[s, h * length : (h + 1) * length] = attended[
                s * length : (s + 1) * length, h * head : (h + 1) * head
            ]
    query_grads, key_grads = [], []
    for s in range(rows // length):
        own = slice(s * length, (s + 1) * length)
        weights = shares[s]
        given = spread[s]
        value_grad = dot(weights.astype(b16), given, 0, 0).astype(b16)
        projected[own, (heads + 1) * head :] = value_grad
        share_grad = dot(given, value[own], 1, 1)
        delta = jnp.sum(weights * share_grad, axis=-1, keepdims=True)
        score = (weights * (share_grad - delta)).astype(b16)
        query_grads.append((dot(score, key[own], 1, 0) * scale).astype(b16).astype(f32))
        key_grads.append((dot(score, query[s], 0, 0) * scale).astype(b16).astype(f32))

    def prepared_back(grad, x, gain):
        turned = grad * cosine[...] + pltpu.roll(grad * sine[...], head // 2, 1)
        normed, inverse = head_norm(x)
        scaled = turned * gain
        mean = jnp.mean(scaled * normed, axis=-1, keepdims=True)
        gain_grad = jnp.sum(turned * normed, axis=0, keepdims=True)
        return ((scaled - normed * mean) * inverse).astype(b16), gain_grad

    total = jnp.zeros((1, head), f32)
    for h in range(heads):
        grad = jnp.concatenate([g[h * length : (h + 1) * length] for g in query_grads], axis=0)
        at = slice(h * head, (h + 1) * head)
        projected[:, at], gain_grad = prepared_back(grad, proj[:, at], gains[0:1])
        total = total + gain_grad
    at = slice(heads * head, (heads + 1) * head)
    grad = jnp.concatenate(key_grads, axis=0)
    projected[:, at], gain_grad = prepared_back(grad, proj[:, at], gains[1:2])
    gain_grads[0:1] = total
    gain_grads[1:2] = gain_grad
    for i, w in enumerate(ins):
        at = slice(i * depth, (i + 1) * depth)
        mixed[:, at] = dot(projected[...], w[:, :cols], 1, 1).astype(b16)
    store(flags, order, mixed, whole, outs)


def in_vmem(kernel, outs, scratch, scalars, *args):
    scalars = scalars if isinstance(scalars, tuple) else (scalars,)
    whole = pl.BlockSpec(memory_space=pltpu.VMEM)
    return pl.pallas_call(
        kernel,
        out_shape=[jax.ShapeDtypeStruct(*o) for o in outs],
        in_specs=[pl.BlockSpec(memory_space=pltpu.SMEM)] * len(scalars) + [whole] * len(args),
        out_specs=[whole] * len(outs),
        scratch_shapes=[pltpu.VMEM(*o) for o in scratch],
        compiler_params=pltpu.CompilerParams(vmem_limit_bytes=48 << 20),
        cost_estimate=pl.CostEstimate(flops=0, bytes_accessed=0, transcendentals=0),
    )(*scalars, *args)


def on_plane(kernel, sources, place, weights, start, outs, scratch, *args):
    pair, half, orders = place
    rows, width = 4 * sources[0].shape[0], sources[0].shape[1]
    direct = width // orders[0].shape[0] % 128 != 0
    if len(sources) == 1:
        rows = sources[0].shape[0]
    elif direct:
        sources = [plane_whole(sources, pair, half)]
    if direct:
        sources = [shuffle_outside(sources[0], orders[0])]
    parts = [((rows, width), b16)] if direct else [((rows // 2, width // 2), b16)] * 4
    counts = (len(sources), len(weights[0]), len(weights[1]), len(parts))
    results = in_vmem(
        functools.partial(kernel, counts, start),
        parts + outs,
        scratch + [((rows, width), b16)] * 2,
        (jnp.stack([pair, half]).astype(jnp.int32), orders[0]),
        *sources,
        *weights[0],
        *weights[1],
        *args,
    )
    parts, others = list(results[: len(parts)]), list(results[len(parts) :])
    if direct:
        parts = plane_parts(shuffle_outside(parts[0], orders[1]), pair, half)
    return parts, others


def attention_forward(sources, place, weights, start, sizes, gains, tables, allowed):
    rows, head, length = tables[0].shape[0], gains.shape[1], allowed.shape[1]
    cols, heads_cols = sizes
    stacked = (rows // length, heads_cols // head * length)
    outs = [
        ((rows, sources[0].shape[1]), b16),
        ((rows, cols), f32),
        (stacked + (head,), b16),
        ((rows, head), b16),
        ((rows, head), b16),
        (stacked + (length,), f32),
        ((rows, heads_cols), b16),
    ]
    return on_plane(
        attend, sources, place, weights, start, outs, [], gains, *tables, allowed
    )


def attention_backward(sources, place, saved, weights, start, gains, tables):
    moved, proj, query, key, value, shares, _ = saved
    outs = [(moved.shape, b16), (proj.shape, b16), (gains.shape, f32)]
    return on_plane(
        attend_back,
        sources,
        place,
        weights,
        start,
        outs,
        [(query.shape, b16)],
        gains,
        *tables,
        proj,
        query,
        key,
        value,
        shares,
    )


def spread(gates, local, width):
    per = width // local
    rows = gates.shape[0]
    return jnp.concatenate(
        [jnp.broadcast_to(gates[:, j : j + 1], (rows, per)) for j in range(local)], axis=1
    )


def fetch(which, sizes, refs, target, sem):
    for k, size in enumerate(sizes):
        parts, refs = refs[:size], refs[size:]

        @pl.when(which == k)
        def _():
            start = 0
            for part in parts:
                rows = part.shape[0]
                pltpu.make_async_copy(part, target.at[pl.ds(start, rows)], sem).start()
                start += rows


def fetch_both(which, sizes, refs, targets, sems):
    for k, (size, target) in enumerate(zip(sizes, targets)):
        fetch(which, size, refs, target, sems.at[k])
        refs = refs[sum(size) :]
    for k, target in enumerate(targets):
        pltpu.make_async_copy(target, target, sems.at[k]).wait()


def experts_ahead(
    local, sizes, scalars, rows_own, rows_other, codes_own, codes_other, router, *refs
):
    choices, outs, scratch = refs[: -6 - 3], refs[-6 - 3 : -3], refs[-3:]
    part_own, part_other, rows_all, gates_out, hidden_out, units_out = outs
    weights_gu, weights_down, sems = scratch
    step, half = pl.program_id(0), pl.num_programs(0) // 2

    @pl.when(step == 0)
    def _():
        fetch_both(scalars[0], sizes, choices, (weights_gu, weights_down), sems)

    first = step < half
    rows = jnp.where(first, rows_own[...], rows_other[...])
    codes = jnp.where(first, codes_own[...], codes_other[...])
    rows_all[...] = rows
    gates = gates_of(dot(rows, router[...], 1, 0), (codes > 0.5).astype(f32))
    gates = jnp.where(codes > 1.5, gates, 0.0)
    ids = lax.broadcasted_iota(jnp.int32, gates.shape, 1)
    spots = lax.broadcasted_iota(jnp.int32, gates_out.shape, 1)
    kept = jnp.zeros(gates_out.shape, f32)
    for j in range(local):
        own = jnp.sum(jnp.where(ids == scalars[1] + j, gates, 0.0), axis=1, keepdims=True)
        kept = jnp.where(spots == j, own, kept)
    gates_out[...] = kept
    hidden = dot(rows, weights_gu[...], 1, 0)
    hidden_out[...] = hidden
    cut = hidden.shape[1] // 2
    units = swiglu(hidden[:, :cut], hidden[:, cut:])
    units_b = (units * spread(kept, local, cut)).astype(b16)
    units_out[...] = units_b
    part = dot(units_b, weights_down[...], 1, 0).astype(b16)

    @pl.when(first)
    def _():
        part_own[...] = part

    @pl.when(step >= half)
    def _():
        part_other[...] = part


def experts_back(local, experts, sizes, scalars, grads_own, grads_other, gates, hidden, *refs):
    choices, outs, scratch = refs[: -4 - 3], refs[-4 - 3 : -3], refs[-3:]
    part_own, part_other, grads_all, hidden_out = outs
    weights_gu, weights_down, sems = scratch
    step, half = pl.program_id(0), pl.num_programs(0) // 2

    @pl.when(step == 0)
    def _():
        fetch_both(scalars[0], sizes, choices, (weights_gu, weights_down), sems)

    first = step < half
    grads = jnp.where(first, grads_own[...], grads_other[...])
    grads_all[...] = grads
    raw = dot(grads, weights_down[...], 1, 1)
    cut = raw.shape[1]
    gate, up = hidden[:, :cut], hidden[:, cut:]
    share = jax.nn.sigmoid(gate)
    silu = gate * share
    scaled = raw * spread(gates[...], local, cut)
    gate_grad = (scaled * up * (share + silu * (1.0 - share))).astype(b16)
    up_grad = (scaled * silu).astype(b16)
    hidden_b = jnp.concatenate([gate_grad, up_grad], axis=1)
    hidden_out[...] = hidden_b
    part = dot(hidden_b, weights_gu[...], 1, 1).astype(b16)
    overlap = raw * silu * up
    per = cut // local
    wide = part_own.shape[1] - part.shape[1]
    spots = lax.broadcasted_iota(jnp.int32, (grads.shape[0], wide), 1)
    extra = jnp.zeros(spots.shape, f32)
    for j in range(local):
        value = jnp.sum(overlap[:, j * per : (j + 1) * per], axis=1, keepdims=True)
        high = value.astype(b16).astype(f32)
        extra = jnp.where(spots == scalars[1] + j, high, extra)
        extra = jnp.where(spots == experts + scalars[1] + j, value - high, extra)
    extra = extra.astype(b16)
    width = part.shape[1]

    @pl.when(first)
    def _():
        part_own[:, :width] = part
        part_own[:, width:] = extra

    @pl.when(step >= half)
    def _():
        part_other[:, :width] = part
        part_other[:, width:] = extra


def by_rows(kernel, which, first_expert, halved, whole, fixed, choices, outs_halved, outs):
    rows = halved[0][0].shape[0]
    block = 256
    count = rows // block
    weights = [choice[0][0].shape for choice in choices]

    def spec(a, index):
        return pl.BlockSpec((block, a.shape[1]), index)

    def own(i, *_):
        return jnp.minimum(i, count - 1), 0

    def other(i, *_):
        return jnp.maximum(i - count, 0), 0

    def each(i, *_):
        return i, 0

    in_specs = []
    for first, second in halved:
        in_specs += [spec(first, own), spec(second, other)]
    in_specs += [spec(a, each) for a in whole]
    in_specs += [pl.BlockSpec(a.shape, lambda i, *_: (0, 0)) for a in fixed]
    sizes = [[len(parts) for parts in choice] for choice in choices]
    choices = [a for choice in choices for parts in choice for a in parts]
    in_specs += [pl.BlockSpec(memory_space=pl.ANY)] * len(choices)
    shapes = [jax.ShapeDtypeStruct((rows, w), b16) for w in (outs_halved, outs_halved)]
    shapes += [jax.ShapeDtypeStruct((2 * rows, w), t) for w, t in outs]
    out_specs = [spec(shapes[0], own), spec(shapes[1], other)]
    out_specs += [spec(a, each) for a in shapes[2:]]
    weights = [pltpu.VMEM(a, b16) for a in weights]
    return pl.pallas_call(
        functools.partial(kernel, sizes),
        grid_spec=pltpu.PrefetchScalarGridSpec(
            num_scalar_prefetch=1,
            grid=(2 * count,),
            in_specs=in_specs,
            out_specs=out_specs,
            scratch_shapes=weights + [pltpu.SemaphoreType.DMA((2,))],
        ),
        out_shape=shapes,
        compiler_params=pltpu.CompilerParams(vmem_limit_bytes=48 << 20),
        cost_estimate=pl.CostEstimate(flops=0, bytes_accessed=0, transcendentals=0),
    )(
        jnp.stack([which, first_expert]).astype(jnp.int32),
        *[a for pair in halved for a in pair],
        *whole,
        *fixed,
        *choices,
    )


def experts_forward(rows, codes, router, which, choices, first_expert, local):
    width = rows[0].shape[1]
    hidden = choices[0][0][0].shape[1]
    outs = [(width, b16), (128, f32), (hidden, f32), (hidden // 2, b16)]
    part_own, part_other, *saved = by_rows(
        functools.partial(experts_ahead, local),
        which,
        first_expert,
        [rows, codes],
        [],
        [router],
        choices,
        width,
        outs,
    )
    return (part_own, part_other), saved


def experts_backward(grads, saved, which, choices, first_expert, local, experts):
    _, gates, hidden, _ = saved
    width = grads[0].shape[1]
    wide = -(-2 * experts // 128) * 128
    outs = [(width, b16), (hidden.shape[1], b16)]
    part_own, part_other, *others = by_rows(
        functools.partial(experts_back, local, experts),
        which,
        first_expert,
        [grads],
        [gates, hidden],
        [],
        choices,
        width + wide,
        outs,
    )
    return (part_own, part_other), others


def own_sums(steps, flags, *refs):
    parts = len(steps)
    ins, outs = refs[: 6 * parts], refs[6 * parts :]

    def write(own, side, core):
        total = side[...].astype(f32) + core[...].astype(f32)
        total = total + jnp.where(flags[0] == flags[1], own[...].astype(f32), 0.0)
        if len(outs) == 1:
            outs[0][...] = total
            return
        per = outs[0].shape[2]
        for i, out in enumerate(outs):
            for j in range(out.shape[0]):
                at = (i * out.shape[0] + j) * per
                out[j] = total[:, at : at + per]

    at = pl.program_id(0)
    for l in range(2):
        for k, (first, last) in enumerate(steps):

            @pl.when((flags[0] == l) & (at >= first) & (at < last))
            def _():
                base = 3 * (l * parts + k)
                write(*ins[base : base + 3])


def owned(core, half, by_layer, pieces):
    step = 256
    steps, specs, rows = [], [], 0
    for own, _, _ in by_layer[0]:
        steps.append((rows // step, (rows + own.shape[0]) // step))
        rows += own.shape[0]
    cols = by_layer[0][0][0].shape[1]
    for l in range(2):
        for first, last in steps:

            def where(i, f, l=l, first=first, last=last):
                inside = jnp.clip(i - first, 0, last - first - 1)
                return jnp.where(f[0] == l, inside, 0), 0

            specs += [pl.BlockSpec((step, cols), where)] * 3
    if pieces == 1:
        outs = [jax.ShapeDtypeStruct((rows, cols), f32)]
        out_specs = [pl.BlockSpec((step, cols), lambda i, f: (i, 0))]
    else:
        shape = (pieces // 2, rows, cols // pieces)
        outs = [jax.ShapeDtypeStruct(shape, f32)] * 2
        block = (pieces // 2, step, cols // pieces)
        out_specs = [pl.BlockSpec(block, lambda i, f: (0, i, 0))] * 2
    terms = [t for layer in by_layer for part in layer for t in part]
    return pl.pallas_call(
        functools.partial(own_sums, steps),
        grid_spec=pltpu.PrefetchScalarGridSpec(
            num_scalar_prefetch=1, grid=(rows // step,), in_specs=specs, out_specs=out_specs
        ),
        out_shape=outs,
        compiler_params=pltpu.CompilerParams(vmem_limit_bytes=48 << 20),
        cost_estimate=pl.CostEstimate(flops=0, bytes_accessed=0, transcendentals=0),
    )(jnp.stack([core, half]).astype(jnp.int32), *terms)


def shards(
    inputs,
    cotangent,
    segments,
    routes,
    counts,
    norm_attn,
    norm_ffn,
    q_gain,
    k_gain,
    w_query,
    w_key,
    w_value,
    w_output,
    w_router,
    w_gate,
    w_up,
    w_down,
):
    core, at, half = lax.axis_index(C), lax.axis_index(E), lax.axis_index(H)
    pair = lax.rem(at // 2, 2)
    n = lax.axis_size(E)
    _, tokens, width = inputs.shape
    rows = tokens // 2
    experts = counts.shape[1]
    local = w_gate.shape[1]
    units = w_gate.shape[3]
    first_expert = at * local
    head_size = q_gain.shape[1]
    place = pair, half, relative_order(core, at)

    def by_group(weight):
        return weight[0].reshape(weight.shape[1], 2, -1).transpose(1, 0, 2)

    packed = jnp.concatenate([by_group(w) for w in (w_query, w_key, w_value, w_output)], axis=2)
    halves = halves_for_cores(packed, core)
    heads_cols = w_output.shape[2] // 2
    cut = packed.shape[2] - heads_cols
    sizes = cut, heads_cols
    weights, starts = [None, None], (0, 0)
    first = [pair_rows(h, pair) for h in (halves[0][..., :cut], halves[0][..., cut:])]
    (weights_in, _), (weights_out, arrived) = (gather_weight(h) for h in first)
    weights[0] = weights_in, weights_out
    grad = lax.dynamic_slice_in_dim(pick(cotangent, core), half * rows, rows, 0)
    grads_all = gather_rows(after(grad, *first))

    def both_layers(own):
        return ordered(core, own, after(core_swap(own), first[0]))

    norm_attn, norm_ffn, q_gain, k_gain = (
        both_layers(a[0]) for a in (norm_attn, norm_ffn, q_gain, k_gain)
    )
    counts = both_layers(counts[0])
    chosen = after(core_swap(pick(routes[0], 1 - core)), first[0])
    chosen = ordered(core, pick(routes[0], core), chosen)
    block_rows = tokens * chosen.shape[2] // (4 * experts)
    codes = [route_codes(chosen[l], counts[l], block_rows) for l in range(2)]
    codes = jnp.concatenate(codes, axis=1)
    codes_own = lax.dynamic_slice_in_dim(codes, half * rows, rows, 0)
    wide = -(-2 * experts // 128) * 128
    codes_sent = jnp.pad(codes_own.astype(b16), ((0, 0), (0, wide - 2 * experts)))
    router_sent = w_router[0].reshape(-1, wide)
    tables_sent = jnp.concatenate([codes_sent, router_sent], axis=0)
    codes_own = [codes_own[:, l * experts : (l + 1) * experts] for l in range(2)]

    seg_own = pick(segments, core)[0]
    seg_ids = ordered(pair, seg_own, after(pair_swap(seg_own), first[0]))
    spots = jnp.arange(tokens)
    allowed = (spots[:, None] >= spots[None, :])[None] & (
        seg_ids[:, :, None] == seg_ids[:, None, :]
    )
    allowed = allowed.astype(f32)
    tables = [jnp.concatenate([t, t], axis=0) for t in rotary_tables(tokens, head_size)]

    at_first = (core == 0) & (half == 0)
    at_last = (core == 1) & (half == 1)
    own_gu = jnp.concatenate([w[0, j] for w in (w_gate, w_up) for j in range(local)], axis=1)
    own_down = w_down[0].reshape(-1, width)
    which = [
        jnp.where(keeps, 0, jnp.where(takes, 2, 1))
        for keeps, takes in ((at_first, at_last), (at_last, at_first))
    ]

    def experts_sent(layer, cuts, *marker):
        if layer == 0:
            by_side = [((0, 0), (0, 1)), ((0, 1), (1, 0))]
            by_core = [((0, 1), (1, 1))]
        else:
            by_side = [((1, 0), (0, 1)), ((1, 1), (1, 0))]
            by_core = [((1, 0), (0, 0))]
        sent = []
        for w, count in zip((own_gu, own_down), cuts):
            step = w.shape[0] // count
            parts = [w[i * step : (i + 1) * step] if count > 1 else w for i in range(count)]
            parts = [send(p, by_side) for p in after(parts, *marker)]
            sent.append(([w], parts, [send(w, by_core)]))
        return sent

    choices = [experts_sent(0, (1, 1)), None]

    layer_in = lax.dynamic_slice_in_dim(pick(inputs, core), half * rows, rows, 0)
    whole_in = pick(inputs, core)
    others_in = after(pair_swap(whole_in), first[0])
    whole_in = ordered(pair, whole_in, others_in).reshape(-1, width)
    sources = [norm_rows(whole_in.astype(f32), norm_attn[0]).astype(b16)]
    sources = after(sources, *choices[0][0][1], *choices[0][1][1], *grads_all)
    gains = jnp.stack([q_gain, k_gain], axis=1)
    kept_attn, kept_rows, kept_experts = [], [], []
    for l in range(2):
        if l == 1:
            mine = norm_rows(layer_in.astype(f32), norm_attn[1]).astype(b16)
            sources = plane_pieces(mine)
        parts, saved = attention_forward(
            sources, place, weights[l], starts[l], sizes, gains[l], tables, allowed
        )
        if l == 0:
            tables_all = [t.reshape(n, -1, wide) for t in gather_rows(after(tables_sent, saved[6]))]
            codes_all = [t[:, :rows].reshape(-1, wide).astype(f32) for t in tables_all]
            routers = [jnp.take(t[:, rows:], position(at), axis=0) for t in tables_all]
            routers = ordered(core, *routers).reshape(2, width, experts)
            codes_all = [[c[:, l * experts : (l + 1) * experts] for c in codes_all] for l in range(2)]
            second_pair = pair_rows(after(halves[1], arrived), pair)
            second_near = near_swap(second_pair)
            parts[0] = after(parts[0], second_pair)
        hidden = layer_in.astype(f32) + plane_scatter(parts, pair, half)
        normed_two = norm_rows(hidden, norm_ffn[l]).astype(b16)
        if l == 0:
            normed_two = after(normed_two, second_near, *codes_all[0], *codes_all[1], routers)
            choices[1] = experts_sent(1, (2, 2), normed_two)
            gu_parts, down_parts = choices[1][0][1], choices[1][1][1]
            rows_all = gather_rows(normed_two, (), gu_parts[:1])
        else:
            rows_all = gather_rows(normed_two, (), down_parts[1:])
        parts, saved_experts = experts_forward(
            rows_all, codes_all[l], routers[l], which[l], choices[l], first_expert, local
        )
        kept_experts.append(saved_experts)
        kept_attn.append(saved)
        kept_rows.append((layer_in, hidden, normed_two))
        if l == 0:
            pieces = after([second_pair[..., :cut], second_pair[..., cut:]], rows_all[0])
            far = [[turn(p, d) for d in range(1, n // 4)] for p in pieces]
            parts = after(parts, *far[0])
            summed = sum_cores(*parts)
            near = [near_swap(p) for p in after(far[0], summed)]
            near = [near, [near_swap(p) for p in after(far[1], *near)]]
            moved = scatter_rows(
                summed, [*far[1], gu_parts[1]], near[0], near[1] + down_parts[:1]
            )
            layer_in = (hidden + moved).astype(b16)
            weights[1] = []
            for k, (a, b) in enumerate(((0, cut), (cut, packed.shape[2]))):
                mine = [second_pair[..., a:b], second_near[..., a:b]]
                for p in zip(far[k], near[k]):
                    mine += p
                mine = [flat(p) for p in mine]
                weights[1].append(mine + [core_swap(p) for p in mine])
    last_parts, last_rows = parts, None

    grads_in, small, grads_experts = ([None] * 2 for _ in range(3))

    def expert_grads(l, marker, grads_all, hidden_b):
        rows_all, _, _, units_b = kept_experts[l]
        units_b, hidden_b = after((units_b, hidden_b), marker)
        cuts = [slice(0, width // 2), slice(width // 2, width)]
        return [dot(rows_all[:, c], hidden_b, 0, 0).astype(b16) for c in cuts] + [
            dot(units_b, grads_all, 0, 0).astype(b16)
        ]

    def to_owners(l, piece):
        if l == 0:
            by_side = [((0, 1), (0, 0)), ((1, 0), (0, 1))]
            by_core = [((1, 1), (0, 1))]
        else:
            by_side = [((0, 1), (1, 0)), ((1, 0), (1, 1))]
            by_core = [((0, 0), (1, 0))]
        return [send(piece, by_side), send(piece, by_core)]

    def both_batches(first, second):
        others = core_swap(either(core, second, first))
        both = ordered(core, either(core, first, second), others)
        swapped = side_swap(both)
        both = ordered(half, both, swapped).transpose(1, 0, 2, 3)
        return both.reshape(2, tokens, width), swapped

    late_qkv, late_out, received = None, None, [[], []]
    for l in (1, 0):
        layer_in, hidden, normed_two = kept_rows[l]
        grad_f = grad.astype(f32)
        if l == 0:
            sent = to_owners(1, after(grads_experts[1][1], grad))
            received[1].append(sent)
            grads_all = gather_rows(grad, (), sent[:1])
            received[1].append(to_owners(1, after(grads_experts[1][2], sent[0])))
        parts, (grads_joined, hidden_b) = experts_backward(
            grads_all, kept_experts[l], which[l], choices[l], first_expert, local, experts
        )
        mid, last, end = [], [], []
        if l == 0:
            late_out = near_parts(late_out)
            last_rows = pair_stage(last_rows)
            parts = after(parts, late_out[1], last_rows[1])
        summed = sum_cores(*parts)
        grads_experts[l] = expert_grads(l, summed, grads_joined, hidden_b)
        piece = grads_experts[l][0]
        if l == 0:
            piece = after(piece, received[1][2][0])
        sent = to_owners(l, piece)
        received[l].append(sent)
        if l == 0:
            late_out = turn_parts(near_sums((after(late_out[0], summed), late_out[1])))
            late_qkv = near_parts(after(late_qkv, summed))
            last_rows = turn_stage((after(last_rows[0], summed), last_rows[1]))
            mid, last, end = late_out[1], last_rows[1], late_qkv[1:]
        else:
            rows_kept, rows_sent = near_pieces(sum_cores(*after(last_parts, parts[0])))
            rows_got = [near_swap(rows_sent[..., : width // 2])]
            end = rows_got
        moved = scatter_rows(
            summed, grads_experts[l][:2] + mid, last, sent[:1] + list(end)
        )
        normed_grad, extra = moved[:, :width], moved[:, width:]
        overlap = extra[:, :experts] + extra[:, experts : 2 * experts]
        chosen_f = (codes_own[l] > 0.5).astype(f32)
        logits = dot(normed_two, routers[l], 1, 0)
        gates_back = jax.vjp(lambda v: gates_of(v, chosen_f), logits)[1]
        logit_b = gates_back(jnp.where(codes_own[l] > 1.5, overlap, 0.0))[0].astype(b16)
        normed_grad = normed_grad + dot(logit_b, routers[l], 1, 1)
        grad_router = dot(logit_b, normed_two, 0, 0)
        hidden_grad, grad_norm_ffn = jax.vjp(norm_rows, hidden, norm_ffn[l])[1](normed_grad)
        hidden_grad = hidden_grad + grad_f
        branch_b = hidden_grad.astype(b16)
        sources = plane_pieces(branch_b)
        parts, (branch_b, projected_b, gain_grads) = attention_backward(
            sources, place, kept_attn[l], weights[l], starts[l], gains[l], tables
        )
        product_out = weight_product(branch_b, kept_attn[l][6])
        product_qkv = weight_product(kept_attn[l][0], projected_b)
        if l == 1:
            late_out, late_qkv = product_out, product_qkv
            rows_got.append(near_swap(after(rows_sent[..., width // 2 :], moved)))
            parts[0] = after(parts[0], rows_got[1])
            last_rows = rows_kept, jnp.concatenate(rows_got, axis=-1)
        else:
            parts[0] = after(parts[0], product_out, product_qkv)
            late_qkv = turn_parts(near_sums(late_qkv, moved))
            layer_out = kept_rows[1][1] + last_stage(last_rows)
            activations, marker = both_batches(kept_rows[1][0], layer_out.astype(b16))
            parts[0] = after(parts[0], *late_qkv[1], marker)
            last_out, last_qkv = near_parts(product_out), near_parts(product_qkv)
        input_grad, grad_norm_attn = jax.vjp(norm_rows, layer_in.astype(f32), norm_attn[l])[1](
            plane_scatter(parts, pair, half)
        )
        grad = (input_grad + hidden_grad).astype(b16)
        if l == 0:
            grad = after(grad, last_out[1])
        grads_in[l] = grad
        gain_row = jnp.concatenate([g.reshape(n, -1) for g in gain_grads], axis=1)
        gain_row = jnp.pad(gain_row, ((0, 0), (0, width // n - gain_row.shape[1])))
        small[l] = jnp.concatenate(
            [grad_router, grad_norm_attn[None], grad_norm_ffn[None], gain_row.reshape(1, -1)],
            axis=0,
        )

    input_grads, marker = both_batches(grads_in[0], grads_in[1])
    last_out = turn_parts(near_sums(last_out))
    late = pair_columns(jnp.concatenate([turn_sums(late_qkv), turn_sums(late_out)], axis=2), pair)
    for p in grads_experts[0][1:]:
        received[0].append(to_owners(0, after(p, marker, received[0][-1][0])))
    received[1] = after(received[1], grad)
    last_qkv = near_sums((last_qkv[0], after(last_qkv[1], *last_out[1], late, marker)))
    last_qkv = turn_parts(last_qkv)

    def of_owner(ks, count):
        return owned(
            core, half, [[(grads_experts[l][k], *received[l][k]) for k in ks] for l in range(2)], count
        )

    grad_gate, grad_up = of_owner((0, 1), 2 * local)
    last_qkv = last_qkv[0], after(last_qkv[1], grad_gate)

    others = core_swap(either(core, small[1], small[0]))
    mine = either(core, small[0], small[1]) + others
    count = mine.shape[0]
    mine = mine.reshape(count, n, width // n).transpose(1, 0, 2)
    mine = jnp.take(mine, position(at), axis=0)
    mine = turn_stage(pair_stage(near_stage(mine)))
    mine = last_stage(mine)
    mine = mine + side_swap(mine)
    per = head_size // n

    widths = [w.shape[2] for w in (w_query, w_key, w_value, w_output)]
    last = [pair_columns(turn_sums(t), pair) for t in (last_out, last_qkv)]
    weight_grads = to_owner(jnp.concatenate(last[::-1], axis=2), late, core, widths, pair)

    (grad_down,) = of_owner((2,), 1)
    grad_down = grad_down.reshape(local, units, width)
    return (
        activations[None],
        input_grads[None],
        mine[experts][None],
        mine[experts + 1][None],
        mine[experts + 2, :per][None],
        mine[experts + 2, per : 2 * per][None],
        *[w[None] for w in weight_grads],
        mine[:experts].T[None],
        grad_gate[None],
        grad_up[None],
        grad_down[None],
    )


def solution(mesh):
    by_layer = P(C, None)
    in_specs = (
        P(None, E, None),
        P(None, E, None),
        P(None, E, None),
        P(C, None, E, None),
        by_layer,
        by_layer,
        by_layer,
        by_layer,
        by_layer,
        P(C, E, H),
        P(C, E, H),
        P(C, E, H),
        P(C, E, H),
        P(C, E, None),
        P(C, E, None, H),
        P(C, E, None, H),
        P(C, E, H, None),
    )
    out_specs = (
        P(C, None, E, None),
        P(C, None, E, None),
        P(C, E),
        P(C, E),
        P(C, E),
        P(C, E),
        P(C, E, H),
        P(C, E, H),
        P(C, E, H),
        P(C, E, H),
        P(C, E, None),
        P(C, E, None, H),
        P(C, E, None, H),
        P(C, E, H, None),
    )
    return jax.shard_map(shards, mesh=mesh, in_specs=in_specs, out_specs=out_specs, check_vma=False)
```
